32 devices in a mesh: aux: 8 (over y, x, core), orb: 4 (over z).
Axes of the slice: x: 2, y: 2, z: 4, core: 2. Of those that a mesh axis runs over, the one named last changes fastest.
Arguments:
- density: bfloat16 [256, 256], P('orb'), may hold values from -6 to 6
- tensor_blocks: bfloat16 [4, 8, 3, 4, 4096], P('orb', 'aux'), may hold values from -0.4375 to 0.4375
- pairs: int32 [4, 8, 3], P('orb', 'aux'), may hold values from 0 to 3, as said below
- kept: int32 [4, 8], P('orb', 'aux'), may hold values from 1 to 3, as said below
Outputs:
- exchange_matrix: float32 [256, 256], P('orb')
The draws below stay inside these ranges and needn't reach their ends.
Inputs may be any that keep to these rules, and one draw needn't show every extreme that they name: `pairs`: within one row atom block and one auxiliary block all 3 slots name different column blocks. `kept`: every auxiliary block has a row atom block whose slots are all used.
All inputs are finite; a program needn't handle non-finite values.
Results may differ from the reference program's by a relative error of at most 0.0032.
Values may be sent and summed in bfloat16 or wider, within the bound.
No kernel may reach another device: no remote copies, remote signals or barrier semaphores. Data moves between devices by JAX's collectives and lax.ppermute only.
A program may use at most 64 MiB of HBM per device.

```python
import jax
import jax.numpy as jnp
from jax import lax

BS = 64
NNZ_MAX = 3
AUX_DEV = 4
NB = 4
NAB = 8
N_AUX = 8


def draw_pairs(key, part):
    key = jax.random.fold_in(key, 11)
    scores = jax.random.randint(key, (NB, NAB, NB), 0, 1 << 20, dtype=jnp.int32)
    scores = scores * NB + jnp.arange(NB, dtype=jnp.int32)[None, None, :]
    order = jnp.argsort(scores, axis=-1)
    return order[:, :, :NNZ_MAX].astype(jnp.int32)


def draw_kept(key, part):
    key = jax.random.fold_in(key, 12)
    first_key, second_key = jax.random.split(key)
    counts = jax.random.randint(first_key, (NB, NAB), 1, NNZ_MAX + 1, dtype=jnp.int32)
    full_rows = jax.random.randint(second_key, (NAB,), 0, NB, dtype=jnp.int32)
    row_ids = jnp.arange(NB, dtype=jnp.int32)
    filled = row_ids[:, None] == full_rows[None, :]
    return jnp.where(filled, NNZ_MAX, counts).astype(jnp.int32)


def shard_levels(own_key, dims, cuts, low, largest):
    level, own = 1.0, jax.random.fold_in(own_key, 6)
    for position, shards_of in cuts:
        steps = jnp.exp(jax.random.uniform(jax.random.fold_in(own, position), (shards_of,), jnp.float32, low / len(cuts), largest / len(cuts)))
        level = level * jnp.repeat(steps, dims[position] // shards_of).reshape([-1 if axis == position else 1 for axis in range(len(dims))])
    return level


def bell_draw(key, dims, spread, reach, cuts=(), held_as=jnp.bfloat16):
    array = spread * jax.random.normal(key, dims, jnp.float32)
    if cuts:
        array = array * shard_levels(key, dims, cuts, -0.22, 0.18)
    return jnp.clip(array, -reach, reach).astype(held_as)


def setup_inputs(seed: int = 0) -> dict:
    seeds = jax.random.split(jax.random.key(seed), 5)
    density = bell_draw(seeds[0], (NB * BS, NB * BS), 1.0, 6.0, ((0, 4),))
    tensor_blocks = bell_draw(seeds[1], (NB, NAB, NNZ_MAX, AUX_DEV, BS * BS), ((BS * NNZ_MAX) ** -0.5 * (N_AUX * AUX_DEV) ** -0.25), 0.4375, ((0, 4), (1, 8)))
    pairs = draw_pairs(jax.random.fold_in(seeds[4], 71), 0)
    kept = draw_kept(jax.random.fold_in(seeds[4], 71), 0)
    return {"density": density, "tensor_blocks": tensor_blocks, "pairs": pairs, "kept": kept}


def reference(density, tensor_blocks, pairs, kept):
    blocks_count, aux_blocks, slots, aux_width, square = tensor_blocks.shape
    width = BS
    full_width = blocks_count * width
    slot_index = jnp.arange(slots, dtype=jnp.int32)
    active = slot_index[None, None, :] < kept[:, :, None]
    masked = jnp.where(active[:, :, :, None, None], tensor_blocks, jnp.zeros_like(tensor_blocks))
    density_rows = density.reshape(blocks_count, width, full_width)
    highest = lax.Precision.HIGHEST

    def one_slab(total, slab):
        blocks = lax.dynamic_index_in_dim(masked, slab, 1, keepdims=False)
        blocks = blocks.reshape(blocks_count, slots, aux_width, width, width).astype(jnp.float32)
        chosen = lax.dynamic_index_in_dim(pairs, slab, 1, keepdims=False)
        selected = density_rows[chosen].astype(jnp.float32)
        half = jnp.einsum("mjpal,mjlc->mpac", blocks, selected, precision=highest).astype(jnp.bfloat16)
        half = lax.optimization_barrier(half)
        half_cols = half.astype(jnp.float32).reshape(blocks_count, aux_width, width, blocks_count, width)
        term = jnp.zeros((blocks_count, width, blocks_count, width), jnp.float32)
        for slot in range(slots):
            picked = jnp.take(half_cols, chosen[:, slot], axis=3)
            term = term + jnp.einsum("mpans,npbs->manb", picked, blocks[:, slot], precision=highest)
        return total + term.reshape(full_width, full_width), None

    total, _ = lax.scan(one_slab, jnp.zeros((full_width, full_width), jnp.float32), jnp.arange(aux_blocks, dtype=jnp.int32))
    return total
```

```python
import jax
import jax.numpy as jnp
from jax import lax
from jax.sharding import PartitionSpec as P

BS = 64


def shards(density, tensor_blocks, pairs, kept):
    width = BS
    full_width = density.shape[1]
    blocks_count = full_width // width
    slots = tensor_blocks.shape[2]
    aux_width = tensor_blocks.shape[3]
    orb = lax.axis_size("orb")
    aux = lax.axis_size("aux")
    me = lax.axis_index("orb")
    slot_index = jnp.arange(slots, dtype=jnp.int32)
    active = slot_index < kept[0, 0]
    masked = jnp.where(active[:, None, None], tensor_blocks[0, 0], 0)
    own = masked.reshape(slots, aux_width, width, width)
    flat = own.transpose(2, 0, 1, 3).reshape(width, slots * aux_width * width)
    own_pairs = pairs.reshape(slots)

    rows, peers, peer_pairs = [density], [flat], [own_pairs]
    for shift in range(1, orb):
        perm = [(i, (i + shift) % orb) for i in range(orb)]
        rows.append(lax.ppermute(density, "orb", perm))
        peers.append(lax.ppermute(flat, "orb", perm))
        peer_pairs.append(lax.ppermute(own_pairs, "orb", perm))

    stacked = jnp.stack(rows)
    selected = stacked[(me - own_pairs) % orb]
    half = jnp.einsum(
        "jpal,jlc->pac", own, selected, preferred_element_type=jnp.float32
    ).astype(jnp.bfloat16)
    half_four = half.reshape(aux_width, width, blocks_count, width)
    columns = []
    for shift in range(orb):
        picked = jnp.take(half_four, peer_pairs[shift], axis=2, mode="clip")
        picked = picked.transpose(1, 2, 0, 3).reshape(width, -1)
        columns.append(
            lax.dot_general(
                picked, peers[shift], (((1,), (1,)), ((), ())), preferred_element_type=jnp.float32
            )
        )
    order = (me - jnp.arange(orb)) % orb
    parts = jnp.stack(columns)[order].transpose(1, 0, 2).reshape(width, full_width)
    step = 1
    while step < aux:
        parts = parts + lax.ppermute(parts, "aux", [(i, i ^ step) for i in range(aux)])
        step *= 2
    return parts


def solution(mesh):
    return jax.shard_map(
        shards,
        mesh=mesh,
        in_specs=(
            P("orb", None),
            P("orb", "aux", None, None, None),
            P("orb", "aux", None),
            P("orb", "aux"),
        ),
        out_specs=P("orb", None),
        check_vma=False,
    )
```

```python
import functools

import jax
import jax.numpy as jnp
from jax import lax
from jax.experimental import pallas as pl
from jax.experimental.pallas import tpu as pltpu
from jax.sharding import PartitionSpec as P

BS = 64


def half_kernel(orb, slots, aux_width, meta_ref, own_ref, *refs):
    rows, (half_ref, held) = refs[:orb], refs[orb:]
    me = lax.axis_index("orb")
    width = BS
    for shift in range(orb):
        held[shift] = rows[shift][:width]
    chosen = [held[lax.rem(me - meta_ref[j] + orb, orb)] for j in range(slots)]
    selected = jnp.concatenate(chosen, axis=0)
    own = own_ref[...]
    pieces = []
    for p in range(aux_width):
        cut = [(j * aux_width + p) * width for j in range(slots)]
        pieces.append(jnp.concatenate([own[:, c : c + width] for c in cut], axis=1))
    left = jnp.concatenate(pieces, axis=0)
    half = jnp.dot(left, selected, preferred_element_type=jnp.float32).astype(jnp.bfloat16)
    for k in range(orb):
        half_ref[k] = jnp.concatenate(
            [
                half[p * width : (p + 1) * width, k * width : (k + 1) * width]
                for p in range(aux_width)
            ],
            axis=1,
        )


def exchange_kernel(orb, slots, aux_width, meta_ref, half_ref, *refs):
    blocks, (out_ref, held) = refs[:orb], refs[orb:]
    me = lax.axis_index("orb")
    depth = aux_width * BS
    for shift in range(orb):
        total = None
        for j in range(slots):
            term = lax.dot_general(
                half_ref[meta_ref[shift * slots + j]],
                blocks[shift][:, j * depth : (j + 1) * depth],
                (((1,), (1,)), ((), ())),
                preferred_element_type=jnp.float32,
            )
            total = term if total is None else total + term
        held[lax.rem(me - shift + orb, orb)] = total
    out_ref[...] = jnp.concatenate([held[n] for n in range(orb)], axis=1)


def shards(density, tensor_blocks, pairs, kept):
    width = BS
    full_width = density.shape[1]
    slots = tensor_blocks.shape[2]
    aux_width = tensor_blocks.shape[3]
    orb = lax.axis_size("orb")
    aux = lax.axis_size("aux")
    slot_index = jnp.arange(slots, dtype=jnp.int32)
    active = slot_index < kept[0, 0]
    masked = jnp.where(active[:, None, None], tensor_blocks[0, 0], 0)
    own = masked.reshape(slots, aux_width, width, width)
    flat = own.transpose(2, 0, 1, 3).reshape(width, slots * aux_width * width)
    own_pairs = pairs.reshape(slots)
    note = jnp.zeros((8, full_width), jnp.bfloat16)
    note = note.at[0, :slots].set(own_pairs.astype(jnp.bfloat16))
    packed = jnp.concatenate([density, note], axis=0)

    rows, blocks, all_pairs = [packed], [flat], [own_pairs]
    for shift in range(1, orb):
        perm = [(i, (i + shift) % orb) for i in range(orb)]
        rows.append(lax.ppermute(packed, "orb", perm))
        blocks.append(lax.ppermute(flat, "orb", perm))
        all_pairs.append(rows[-1][width, :slots].astype(jnp.int32))

    vmem = pl.BlockSpec(memory_space=pltpu.VMEM)
    smem = pl.BlockSpec(memory_space=pltpu.SMEM)
    half = pl.pallas_call(
        functools.partial(half_kernel, orb, slots, aux_width),
        out_shape=jax.ShapeDtypeStruct((orb, width, aux_width * width), jnp.bfloat16),
        in_specs=[smem, vmem] + [vmem] * orb,
        out_specs=vmem,
        scratch_shapes=[pltpu.VMEM((orb, width, full_width), jnp.bfloat16)],
        compiler_params=pltpu.CompilerParams(vmem_limit_bytes=32 * 1024 * 1024),
        name="half",
    )(own_pairs, flat, *rows)
    parts = pl.pallas_call(
        functools.partial(exchange_kernel, orb, slots, aux_width),
        out_shape=jax.ShapeDtypeStruct((width, full_width), jnp.float32),
        in_specs=[smem, vmem] + [vmem] * orb,
        out_specs=vmem,
        scratch_shapes=[pltpu.VMEM((orb, width, width), jnp.float32)],
        compiler_params=pltpu.CompilerParams(vmem_limit_bytes=32 * 1024 * 1024),
        name="exchange",
    )(jnp.concatenate(all_pairs), half, *blocks)

    step = 1
    while step < aux:
        ways = 2 if step == 1 or step * 4 > aux else 4
        terms = [parts]
        for way in range(1, ways):
            terms.append(lax.ppermute(parts, "aux", [(i, i ^ (way * step)) for i in range(aux)]))
        while len(terms) > 1:
            terms = [terms[i] + terms[i + 1] for i in range(0, len(terms), 2)]
        parts = terms[0]
        step *= ways
    return parts


def solution(mesh):
    return jax.shard_map(
        shards,
        mesh=mesh,
        in_specs=(
            P("orb", None),
            P("orb", "aux", None, None, None),
            P("orb", "aux", None),
            P("orb", "aux"),
        ),
        out_specs=P("orb", None),
        check_vma=False,
    )
```

```python
import functools

import jax
import jax.numpy as jnp
from jax import lax
from jax.experimental import pallas as pl
from jax.experimental.pallas import tpu as pltpu
from jax.sharding import PartitionSpec as P

BS = 64


def half_kernel(orb, slots, aux_width, meta_ref, own_ref, *refs):
    rows, (half_ref, held) = refs[:orb], refs[orb:]
    me = lax.axis_index("orb")
    width = BS
    for shift in range(orb):
        held[lax.rem(me - shift + orb, orb)] = rows[shift][...]
    held[orb] = jnp.zeros_like(held[orb])
    selected = jnp.concatenate([held[meta_ref[j]] for j in range(slots)], axis=0)
    left = jnp.concatenate(
        [
            jnp.concatenate([own_ref[j, p] for j in range(slots)], axis=1)
            for p in range(aux_width)
        ],
        axis=0,
    )
    half = jnp.dot(left, selected, preferred_element_type=jnp.float32).astype(jnp.bfloat16)
    for k in range(orb):
        half_ref[k] = jnp.concatenate(
            [
                half[p * width : (p + 1) * width, k * width : (k + 1) * width]
                for p in range(aux_width)
            ],
            axis=1,
        )
    half_ref[orb] = jnp.zeros_like(half_ref[orb])


def exchange_kernel(orb, slots, aux_width, meta_ref, half_ref, *refs):
    blocks, (out_ref, held) = refs[:orb], refs[orb:]
    me = lax.axis_index("orb")
    for shift in range(orb):
        total = None
        for j in range(slots):
            right = jnp.concatenate([blocks[shift][j, p] for p in range(aux_width)], axis=1)
            term = lax.dot_general(
                half_ref[meta_ref[shift * slots + j]],
                right,
                (((1,), (1,)), ((), ())),
                preferred_element_type=jnp.float32,
            )
            total = term if total is None else total + term
        held[lax.rem(me - shift + orb, orb)] = total
    out_ref[...] = jnp.concatenate([held[n] for n in range(orb)], axis=1)


def shards(density, tensor_blocks, pairs, kept):
    width = BS
    full_width = density.shape[1]
    slots = tensor_blocks.shape[2]
    aux_width = tensor_blocks.shape[3]
    orb = lax.axis_size("orb")
    aux = lax.axis_size("aux")
    perms = [[(i, (i + shift) % orb) for i in range(orb)] for shift in range(orb)]
    slot_index = jnp.arange(slots, dtype=jnp.int32)
    codes = jnp.where(slot_index < kept[0, 0], pairs.reshape(slots), orb)
    rows, blocks, all_codes = [density], [tensor_blocks], [codes]
    for shift in range(1, orb):
        rows.append(lax.ppermute(density, "orb", perms[shift]))
        blocks.append(lax.ppermute(tensor_blocks, "orb", perms[shift]))
    sent, rows = lax.optimization_barrier((codes, rows))
    for shift in range(1, orb):
        all_codes.append(lax.ppermute(sent, "orb", perms[shift]))
    blocks = [b.reshape(slots, aux_width, width, width) for b in blocks]

    vmem = pl.BlockSpec(memory_space=pltpu.VMEM)
    smem = pl.BlockSpec(memory_space=pltpu.SMEM)
    half = pl.pallas_call(
        functools.partial(half_kernel, orb, slots, aux_width),
        out_shape=jax.ShapeDtypeStruct((orb + 1, width, aux_width * width), jnp.bfloat16),
        in_specs=[smem, vmem] + [vmem] * orb,
        out_specs=vmem,
        scratch_shapes=[pltpu.VMEM((orb + 1, width, full_width), jnp.bfloat16)],
        compiler_params=pltpu.CompilerParams(vmem_limit_bytes=32 * 1024 * 1024),
        name="half",
    )(codes, blocks[0], *rows)
    parts = pl.pallas_call(
        functools.partial(exchange_kernel, orb, slots, aux_width),
        out_shape=jax.ShapeDtypeStruct((width, full_width), jnp.float32),
        in_specs=[smem, vmem] + [vmem] * orb,
        out_specs=vmem,
        scratch_shapes=[pltpu.VMEM((orb, width, width), jnp.float32)],
        compiler_params=pltpu.CompilerParams(vmem_limit_bytes=32 * 1024 * 1024),
        name="exchange",
    )(jnp.concatenate(all_codes), half, *blocks)

    step = 1
    while step < aux:
        ways = 2 if step == 1 or step * 4 > aux else 4
        terms = [parts]
        for way in range(1, ways):
            terms.append(lax.ppermute(parts, "aux", [(i, i ^ (way * step)) for i in range(aux)]))
        while len(terms) > 1:
            terms = [terms[i] + terms[i + 1] for i in range(0, len(terms), 2)]
        parts = terms[0]
        step *= ways
    return parts


def solution(mesh):
    return jax.shard_map(
        shards,
        mesh=mesh,
        in_specs=(
            P("orb", None),
            P("orb", "aux", None, None, None),
            P("orb", "aux", None),
            P("orb", "aux"),
        ),
        out_specs=P("orb", None),
        check_vma=False,
    )
```

```python
import functools

import jax
import jax.numpy as jnp
from jax import lax
from jax.experimental import pallas as pl
from jax.experimental.pallas import tpu as pltpu
from jax.sharding import PartitionSpec as P

BS = 64
LANES = 128
NOTE = 16


def send_to(i, way, count):
    return i ^ way if count & (count - 1) == 0 else (i + way) % count


def source_of(i, way, count):
    return i ^ way if count & (count - 1) == 0 else lax.rem(i - way + count, count)


def pack_kernel(
    orb, pairs_hbm, kept_hbm, density_hbm, blocks_hbm, out_ref, pairs, kept, rows, blocks, sems
):
    sources = (blocks_hbm, density_hbm, pairs_hbm, kept_hbm)
    targets = (blocks, rows, pairs, kept)
    copies = [
        pltpu.make_async_copy(src, dst, sems.at[i])
        for i, (src, dst) in enumerate(zip(sources, targets))
    ]
    for copy in copies:
        copy.start()
    for copy in copies:
        copy.wait()
    slots, aux_width = blocks.shape[2:4]
    square = blocks[0, 0].reshape(slots * aux_width, BS, BS)
    tile = 0
    for pair in range(0, slots * aux_width, 2):
        both = jnp.concatenate([square[pair], square[pair + 1]], axis=1)
        out_ref[tile * BS : (tile + 1) * BS] = both
        tile += 1
    for at in range(0, rows.shape[1], LANES):
        out_ref[tile * BS : (tile + 1) * BS] = rows[:, at : at + LANES]
        tile += 1
    shape = (NOTE, LANES)
    lane = lax.broadcasted_iota(jnp.int32, shape, 1)
    note = jnp.zeros(shape, jnp.int32)
    for j in range(slots):
        note = jnp.where(lane == j, jnp.where(j < kept[0, 0], pairs[0, 0, j], orb), note)
    out_ref[tile * BS :] = note.astype(jnp.float32).astype(jnp.bfloat16)


def exchange_kernel(orb, slots, aux_width, meta_ref, *refs):
    packs, (out_ref, rows, half_ref, held) = refs[:orb], refs[orb:]
    me = lax.axis_index("orb")
    full_width = out_ref.shape[1]
    per_slot = aux_width * BS // LANES

    def tiles(way, first, count):
        return [packs[way][t * BS : (t + 1) * BS] for t in range(first, first + count)]

    for way in range(orb):
        owner = source_of(me, way, orb)
        for t, part in enumerate(tiles(way, slots * per_slot, full_width // LANES)):
            rows[owner, :, t * LANES : (t + 1) * LANES] = part
    rows[orb] = jnp.zeros_like(rows[orb])
    selected = jnp.concatenate([rows[meta_ref[j]] for j in range(slots)], axis=0)
    own = jnp.concatenate(tiles(0, 0, slots * per_slot), axis=1)
    left = []
    for p in range(aux_width):
        cuts = [(j * aux_width + p) * BS for j in range(slots)]
        left.append(jnp.concatenate([own[:, cut : cut + BS] for cut in cuts], axis=1))
    left = jnp.concatenate(left, axis=0)
    half = jnp.dot(left, selected, preferred_element_type=jnp.float32).astype(jnp.bfloat16)
    for k in range(orb):
        half_ref[k] = jnp.concatenate(
            [half[p * BS : (p + 1) * BS, k * BS : (k + 1) * BS] for p in range(aux_width)],
            axis=1,
        )
    half_ref[orb] = jnp.zeros_like(half_ref[orb])
    for way in range(orb):
        total = None
        for j in range(slots):
            term = lax.dot_general(
                half_ref[meta_ref[way * slots + j]],
                jnp.concatenate(tiles(way, j * per_slot, per_slot), axis=1),
                (((1,), (1,)), ((), ())),
                preferred_element_type=jnp.float32,
            )
            total = term if total is None else total + term
        held[source_of(me, way, orb)] = total
    out_ref[...] = jnp.concatenate([held[n] for n in range(orb)], axis=1)


def shards(density, tensor_blocks, pairs, kept):
    full_width = density.shape[1]
    slots = tensor_blocks.shape[2]
    aux_width = tensor_blocks.shape[3]
    orb = lax.axis_size("orb")
    aux = lax.axis_size("aux")
    size = (slots * aux_width * BS + full_width) // LANES * BS
    vmem = pl.BlockSpec(memory_space=pltpu.VMEM)
    smem = pl.BlockSpec(memory_space=pltpu.SMEM)
    params = pltpu.CompilerParams(vmem_limit_bytes=32 * 1024 * 1024)

    packed = pl.pallas_call(
        functools.partial(pack_kernel, orb),
        out_shape=jax.ShapeDtypeStruct((size + NOTE, LANES), jnp.bfloat16),
        in_specs=[pl.BlockSpec(memory_space=pltpu.HBM)] * 4,
        out_specs=vmem,
        scratch_shapes=[
            pltpu.SMEM(pairs.shape, jnp.int32),
            pltpu.SMEM(kept.shape, jnp.int32),
            pltpu.VMEM(density.shape, jnp.bfloat16),
            pltpu.VMEM(tensor_blocks.shape, jnp.bfloat16),
            pltpu.SemaphoreType.DMA((4,)),
        ],
        compiler_params=params,
        name="pack",
    )(pairs, kept, density, tensor_blocks)
    packs = [packed]
    for way in range(1, orb):
        packs.append(lax.ppermute(packed, "orb", [(i, send_to(i, way, orb)) for i in range(orb)]))
    codes = jnp.concatenate([pack[size, :slots] for pack in packs]).astype(jnp.int32)

    parts = pl.pallas_call(
        functools.partial(exchange_kernel, orb, slots, aux_width),
        out_shape=jax.ShapeDtypeStruct((BS, full_width), jnp.float32),
        in_specs=[smem] + [vmem] * orb,
        out_specs=vmem,
        scratch_shapes=[
            pltpu.VMEM((orb + 1, BS, full_width), jnp.bfloat16),
            pltpu.VMEM((orb + 1, BS, aux_width * BS), jnp.bfloat16),
            pltpu.VMEM((orb, BS, BS), jnp.float32),
        ],
        compiler_params=params,
        name="exchange",
    )(codes, *packs)

    step = 1
    while step < aux:
        ways = 2 if step == 1 or step * 4 > aux else 4
        terms = [parts]
        for way in range(1, ways):
            terms.append(lax.ppermute(parts, "aux", [(i, i ^ (way * step)) for i in range(aux)]))
        while len(terms) > 1:
            terms = [terms[i] + terms[i + 1] for i in range(0, len(terms), 2)]
        parts = terms[0]
        step *= ways
    return parts


def solution(mesh):
    return jax.shard_map(
        shards,
        mesh=mesh,
        in_specs=(
            P("orb", None),
            P("orb", "aux", None, None, None),
            P("orb", "aux", None),
            P("orb", "aux"),
        ),
        out_specs=P("orb", None),
        check_vma=False,
    )
```

```python
import functools

import jax
import jax.numpy as jnp
from jax import lax
from jax.experimental import pallas as pl
from jax.experimental.pallas import tpu as pltpu
from jax.sharding import PartitionSpec as P

BS = 64
LANES = 128
NOTE = 16


def pack_kernel(orb, kept, pairs_hbm, density_hbm, blocks_hbm, out_ref, pairs, rows, blocks, sems):
    copies = [
        pltpu.make_async_copy(src, dst, sems.at[i])
        for i, (src, dst) in enumerate(
            ((blocks_hbm, blocks), (density_hbm, rows), (pairs_hbm, pairs))
        )
    ]
    for copy in copies:
        copy.start()
    for copy in copies:
        copy.wait()
    slots, aux_width = blocks.shape[2:4]
    square = blocks[0, 0].reshape(slots * aux_width, BS, BS)
    tile = 0
    for pair in range(0, slots * aux_width, 2):
        both = jnp.concatenate([square[pair], square[pair + 1]], axis=1)
        out_ref[tile * BS : (tile + 1) * BS] = both
        tile += 1
    for at in range(0, rows.shape[1], LANES):
        out_ref[tile * BS : (tile + 1) * BS] = rows[:, at : at + LANES]
        tile += 1
    shape = (NOTE, LANES)
    lane = lax.broadcasted_iota(jnp.int32, shape, 1)
    note = jnp.zeros(shape, jnp.int32)
    for j in range(slots):
        note = jnp.where(lane == j, jnp.where(j < kept[0, 0], pairs[0, 0, j], orb), note)
    out_ref[tile * BS :] = note.astype(jnp.float32).astype(jnp.bfloat16)


def exchange_kernel(orb, slots, aux_width, meta_ref, *refs):
    packs, (out_ref, rows, half_ref, held) = refs[:orb], refs[orb:]
    me = lax.axis_index("orb")
    full_width = out_ref.shape[1]
    per_slot = aux_width * BS // LANES

    def tiles(way, first, count):
        return [packs[way][t * BS : (t + 1) * BS] for t in range(first, first + count)]

    for way in range(orb):
        owner = lax.rem(me - way + orb, orb)
        for t, part in enumerate(tiles(way, slots * per_slot, full_width // LANES)):
            rows[owner, :, t * LANES : (t + 1) * LANES] = part
    rows[orb] = jnp.zeros_like(rows[orb])
    selected = jnp.concatenate([rows[meta_ref[j]] for j in range(slots)], axis=0)
    own = jnp.concatenate(tiles(0, 0, slots * per_slot), axis=1)
    left = []
    for p in range(aux_width):
        cuts = [(j * aux_width + p) * BS for j in range(slots)]
        left.append(jnp.concatenate([own[:, cut : cut + BS] for cut in cuts], axis=1))
    left = jnp.concatenate(left, axis=0)
    half = jnp.dot(left, selected, preferred_element_type=jnp.float32).astype(jnp.bfloat16)
    for k in range(orb):
        half_ref[k] = jnp.concatenate(
            [half[p * BS : (p + 1) * BS, k * BS : (k + 1) * BS] for p in range(aux_width)],
            axis=1,
        )
    half_ref[orb] = jnp.zeros_like(half_ref[orb])
    for way in range(orb):
        total = None
        for j in range(slots):
            term = lax.dot_general(
                half_ref[meta_ref[way * slots + j]],
                jnp.concatenate(tiles(way, j * per_slot, per_slot), axis=1),
                (((1,), (1,)), ((), ())),
                preferred_element_type=jnp.float32,
            )
            total = term if total is None else total + term
        held[lax.rem(me - way + orb, orb)] = total
    out_ref[...] = jnp.concatenate([held[n] for n in range(orb)], axis=1)


def shards(density, tensor_blocks, pairs, kept):
    full_width = density.shape[1]
    slots = tensor_blocks.shape[2]
    aux_width = tensor_blocks.shape[3]
    orb = lax.axis_size("orb")
    aux = lax.axis_size("aux")
    size = (slots * aux_width * BS + full_width) // LANES * BS
    vmem = pl.BlockSpec(memory_space=pltpu.VMEM)
    smem = pl.BlockSpec(memory_space=pltpu.SMEM)
    params = pltpu.CompilerParams(vmem_limit_bytes=32 * 1024 * 1024)

    packed = pl.pallas_call(
        functools.partial(pack_kernel, orb),
        out_shape=jax.ShapeDtypeStruct((size + NOTE, LANES), jnp.bfloat16),
        in_specs=[smem] + [pl.BlockSpec(memory_space=pltpu.HBM)] * 3,
        out_specs=vmem,
        scratch_shapes=[
            pltpu.SMEM(pairs.shape, jnp.int32),
            pltpu.VMEM(density.shape, jnp.bfloat16),
            pltpu.VMEM(tensor_blocks.shape, jnp.bfloat16),
            pltpu.SemaphoreType.DMA((3,)),
        ],
        compiler_params=params,
        name="pack",
    )(kept, *(pltpu.with_memory_space_constraint(a, pltpu.HBM) for a in (pairs, density, tensor_blocks)))
    packs = [packed]
    for way in range(1, orb):
        packs.append(lax.ppermute(packed, "orb", [(i, (i + way) % orb) for i in range(orb)]))
    codes = jnp.concatenate([pack[size, :slots] for pack in packs]).astype(jnp.int32)

    parts = pl.pallas_call(
        functools.partial(exchange_kernel, orb, slots, aux_width),
        out_shape=jax.ShapeDtypeStruct((BS, full_width), jnp.float32),
        in_specs=[smem] + [vmem] * orb,
        out_specs=vmem,
        scratch_shapes=[
            pltpu.VMEM((orb + 1, BS, full_width), jnp.bfloat16),
            pltpu.VMEM((orb + 1, BS, aux_width * BS), jnp.bfloat16),
            pltpu.VMEM((orb, BS, BS), jnp.float32),
        ],
        compiler_params=params,
        name="exchange",
    )(codes, *packs)

    step = 1
    while step < aux:
        ways = 2 if step == 1 or step * 4 > aux else 4
        terms = [parts]
        for way in range(1, ways):
            terms.append(lax.ppermute(parts, "aux", [(i, i ^ (way * step)) for i in range(aux)]))
        while len(terms) > 1:
            terms = [terms[i] + terms[i + 1] for i in range(0, len(terms), 2)]
        parts = terms[0]
        step *= ways
    return parts


def solution(mesh):
    return jax.shard_map(
        shards,
        mesh=mesh,
        in_specs=(
            P("orb", None),
            P("orb", "aux", None, None, None),
            P("orb", "aux", None),
            P("orb", "aux"),
        ),
        out_specs=P("orb", None),
        check_vma=False,
    )
```

```python
import functools

import jax
import jax.numpy as jnp
from jax import lax
from jax.experimental import pallas as pl
from jax.experimental.pallas import tpu as pltpu
from jax.sharding import PartitionSpec as P

BS = 64
LANES = 128
NOTE = 16


def pack_kernel(orb, kept, pairs_hbm, density_hbm, blocks_hbm, out_ref, pairs, rows, blocks, sems):
    copies = [
        pltpu.make_async_copy(src, dst, sems.at[i])
        for i, (src, dst) in enumerate(
            ((blocks_hbm, blocks), (density_hbm, rows), (pairs_hbm, pairs))
        )
    ]
    for copy in copies:
        copy.start()
    for copy in copies:
        copy.wait()
    slots, aux_width = blocks.shape[2:4]
    square = blocks[0, 0].reshape(slots * aux_width, BS, BS)
    tile = 0
    for pair in range(0, slots * aux_width, 2):
        both = jnp.concatenate([square[pair], square[pair + 1]], axis=1)
        out_ref[tile * BS : (tile + 1) * BS] = both
        tile += 1
    for at in range(0, rows.shape[1], LANES):
        out_ref[tile * BS : (tile + 1) * BS] = rows[:, at : at + LANES]
        tile += 1
    shape = (NOTE, LANES)
    lane = lax.broadcasted_iota(jnp.int32, shape, 1)
    note = jnp.zeros(shape, jnp.int32)
    for j in range(slots):
        note = jnp.where(lane == j, jnp.where(j < kept[0, 0], pairs[0, 0, j], orb), note)
    out_ref[tile * BS :] = note.astype(jnp.float32).astype(jnp.bfloat16)


def exchange_kernel(slots, aux_width, meta_ref, packs, out_ref, rows, half_ref):
    orb = packs.shape[0]
    me = lax.axis_index("orb")
    full_width = out_ref.shape[1]
    per_slot = aux_width * BS // LANES

    def tiles(owner, first, count):
        return [packs[owner, t * BS : (t + 1) * BS] for t in range(first, first + count)]

    for owner in range(orb):
        for t, part in enumerate(tiles(owner, slots * per_slot, full_width // LANES)):
            rows[owner, :, t * LANES : (t + 1) * LANES] = part
    rows[orb] = jnp.zeros_like(rows[orb])
    selected = [rows[meta_ref[me * slots + j]] for j in range(slots)]
    selected = jnp.concatenate(selected, axis=0)
    own = jnp.concatenate(tiles(me, 0, slots * per_slot), axis=1)
    left = []
    for p in range(aux_width):
        cuts = [(j * aux_width + p) * BS for j in range(slots)]
        left.append(jnp.concatenate([own[:, cut : cut + BS] for cut in cuts], axis=1))
    left = jnp.concatenate(left, axis=0)
    half = jnp.dot(left, selected, preferred_element_type=jnp.float32).astype(jnp.bfloat16)
    for k in range(orb):
        half_ref[k] = jnp.concatenate(
            [half[p * BS : (p + 1) * BS, k * BS : (k + 1) * BS] for p in range(aux_width)],
            axis=1,
        )
    half_ref[orb] = jnp.zeros_like(half_ref[orb])
    columns = []
    for owner in range(orb):
        total = None
        for j in range(slots):
            term = lax.dot_general(
                half_ref[meta_ref[owner * slots + j]],
                jnp.concatenate(tiles(owner, j * per_slot, per_slot), axis=1),
                (((1,), (1,)), ((), ())),
                preferred_element_type=jnp.float32,
            )
            total = term if total is None else total + term
        columns.append(total)
    out_ref[...] = jnp.concatenate(columns, axis=1)


def shards(density, tensor_blocks, pairs, kept):
    full_width = density.shape[1]
    slots = tensor_blocks.shape[2]
    aux_width = tensor_blocks.shape[3]
    orb = lax.axis_size("orb")
    aux = lax.axis_size("aux")
    size = (slots * aux_width * BS + full_width) // LANES * BS
    vmem = pl.BlockSpec(memory_space=pltpu.VMEM)
    smem = pl.BlockSpec(memory_space=pltpu.SMEM)
    params = pltpu.CompilerParams(vmem_limit_bytes=32 * 1024 * 1024)

    packed = pl.pallas_call(
        functools.partial(pack_kernel, orb),
        out_shape=jax.ShapeDtypeStruct((size + NOTE, LANES), jnp.bfloat16),
        in_specs=[smem] + [pl.BlockSpec(memory_space=pltpu.HBM)] * 3,
        out_specs=vmem,
        scratch_shapes=[
            pltpu.SMEM(pairs.shape, jnp.int32),
            pltpu.VMEM(density.shape, jnp.bfloat16),
            pltpu.VMEM(tensor_blocks.shape, jnp.bfloat16),
            pltpu.SemaphoreType.DMA((3,)),
        ],
        compiler_params=params,
        name="pack",
    )(kept, *(pltpu.with_memory_space_constraint(a, pltpu.HBM) for a in (pairs, density, tensor_blocks)))
    copies = jnp.broadcast_to(packed, (orb, *packed.shape))
    packs = lax.all_to_all(copies, "orb", 0, 0)
    codes = packs[:, size, :slots].astype(jnp.int32).reshape(orb * slots)

    parts = pl.pallas_call(
        functools.partial(exchange_kernel, slots, aux_width),
        out_shape=jax.ShapeDtypeStruct((BS, full_width), jnp.float32),
        in_specs=[smem, vmem],
        out_specs=vmem,
        scratch_shapes=[
            pltpu.VMEM((orb + 1, BS, full_width), jnp.bfloat16),
            pltpu.VMEM((orb + 1, BS, aux_width * BS), jnp.bfloat16),
        ],
        compiler_params=params,
        name="exchange",
    )(codes, packs)

    step = 1
    while step < aux:
        ways = 2 if step == 1 or step * 4 > aux else 4
        terms = [parts]
        for way in range(1, ways):
            terms.append(lax.ppermute(parts, "aux", [(i, i ^ (way * step)) for i in range(aux)]))
        while len(terms) > 1:
            terms = [terms[i] + terms[i + 1] for i in range(0, len(terms), 2)]
        parts = terms[0]
        step *= ways
    return parts


def solution(mesh):
    return jax.shard_map(
        shards,
        mesh=mesh,
        in_specs=(
            P("orb", None),
            P("orb", "aux", None, None, None),
            P("orb", "aux", None),
            P("orb", "aux"),
        ),
        out_specs=P("orb", None),
        check_vma=False,
    )
```

```python
import functools

import jax
import jax.numpy as jnp
from jax import lax
from jax.experimental import pallas as pl
from jax.experimental.pallas import tpu as pltpu
from jax.sharding import PartitionSpec as P

BS = 64
LANES = 128
NOTE = 16


def pack_kernel(orb, kept, pairs_hbm, density_hbm, blocks_hbm, out_ref, pairs, rows, blocks, sems):
    copies = [
        pltpu.make_async_copy(src, dst, sems.at[i])
        for i, (src, dst) in enumerate(
            ((blocks_hbm, blocks), (density_hbm, rows), (pairs_hbm, pairs))
        )
    ]
    for copy in copies:
        copy.start()
    for copy in copies:
        copy.wait()
    slots, aux_width = blocks.shape[2:4]
    square = blocks[0, 0].reshape(slots * aux_width, BS, BS)
    tile = 0
    for pair in range(0, slots * aux_width, 2):
        both = jnp.concatenate([square[pair], square[pair + 1]], axis=1)
        out_ref[tile * BS : (tile + 1) * BS] = both
        tile += 1
    for at in range(0, rows.shape[1], LANES):
        out_ref[tile * BS : (tile + 1) * BS] = rows[:, at : at + LANES]
        tile += 1
    shape = (NOTE, LANES)
    lane = lax.broadcasted_iota(jnp.int32, shape, 1)
    note = jnp.zeros(shape, jnp.int32)
    for j in range(slots):
        note = jnp.where(lane == j, jnp.where(j < kept[0, 0], pairs[0, 0, j], orb), note)
    out_ref[tile * BS :] = note.astype(jnp.float32).astype(jnp.bfloat16)


def exchange_kernel(orb, slots, aux_width, meta_ref, *refs):
    packs, (out_ref, rows, half_ref, held) = refs[:orb], refs[orb:]
    me = lax.axis_index("orb")
    full_width = out_ref.shape[1]
    per_slot = aux_width * BS // LANES

    def tiles(way, first, count):
        return [packs[way][t * BS : (t + 1) * BS] for t in range(first, first + count)]

    for way in range(orb):
        owner = lax.rem(me - way + orb, orb)
        for t, part in enumerate(tiles(way, slots * per_slot, full_width // LANES)):
            rows[owner, :, t * LANES : (t + 1) * LANES] = part
    rows[orb] = jnp.zeros_like(rows[orb])
    selected = jnp.concatenate([rows[meta_ref[j]] for j in range(slots)], axis=0)
    own = jnp.concatenate(tiles(0, 0, slots * per_slot), axis=1)
    left = []
    for p in range(aux_width):
        cuts = [(j * aux_width + p) * BS for j in range(slots)]
        left.append(jnp.concatenate([own[:, cut : cut + BS] for cut in cuts], axis=1))
    left = jnp.concatenate(left, axis=0)
    half = jnp.dot(left, selected, preferred_element_type=jnp.float32).astype(jnp.bfloat16)
    for k in range(orb):
        half_ref[k] = jnp.concatenate(
            [half[p * BS : (p + 1) * BS, k * BS : (k + 1) * BS] for p in range(aux_width)],
            axis=1,
        )
    half_ref[orb] = jnp.zeros_like(half_ref[orb])
    for way in range(orb):
        total = None
        for j in range(slots):
            term = lax.dot_general(
                half_ref[meta_ref[way * slots + j]],
                jnp.concatenate(tiles(way, j * per_slot, per_slot), axis=1),
                (((1,), (1,)), ((), ())),
                preferred_element_type=jnp.float32,
            )
            total = term if total is None else total + term
        held[lax.rem(me - way + orb, orb)] = total
    out_ref[...] = jnp.concatenate([held[n] for n in range(orb)], axis=1)


def shards(density, tensor_blocks, pairs, kept):
    full_width = density.shape[1]
    slots = tensor_blocks.shape[2]
    aux_width = tensor_blocks.shape[3]
    orb = lax.axis_size("orb")
    aux = lax.axis_size("aux")
    size = (slots * aux_width * BS + full_width) // LANES * BS
    vmem = pl.BlockSpec(memory_space=pltpu.VMEM)
    smem = pl.BlockSpec(memory_space=pltpu.SMEM)
    params = pltpu.CompilerParams(vmem_limit_bytes=32 * 1024 * 1024)

    packed = pl.pallas_call(
        functools.partial(pack_kernel, orb),
        out_shape=jax.ShapeDtypeStruct((size + NOTE, LANES), jnp.bfloat16),
        in_specs=[smem] + [pl.BlockSpec(memory_space=pltpu.HBM)] * 3,
        out_specs=vmem,
        scratch_shapes=[
            pltpu.SMEM(pairs.shape, jnp.int32),
            pltpu.VMEM(density.shape, jnp.bfloat16),
            pltpu.VMEM(tensor_blocks.shape, jnp.bfloat16),
            pltpu.SemaphoreType.DMA((3,)),
        ],
        compiler_params=params,
        name="pack",
    )(kept, *(pltpu.with_memory_space_constraint(a, pltpu.HBM) for a in (pairs, density, tensor_blocks)))
    packs = [packed]
    for way in range(1, orb):
        packs.append(lax.ppermute(packed, "orb", [(i, (i + way) % orb) for i in range(orb)]))
    codes = jnp.concatenate([pack[size, :slots] for pack in packs]).astype(jnp.int32)

    parts = pl.pallas_call(
        functools.partial(exchange_kernel, orb, slots, aux_width),
        out_shape=jax.ShapeDtypeStruct((BS, full_width), jnp.float32),
        in_specs=[smem] + [vmem] * orb,
        out_specs=vmem,
        scratch_shapes=[
            pltpu.VMEM((orb + 1, BS, full_width), jnp.bfloat16),
            pltpu.VMEM((orb + 1, BS, aux_width * BS), jnp.bfloat16),
            pltpu.VMEM((orb, BS, BS), jnp.float32),
        ],
        compiler_params=params,
        name="exchange",
    )(codes, *packs)

    step = 1
    while step < aux:
        ways = 2 if step == 1 or step * 4 > aux else 4
        if step == 2:
            parts = parts.astype(jnp.bfloat16)
        terms = [parts]
        for way in range(1, ways):
            terms.append(lax.ppermute(parts, "aux", [(i, i ^ (way * step)) for i in range(aux)]))
        terms = [term.astype(jnp.float32) for term in terms]
        while len(terms) > 1:
            terms = [terms[i] + terms[i + 1] for i in range(0, len(terms), 2)]
        parts = terms[0]
        step *= ways
    return parts


def solution(mesh):
    return jax.shard_map(
        shards,
        mesh=mesh,
        in_specs=(
            P("orb", None),
            P("orb", "aux", None, None, None),
            P("orb", "aux", None),
            P("orb", "aux"),
        ),
        out_specs=P("orb", None),
        check_vma=False,
    )
```

```python
import functools

import jax
import jax.numpy as jnp
from jax import lax
from jax.experimental import pallas as pl
from jax.experimental.pallas import tpu as pltpu
from jax.sharding import PartitionSpec as P

BS = 64
LANES = 128
NOTE = 16


def lay_blocks(raw, out_ref):
    slots, aux_width = raw.shape[:2]
    square = raw.reshape(slots * aux_width, BS, BS)
    for tile in range(slots * aux_width // 2):
        both = jnp.concatenate([square[2 * tile], square[2 * tile + 1]], axis=1)
        out_ref[tile * BS : (tile + 1) * BS] = both
    return slots * aux_width // 2


def pack_kernel(
    orb, kept, pairs_hbm, density_hbm, blocks_hbm, out_ref, tail_ref, pairs, rows, blocks, sems
):
    copies = [
        pltpu.make_async_copy(src, dst, sems.at[i])
        for i, (src, dst) in enumerate(
            ((blocks_hbm, blocks), (density_hbm, rows), (pairs_hbm, pairs))
        )
    ]
    for copy in copies:
        copy.start()
    for copy in copies:
        copy.wait()
    slots = blocks.shape[2]
    tile = lay_blocks(blocks[0, 0], out_ref)
    for at in range(0, rows.shape[1], LANES):
        part = rows[:, at : at + LANES]
        out_ref[tile * BS : (tile + 1) * BS] = part
        tail_ref[at // LANES * BS : (at // LANES + 1) * BS] = part
        tile += 1
    shape = (NOTE, LANES)
    lane = lax.broadcasted_iota(jnp.int32, shape, 1)
    note = jnp.zeros(shape, jnp.int32)
    for j in range(slots):
        note = jnp.where(lane == j, jnp.where(j < kept[0, 0], pairs[0, 0, j], orb), note)
    note = note.astype(jnp.float32).astype(jnp.bfloat16)
    out_ref[tile * BS :] = note
    tail_ref[rows.shape[1] // LANES * BS :] = note


def relay_kernel(blocks, out_ref):
    lay_blocks(blocks[0, 0], out_ref)


def exchange_kernel(orb, slots, aux_width, meta_ref, *refs):
    packs, tails, (out_ref, rows, half_ref, held) = refs[:orb], refs[orb : 2 * orb], refs[2 * orb :]
    me = lax.axis_index("orb")
    full_width = out_ref.shape[1]
    per_slot = aux_width * BS // LANES
    count = full_width // LANES

    def tiles(way, first, count):
        return [packs[way][t * BS : (t + 1) * BS] for t in range(first, first + count)]

    for way in range(orb):
        owner = lax.rem(me - way + orb, orb)
        first = tails[way].shape[0] - NOTE - count * BS
        for t in range(count):
            rows[owner, :, t * LANES : (t + 1) * LANES] = tails[way][
                first + t * BS : first + (t + 1) * BS
            ]
    rows[orb] = jnp.zeros_like(rows[orb])
    selected = jnp.concatenate([rows[meta_ref[j]] for j in range(slots)], axis=0)
    own = jnp.concatenate(tiles(0, 0, slots * per_slot), axis=1)
    left = []
    for p in range(aux_width):
        cuts = [(j * aux_width + p) * BS for j in range(slots)]
        left.append(jnp.concatenate([own[:, cut : cut + BS] for cut in cuts], axis=1))
    left = jnp.concatenate(left, axis=0)
    half = jnp.dot(left, selected, preferred_element_type=jnp.float32).astype(jnp.bfloat16)
    for k in range(orb):
        half_ref[k] = jnp.concatenate(
            [half[p * BS : (p + 1) * BS, k * BS : (k + 1) * BS] for p in range(aux_width)],
            axis=1,
        )
    half_ref[orb] = jnp.zeros_like(half_ref[orb])
    for way in range(orb):
        total = None
        for j in range(slots):
            term = lax.dot_general(
                half_ref[meta_ref[way * slots + j]],
                jnp.concatenate(tiles(way, j * per_slot, per_slot), axis=1),
                (((1,), (1,)), ((), ())),
                preferred_element_type=jnp.float32,
            )
            total = term if total is None else total + term
        held[lax.rem(me - way + orb, orb)] = total
    out_ref[...] = jnp.concatenate([held[n] for n in range(orb)], axis=1)


def shards(density, tensor_blocks, pairs, kept):
    full_width = density.shape[1]
    slots = tensor_blocks.shape[2]
    aux_width = tensor_blocks.shape[3]
    orb = lax.axis_size("orb")
    aux = lax.axis_size("aux")
    size = (slots * aux_width * BS + full_width) // LANES * BS
    vmem = pl.BlockSpec(memory_space=pltpu.VMEM)
    smem = pl.BlockSpec(memory_space=pltpu.SMEM)
    params = pltpu.CompilerParams(vmem_limit_bytes=32 * 1024 * 1024)

    packed, tail = pl.pallas_call(
        functools.partial(pack_kernel, orb),
        out_shape=[
            jax.ShapeDtypeStruct((rows + NOTE, LANES), jnp.bfloat16)
            for rows in (size, full_width // LANES * BS)
        ],
        in_specs=[smem] + [pl.BlockSpec(memory_space=pltpu.HBM)] * 3,
        out_specs=[vmem, vmem],
        scratch_shapes=[
            pltpu.SMEM(pairs.shape, jnp.int32),
            pltpu.VMEM(density.shape, jnp.bfloat16),
            pltpu.VMEM(tensor_blocks.shape, jnp.bfloat16),
            pltpu.SemaphoreType.DMA((3,)),
        ],
        compiler_params=params,
        name="pack",
    )(kept, *(pltpu.with_memory_space_constraint(a, pltpu.HBM) for a in (pairs, density, tensor_blocks)))
    packs, tails = [packed], [packed]
    for way in range(1, orb):
        perm = [(i, (i + way) % orb) for i in range(orb)]
        if way == orb // 2:
            raw = lax.ppermute(tensor_blocks, "orb", perm)
            packs.append(
                pl.pallas_call(
                    relay_kernel,
                    out_shape=jax.ShapeDtypeStruct(
                        (slots * aux_width * BS * BS // LANES, LANES), jnp.bfloat16
                    ),
                    in_specs=[vmem],
                    out_specs=vmem,
                    compiler_params=params,
                    name="relay",
                )(raw)
            )
            tails.append(lax.ppermute(tail, "orb", perm))
        else:
            packs.append(lax.ppermute(packed, "orb", perm))
            tails.append(packs[-1])
    codes = jnp.concatenate([pack[-NOTE, :slots] for pack in tails]).astype(jnp.int32)

    parts = pl.pallas_call(
        functools.partial(exchange_kernel, orb, slots, aux_width),
        out_shape=jax.ShapeDtypeStruct((BS, full_width), jnp.float32),
        in_specs=[smem] + [vmem] * (2 * orb),
        out_specs=vmem,
        scratch_shapes=[
            pltpu.VMEM((orb + 1, BS, full_width), jnp.bfloat16),
            pltpu.VMEM((orb + 1, BS, aux_width * BS), jnp.bfloat16),
            pltpu.VMEM((orb, BS, BS), jnp.float32),
        ],
        compiler_params=params,
        name="exchange",
    )(codes, *packs, *tails)

    step = 1
    while step < aux:
        ways = 2 if step == 1 or step * 4 > aux else 4
        terms = [parts]
        for way in range(1, ways):
            terms.append(lax.ppermute(parts, "aux", [(i, i ^ (way * step)) for i in range(aux)]))
        while len(terms) > 1:
            terms = [terms[i] + terms[i + 1] for i in range(0, len(terms), 2)]
        parts = terms[0]
        step *= ways
    return parts


def solution(mesh):
    return jax.shard_map(
        shards,
        mesh=mesh,
        in_specs=(
            P("orb", None),
            P("orb", "aux", None, None, None),
            P("orb", "aux", None),
            P("orb", "aux"),
        ),
        out_specs=P("orb", None),
        check_vma=False,
    )
```

```python
import functools

import jax
import jax.numpy as jnp
from jax import lax
from jax.experimental import pallas as pl
from jax.experimental.pallas import tpu as pltpu
from jax.sharding import PartitionSpec as P

BS = 64
LANES = 128
NOTE = 16


def routes(orb):
    if orb == 4:
        return [(0, 1, 2, 3), (1, 3, 0, 2), (2, 0, 3, 1), (3, 2, 1, 0)]
    return [tuple((i + way) % orb for i in range(orb)) for way in range(orb)]


def owner_of(me, way, orb):
    if orb == 4:
        route = routes(orb)[way]
        owner = jnp.int32(route.index(0))
        for i in range(1, orb):
            owner = jnp.where(me == i, route.index(i), owner)
        return owner
    return lax.rem(me - way + orb, orb)


def lay_blocks(raw, out_ref):
    slots, aux_width = raw.shape[:2]
    square = raw.reshape(slots * aux_width, BS, BS)
    for tile in range(slots * aux_width // 2):
        both = jnp.concatenate([square[2 * tile], square[2 * tile + 1]], axis=1)
        out_ref[tile * BS : (tile + 1) * BS] = both
    return slots * aux_width // 2


def pack_kernel(
    orb, kept, pairs_hbm, density_hbm, blocks_hbm, out_ref, tail_ref, pairs, rows, blocks, sems
):
    copies = [
        pltpu.make_async_copy(src, dst, sems.at[i])
        for i, (src, dst) in enumerate(
            ((blocks_hbm, blocks), (density_hbm, rows), (pairs_hbm, pairs))
        )
    ]
    for copy in copies:
        copy.start()
    for copy in copies:
        copy.wait()
    slots = blocks.shape[2]
    tile = lay_blocks(blocks[0, 0], out_ref)
    for at in range(0, rows.shape[1], LANES):
        part = rows[:, at : at + LANES]
        out_ref[tile * BS : (tile + 1) * BS] = part
        tail_ref[at // LANES * BS : (at // LANES + 1) * BS] = part
        tile += 1
    shape = (NOTE, LANES)
    lane = lax.broadcasted_iota(jnp.int32, shape, 1)
    note = jnp.zeros(shape, jnp.int32)
    for j in range(slots):
        note = jnp.where(lane == j, jnp.where(j < kept[0, 0], pairs[0, 0, j], orb), note)
    note = note.astype(jnp.float32).astype(jnp.bfloat16)
    out_ref[tile * BS :] = note
    tail_ref[rows.shape[1] // LANES * BS :] = note


def relay_kernel(blocks, out_ref):
    lay_blocks(blocks[0, 0], out_ref)


def exchange_kernel(orb, slots, aux_width, meta_ref, *refs):
    packs, tails, (out_ref, rows, half_ref, held) = refs[:orb], refs[orb : 2 * orb], refs[2 * orb :]
    me = lax.axis_index("orb")
    full_width = out_ref.shape[1]
    per_slot = aux_width * BS // LANES
    count = full_width // LANES

    def tiles(way, first, count):
        return [packs[way][t * BS : (t + 1) * BS] for t in range(first, first + count)]

    for way in range(orb):
        owner = owner_of(me, way, orb)
        first = tails[way].shape[0] - NOTE - count * BS
        for t in range(count):
            rows[owner, :, t * LANES : (t + 1) * LANES] = tails[way][
                first + t * BS : first + (t + 1) * BS
            ]
    rows[orb] = jnp.zeros_like(rows[orb])
    selected = jnp.concatenate([rows[meta_ref[j]] for j in range(slots)], axis=0)
    own = jnp.concatenate(tiles(0, 0, slots * per_slot), axis=1)
    left = []
    for p in range(aux_width):
        cuts = [(j * aux_width + p) * BS for j in range(slots)]
        left.append(jnp.concatenate([own[:, cut : cut + BS] for cut in cuts], axis=1))
    left = jnp.concatenate(left, axis=0)
    half = jnp.dot(left, selected, preferred_element_type=jnp.float32).astype(jnp.bfloat16)
    for k in range(orb):
        half_ref[k] = jnp.concatenate(
            [half[p * BS : (p + 1) * BS, k * BS : (k + 1) * BS] for p in range(aux_width)],
            axis=1,
        )
    half_ref[orb] = jnp.zeros_like(half_ref[orb])
    for way in range(orb):
        total = None
        for j in range(slots):
            term = lax.dot_general(
                half_ref[meta_ref[way * slots + j]],
                jnp.concatenate(tiles(way, j * per_slot, per_slot), axis=1),
                (((1,), (1,)), ((), ())),
                preferred_element_type=jnp.float32,
            )
            total = term if total is None else total + term
        held[owner_of(me, way, orb)] = total
    out_ref[...] = jnp.concatenate([held[n] for n in range(orb)], axis=1)


def shards(density, tensor_blocks, pairs, kept):
    full_width = density.shape[1]
    slots = tensor_blocks.shape[2]
    aux_width = tensor_blocks.shape[3]
    orb = lax.axis_size("orb")
    aux = lax.axis_size("aux")
    size = (slots * aux_width * BS + full_width) // LANES * BS
    vmem = pl.BlockSpec(memory_space=pltpu.VMEM)
    smem = pl.BlockSpec(memory_space=pltpu.SMEM)
    params = pltpu.CompilerParams(vmem_limit_bytes=32 * 1024 * 1024)

    packed, tail = pl.pallas_call(
        functools.partial(pack_kernel, orb),
        out_shape=[
            jax.ShapeDtypeStruct((rows + NOTE, LANES), jnp.bfloat16)
            for rows in (size, full_width // LANES * BS)
        ],
        in_specs=[smem] + [pl.BlockSpec(memory_space=pltpu.HBM)] * 3,
        out_specs=[vmem, vmem],
        scratch_shapes=[
            pltpu.SMEM(pairs.shape, jnp.int32),
            pltpu.VMEM(density.shape, jnp.bfloat16),
            pltpu.VMEM(tensor_blocks.shape, jnp.bfloat16),
            pltpu.SemaphoreType.DMA((3,)),
        ],
        compiler_params=params,
        name="pack",
    )(kept, *(pltpu.with_memory_space_constraint(a, pltpu.HBM) for a in (pairs, density, tensor_blocks)))
    packs, tails = [packed], [packed]
    for way in range(1, orb):
        perm = list(enumerate(routes(orb)[way]))
        if way == 1:
            raw = lax.ppermute(tensor_blocks, "orb", perm)
            packs.append(
                pl.pallas_call(
                    relay_kernel,
                    out_shape=jax.ShapeDtypeStruct(
                        (slots * aux_width * BS * BS // LANES, LANES), jnp.bfloat16
                    ),
                    in_specs=[vmem],
                    out_specs=vmem,
                    compiler_params=params,
                    name="relay",
                )(raw)
            )
            tails.append(lax.ppermute(tail, "orb", perm))
        else:
            packs.append(lax.ppermute(packed, "orb", perm))
            tails.append(packs[-1])
    codes = jnp.concatenate([pack[-NOTE, :slots] for pack in tails]).astype(jnp.int32)

    parts = pl.pallas_call(
        functools.partial(exchange_kernel, orb, slots, aux_width),
        out_shape=jax.ShapeDtypeStruct((BS, full_width), jnp.float32),
        in_specs=[smem] + [vmem] * (2 * orb),
        out_specs=vmem,
        scratch_shapes=[
            pltpu.VMEM((orb + 1, BS, full_width), jnp.bfloat16),
            pltpu.VMEM((orb + 1, BS, aux_width * BS), jnp.bfloat16),
            pltpu.VMEM((orb, BS, BS), jnp.float32),
        ],
        compiler_params=params,
        name="exchange",
    )(codes, *packs, *tails)

    step = 1
    while step < aux:
        ways = 2 if step == 1 or step * 4 > aux else 4
        terms = [parts]
        for way in range(1, ways):
            terms.append(lax.ppermute(parts, "aux", [(i, i ^ (way * step)) for i in range(aux)]))
        while len(terms) > 1:
            terms = [terms[i] + terms[i + 1] for i in range(0, len(terms), 2)]
        parts = terms[0]
        step *= ways
    return parts


def solution(mesh):
    return jax.shard_map(
        shards,
        mesh=mesh,
        in_specs=(
            P("orb", None),
            P("orb", "aux", None, None, None),
            P("orb", "aux", None),
            P("orb", "aux"),
        ),
        out_specs=P("orb", None),
        check_vma=False,
    )
```

```python
import functools

import jax
import jax.numpy as jnp
from jax import lax
from jax.experimental import pallas as pl
from jax.experimental.pallas import tpu as pltpu
from jax.sharding import PartitionSpec as P

BS = 64
LANES = 128
NOTE = 16


def lay_blocks(raw, out_ref):
    slots, aux_width = raw.shape[:2]
    square = raw.reshape(slots * aux_width, BS, BS)
    for tile in range(slots * aux_width // 2):
        both = jnp.concatenate([square[2 * tile], square[2 * tile + 1]], axis=1)
        out_ref[tile * BS : (tile + 1) * BS] = both
    return slots * aux_width // 2


def pack_kernel(
    orb, kept, pairs_hbm, density_hbm, raw_hbm, out_ref, note_ref, pairs, rows, raw, sems
):
    height = rows.shape[0]
    first = pl.multiple_of(lax.rem(lax.axis_index("aux"), 2) * height, height)
    copies = [
        pltpu.make_async_copy(src, dst, sems.at[i])
        for i, (src, dst) in enumerate(
            (
                (raw_hbm, raw),
                (density_hbm.at[pl.ds(first, height)], rows),
                (pairs_hbm, pairs),
            )
        )
    ]
    for copy in copies:
        copy.start()
    for copy in copies:
        copy.wait()
    lay_blocks(raw[0, 0], out_ref)
    tiles = rows.shape[1] // LANES
    for t in range(tiles):
        note_ref[t * height : (t + 1) * height] = rows[:, t * LANES : (t + 1) * LANES]
    shape = (NOTE, LANES)
    lane = lax.broadcasted_iota(jnp.int32, shape, 1)
    note = jnp.zeros(shape, jnp.int32)
    for j in range(pairs.shape[2]):
        note = jnp.where(lane == j, jnp.where(j < kept[0, 0], pairs[0, 0, j], orb), note)
    note_ref[tiles * height :] = note.astype(jnp.float32).astype(jnp.bfloat16)


def merge_kernel(*refs):
    notes, (parts_ref, codes_ref) = refs[:-2], refs[-2:]
    part = notes[0].shape[0] - NOTE
    codes_ref[0] = notes[0][part:][:8].astype(jnp.float32).astype(jnp.int32)
    for i, note in enumerate(notes[1:]):
        parts_ref[i * part : (i + 1) * part] = note[:part]
        codes_ref[i + 1] = note[part:][:8].astype(jnp.float32).astype(jnp.int32)


def relay_kernel(raw, out_ref):
    lay_blocks(raw[0, 0], out_ref)


def half_kernel(orb, slots, aux_width, meta_ref, density_ref, blocks_ref, *refs):
    own_parts, swapped, half_ref, rows = refs[: orb - 1], refs[orb - 1], refs[orb], refs[orb + 1]
    me = lax.axis_index("orb")
    parity = lax.rem(lax.axis_index("aux"), 2)
    height = BS // 2
    count = density_ref.shape[1] // LANES
    near = pl.multiple_of(parity * height, height)
    far = pl.multiple_of((1 - parity) * height, height)
    rows[me] = density_ref[...]
    for way in range(1, orb):
        owner = lax.rem(me - way + orb, orb)
        for t in range(count):
            lanes = slice(t * LANES, (t + 1) * LANES)
            at = (way - 1) * count + t
            rows[owner, pl.ds(near, height), lanes] = own_parts[way - 1][
                t * height : (t + 1) * height
            ]
            rows[owner, pl.ds(far, height), lanes] = swapped[at * height : (at + 1) * height]
    rows[orb] = jnp.zeros_like(rows[orb])
    selected = jnp.concatenate([rows[meta_ref[j]] for j in range(slots)], axis=0)
    tiles = blocks_ref.shape[0] // BS
    own = jnp.concatenate([blocks_ref[t * BS : (t + 1) * BS] for t in range(tiles)], axis=1)
    left = []
    for p in range(aux_width):
        cuts = [(j * aux_width + p) * BS for j in range(slots)]
        left.append(jnp.concatenate([own[:, cut : cut + BS] for cut in cuts], axis=1))
    left = jnp.concatenate(left, axis=0)
    half = jnp.dot(left, selected, preferred_element_type=jnp.float32).astype(jnp.bfloat16)
    for k in range(orb):
        half_ref[k] = jnp.concatenate(
            [half[p * BS : (p + 1) * BS, k * BS : (k + 1) * BS] for p in range(aux_width)],
            axis=1,
        )
    half_ref[orb] = jnp.zeros_like(half_ref[orb])


def exchange_kernel(orb, slots, aux_width, meta_ref, half_ref, *refs):
    packs, (out_ref, held) = refs[:orb], refs[orb:]
    me = lax.axis_index("orb")
    per_slot = aux_width * BS // LANES
    for way in range(orb):
        total = None
        for j in range(slots):
            tiles = [
                packs[way][t * BS : (t + 1) * BS] for t in range(j * per_slot, (j + 1) * per_slot)
            ]
            term = lax.dot_general(
                half_ref[meta_ref[way * slots + j]],
                jnp.concatenate(tiles, axis=1),
                (((1,), (1,)), ((), ())),
                preferred_element_type=jnp.float32,
            )
            total = term if total is None else total + term
        held[lax.rem(me - way + orb, orb)] = total
    out_ref[...] = jnp.concatenate([held[n] for n in range(orb)], axis=1)


def shards(density, tensor_blocks, pairs, kept):
    full_width = density.shape[1]
    slots = tensor_blocks.shape[2]
    aux_width = tensor_blocks.shape[3]
    orb = lax.axis_size("orb")
    aux = lax.axis_size("aux")
    height = BS // 2
    part = height * full_width // LANES
    size = slots * aux_width * BS // LANES * BS
    vmem = pl.BlockSpec(memory_space=pltpu.VMEM)
    smem = pl.BlockSpec(memory_space=pltpu.SMEM)
    hbm = pl.BlockSpec(memory_space=pltpu.HBM)
    params = pltpu.CompilerParams(vmem_limit_bytes=32 * 1024 * 1024)
    laid = jax.ShapeDtypeStruct((size, LANES), jnp.bfloat16)
    perms = [[(i, (i + way) % orb) for i in range(orb)] for way in range(orb)]

    own, note = pl.pallas_call(
        functools.partial(pack_kernel, orb),
        out_shape=[laid, jax.ShapeDtypeStruct((part + NOTE, LANES), jnp.bfloat16)],
        in_specs=[smem, hbm, hbm, hbm],
        out_specs=[vmem, vmem],
        scratch_shapes=[
            pltpu.SMEM(pairs.shape, jnp.int32),
            pltpu.VMEM((height, full_width), jnp.bfloat16),
            pltpu.VMEM(tensor_blocks.shape, jnp.bfloat16),
            pltpu.SemaphoreType.DMA((3,)),
        ],
        compiler_params=params,
        name="pack",
    )(
        kept,
        *(pltpu.with_memory_space_constraint(a, pltpu.HBM) for a in (pairs, density, tensor_blocks)),
    )
    notes = [note] + [lax.ppermute(note, "orb", perms[way]) for way in range(1, orb)]
    raw = lax.ppermute(tensor_blocks, "orb", perms[orb // 2])
    notes, raw = lax.optimization_barrier((notes, raw))
    packs = [own]
    for way in range(1, orb):
        if way == orb // 2:
            packs.append(
                pl.pallas_call(
                    relay_kernel,
                    out_shape=laid,
                    in_specs=[vmem],
                    out_specs=vmem,
                    compiler_params=params,
                    name="relay",
                )(raw)
            )
        else:
            packs.append(lax.ppermute(own, "orb", perms[way]))
    parts, codes = pl.pallas_call(
        merge_kernel,
        out_shape=[
            jax.ShapeDtypeStruct(((orb - 1) * part, LANES), jnp.bfloat16),
            jax.ShapeDtypeStruct((orb, 8, LANES), jnp.int32),
        ],
        in_specs=[vmem] * orb,
        out_specs=[vmem, vmem],
        compiler_params=params,
        name="merge",
    )(*notes)
    codes = codes[:, 0, :slots].reshape(orb * slots)
    swapped = lax.ppermute(parts, "aux", [(i, i ^ 1) for i in range(aux)])
    half = pl.pallas_call(
        functools.partial(half_kernel, orb, slots, aux_width),
        out_shape=jax.ShapeDtypeStruct((orb + 1, BS, aux_width * BS), jnp.bfloat16),
        in_specs=[smem] + [vmem] * (orb + 2),
        out_specs=vmem,
        scratch_shapes=[pltpu.VMEM((orb + 1, BS, full_width), jnp.bfloat16)],
        compiler_params=params,
        name="half",
    )(codes, density, own, *notes[1:], swapped)
    parts = pl.pallas_call(
        functools.partial(exchange_kernel, orb, slots, aux_width),
        out_shape=jax.ShapeDtypeStruct((BS, full_width), jnp.float32),
        in_specs=[smem] + [vmem] * (orb + 1),
        out_specs=vmem,
        scratch_shapes=[pltpu.VMEM((orb, BS, BS), jnp.float32)],
        compiler_params=params,
        name="exchange",
    )(codes, half, *packs)

    step = 1
    while step < aux:
        ways = 2 if step == 1 or step * 4 > aux else 4
        terms = [parts]
        for way in range(1, ways):
            terms.append(lax.ppermute(parts, "aux", [(i, i ^ (way * step)) for i in range(aux)]))
        while len(terms) > 1:
            terms = [terms[i] + terms[i + 1] for i in range(0, len(terms), 2)]
        parts = terms[0]
        step *= ways
    return parts


def solution(mesh):
    return jax.shard_map(
        shards,
        mesh=mesh,
        in_specs=(
            P("orb", None),
            P("orb", "aux", None, None, None),
            P("orb", "aux", None),
            P("orb", "aux"),
        ),
        out_specs=P("orb", None),
        check_vma=False,
    )
```

```python
import functools

import jax
import jax.numpy as jnp
from jax import lax
from jax.experimental import pallas as pl
from jax.experimental.pallas import tpu as pltpu
from jax.sharding import PartitionSpec as P

BS = 64
LANES = 128
NOTE = 16


def lay_blocks(raw, out_ref):
    slots, aux_width = raw.shape[:2]
    square = raw.reshape(slots * aux_width, BS, BS)
    for tile in range(slots * aux_width // 2):
        both = jnp.concatenate([square[2 * tile], square[2 * tile + 1]], axis=1)
        out_ref[tile * BS : (tile + 1) * BS] = both
    return slots * aux_width // 2


def core_parity():
    return lax.rem(lax.axis_index("aux"), 2)


def pack_kernel(
    orb, kept, pairs_hbm, density_hbm, raw_hbm, full_ref, tail_ref, pairs, rows, raw, sems
):
    copies = [
        pltpu.make_async_copy(src, dst, sems.at[i])
        for i, (src, dst) in enumerate(((raw_hbm, raw), (density_hbm, rows), (pairs_hbm, pairs)))
    ]
    for copy in copies:
        copy.start()
    for copy in copies:
        copy.wait()
    size = lay_blocks(raw[0, 0], full_ref) * BS
    height = BS // 2
    near = pl.multiple_of(core_parity() * height, height)
    tiles = rows.shape[1] // LANES
    for t in range(tiles):
        lanes = slice(t * LANES, (t + 1) * LANES)
        full_ref[size + t * BS : size + (t + 1) * BS] = rows[:, lanes]
        tail_ref[t * height : (t + 1) * height] = rows[pl.ds(near, height), lanes]
    shape = (NOTE, LANES)
    lane = lax.broadcasted_iota(jnp.int32, shape, 1)
    note = jnp.zeros(shape, jnp.int32)
    for j in range(pairs.shape[2]):
        note = jnp.where(lane == j, jnp.where(j < kept[0, 0], pairs[0, 0, j], orb), note)
    note = note.astype(jnp.float32).astype(jnp.bfloat16)
    full_ref[size + tiles * BS :] = note
    tail_ref[tiles * height :] = note


def lean_kernel(full_ref, out_ref):
    size = out_ref.shape[0] - NOTE
    out_ref[:size] = full_ref[:size]
    out_ref[size:] = full_ref[full_ref.shape[0] - NOTE :]


def relay_kernel(raw, out_ref):
    lay_blocks(raw[0, 0], out_ref)


def merge_kernel(size, *refs):
    parts, out_ref = refs[:-1], refs[-1]
    at = 0
    for i, part in enumerate(parts):
        first = size if i < len(parts) - 1 else 0
        count = part.shape[0] - NOTE - first
        out_ref[at : at + count] = part[first : first + count]
        at += count


def half_kernel(orb, slots, aux_width, meta_ref, density_ref, own_ref, *refs):
    fulls, (tail, swapped, half_ref, rows) = refs[:-4], refs[-4:]
    me = lax.axis_index("orb")
    parity = core_parity()
    height = BS // 2
    count = density_ref.shape[1] // LANES
    size = slots * aux_width * BS // LANES * BS
    near = pl.multiple_of(parity * height, height)
    far = pl.multiple_of((1 - parity) * height, height)
    rows[me] = density_ref[...]
    for i, full in enumerate(fulls):
        ahead = lax.rem(me + (1 - 2 * parity) * (i + 1) + orb, orb)
        behind = lax.rem(me - (1 - 2 * parity) * (i + 1) + orb, orb)
        for t in range(count):
            lanes = slice(t * LANES, (t + 1) * LANES)
            at = (i * count + t) * BS
            rows[ahead, :, lanes] = full[size + t * BS : size + (t + 1) * BS]
            rows[behind, :, lanes] = swapped[at : at + BS]
    across = lax.rem(me + orb // 2, orb)
    for t in range(count):
        lanes = slice(t * LANES, (t + 1) * LANES)
        at = len(fulls) * count * BS + t * height
        rows[across, pl.ds(near, height), lanes] = tail[t * height : (t + 1) * height]
        rows[across, pl.ds(far, height), lanes] = swapped[at : at + height]
    rows[orb] = jnp.zeros_like(rows[orb])
    selected = jnp.concatenate([rows[meta_ref[j]] for j in range(slots)], axis=0)
    own = jnp.concatenate([own_ref[at : at + BS] for at in range(0, size, BS)], axis=1)
    left = []
    for p in range(aux_width):
        cuts = [(j * aux_width + p) * BS for j in range(slots)]
        left.append(jnp.concatenate([own[:, cut : cut + BS] for cut in cuts], axis=1))
    left = jnp.concatenate(left, axis=0)
    half = jnp.dot(left, selected, preferred_element_type=jnp.float32).astype(jnp.bfloat16)
    for k in range(orb):
        half_ref[k] = jnp.concatenate(
            [half[p * BS : (p + 1) * BS, k * BS : (k + 1) * BS] for p in range(aux_width)],
            axis=1,
        )
    half_ref[orb] = jnp.zeros_like(half_ref[orb])


def exchange_kernel(orb, slots, aux_width, meta_ref, half_ref, *refs):
    packs, (out_ref, held) = refs[:orb], refs[orb:]
    me = lax.axis_index("orb")
    parity = core_parity()
    per_slot = aux_width * BS // LANES
    steps = [0, orb // 2]
    for i in range(1, orb // 2):
        steps += [(1 - 2 * parity) * i, (2 * parity - 1) * i]
    for way in range(orb):
        total = None
        for j in range(slots):
            tiles = [
                packs[way][t * BS : (t + 1) * BS] for t in range(j * per_slot, (j + 1) * per_slot)
            ]
            term = lax.dot_general(
                half_ref[meta_ref[way * slots + j]],
                jnp.concatenate(tiles, axis=1),
                (((1,), (1,)), ((), ())),
                preferred_element_type=jnp.float32,
            )
            total = term if total is None else total + term
        held[lax.rem(me + steps[way] + orb, orb)] = total
    out_ref[...] = jnp.concatenate([held[n] for n in range(orb)], axis=1)


def shards(density, tensor_blocks, pairs, kept):
    full_width = density.shape[1]
    slots = tensor_blocks.shape[2]
    aux_width = tensor_blocks.shape[3]
    orb = lax.axis_size("orb")
    aux = lax.axis_size("aux")
    rows = full_width // LANES * BS
    size = slots * aux_width * BS // LANES * BS
    vmem = pl.BlockSpec(memory_space=pltpu.VMEM)
    smem = pl.BlockSpec(memory_space=pltpu.SMEM)
    hbm = pl.BlockSpec(memory_space=pltpu.HBM)
    params = pltpu.CompilerParams(vmem_limit_bytes=32 * 1024 * 1024)

    def array(height):
        return jax.ShapeDtypeStruct((height, LANES), jnp.bfloat16)

    def shift(x, even, odd):
        steps = (even, odd)
        perm = [
            (a * orb + o, a * orb + (o + steps[a % 2]) % orb)
            for a in range(aux)
            for o in range(orb)
        ]
        return lax.ppermute(x, ("aux", "orb"), perm)

    full, tail = pl.pallas_call(
        functools.partial(pack_kernel, orb),
        out_shape=[array(size + rows + NOTE), array(rows // 2 + NOTE)],
        in_specs=[smem, hbm, hbm, hbm],
        out_specs=[vmem] * 2,
        scratch_shapes=[
            pltpu.SMEM(pairs.shape, jnp.int32),
            pltpu.VMEM(density.shape, jnp.bfloat16),
            pltpu.VMEM(tensor_blocks.shape, jnp.bfloat16),
            pltpu.SemaphoreType.DMA((3,)),
        ],
        compiler_params=params,
        name="pack",
    )(
        kept,
        *(pltpu.with_memory_space_constraint(a, pltpu.HBM) for a in (pairs, density, tensor_blocks)),
    )
    lean = pl.pallas_call(
        lean_kernel,
        out_shape=array(size + NOTE),
        in_specs=[vmem],
        out_specs=vmem,
        compiler_params=params,
        name="lean",
    )(full)
    raw = shift(tensor_blocks, orb // 2, orb // 2)
    tail_in = shift(tail, orb // 2, orb // 2)
    fulls = [shift(full, -i, i) for i in range(1, orb // 2)]
    leans = [shift(lean, i, -i) for i in range(1, orb // 2)]

    tail_in, raw = lax.optimization_barrier((tail_in, raw))
    merged = pl.pallas_call(
        functools.partial(merge_kernel, size),
        out_shape=array(len(fulls) * rows + rows // 2),
        in_specs=[vmem] * (len(fulls) + 1),
        out_specs=vmem,
        compiler_params=params,
        name="merge",
    )(*fulls, tail_in)
    swapped = lax.ppermute(merged, "aux", [(i, i ^ 1) for i in range(aux)])
    across = pl.pallas_call(
        relay_kernel,
        out_shape=array(size),
        in_specs=[vmem],
        out_specs=vmem,
        compiler_params=params,
        name="relay",
    )(raw)
    half = pl.pallas_call(
        functools.partial(half_kernel, orb, slots, aux_width),
        out_shape=jax.ShapeDtypeStruct((orb + 1, BS, aux_width * BS), jnp.bfloat16),
        in_specs=[smem] + [vmem] * (len(fulls) + 4),
        out_specs=vmem,
        scratch_shapes=[pltpu.VMEM((orb + 1, BS, full_width), jnp.bfloat16)],
        compiler_params=params,
        name="half",
    )(tail[-NOTE, :slots].astype(jnp.int32), density, full, *fulls, tail_in, swapped)
    half, leans = lax.optimization_barrier((half, leans))
    packs, notes = [full, across], [tail, tail_in]
    for pair in zip(fulls, leans):
        packs += pair
        notes += pair
    codes = jnp.concatenate([n[-NOTE, :slots] for n in notes]).astype(jnp.int32)
    parts = pl.pallas_call(
        functools.partial(exchange_kernel, orb, slots, aux_width),
        out_shape=jax.ShapeDtypeStruct((BS, full_width), jnp.float32),
        in_specs=[smem] + [vmem] * (orb + 1),
        out_specs=vmem,
        scratch_shapes=[pltpu.VMEM((orb, BS, BS), jnp.float32)],
        compiler_params=params,
        name="exchange",
    )(codes, half, *packs)

    step = 1
    while step < aux:
        ways = 2 if step == 1 or step * 4 > aux else 4
        terms = [parts]
        for way in range(1, ways):
            terms.append(lax.ppermute(parts, "aux", [(i, i ^ (way * step)) for i in range(aux)]))
        while len(terms) > 1:
            terms = [terms[i] + terms[i + 1] for i in range(0, len(terms), 2)]
        parts = terms[0]
        step *= ways
    return parts


def solution(mesh):
    return jax.shard_map(
        shards,
        mesh=mesh,
        in_specs=(
            P("orb", None),
            P("orb", "aux", None, None, None),
            P("orb", "aux", None),
            P("orb", "aux"),
        ),
        out_specs=P("orb", None),
        check_vma=False,
    )
```

```python
import functools

import jax
import jax.numpy as jnp
from jax import lax
from jax.experimental import pallas as pl
from jax.experimental.pallas import tpu as pltpu
from jax.sharding import PartitionSpec as P

BS = 64
LANES = 128
NOTE = 16


def lay_blocks(raw, out_ref):
    slots, aux_width = raw.shape[:2]
    square = raw.reshape(slots * aux_width, BS, BS)
    for tile in range(slots * aux_width // 2):
        both = jnp.concatenate([square[2 * tile], square[2 * tile + 1]], axis=1)
        out_ref[tile * BS : (tile + 1) * BS] = both
    return slots * aux_width // 2


def partner(i, step, sign, orb):
    if orb == 4:
        return i ^ (2 - sign)
    return (i + sign * step) % orb


def owner_of(me, step, sign, orb):
    if orb == 4:
        return me ^ (2 - sign)
    return lax.rem(me - sign * step + orb, orb)


def core_parity():
    return lax.rem(lax.axis_index("aux"), 2)


def pack_kernel(
    orb, kept, pairs_hbm, density_hbm, raw_hbm, full_ref, tail_ref, pairs, rows, raw, sems
):
    copies = [
        pltpu.make_async_copy(src, dst, sems.at[i])
        for i, (src, dst) in enumerate(((raw_hbm, raw), (density_hbm, rows), (pairs_hbm, pairs)))
    ]
    for copy in copies:
        copy.start()
    for copy in copies:
        copy.wait()
    size = lay_blocks(raw[0, 0], full_ref) * BS
    height = BS // 2
    near = pl.multiple_of(core_parity() * height, height)
    tiles = rows.shape[1] // LANES
    for t in range(tiles):
        lanes = slice(t * LANES, (t + 1) * LANES)
        full_ref[size + t * BS : size + (t + 1) * BS] = rows[:, lanes]
        tail_ref[t * height : (t + 1) * height] = rows[pl.ds(near, height), lanes]
    shape = (NOTE, LANES)
    lane = lax.broadcasted_iota(jnp.int32, shape, 1)
    note = jnp.zeros(shape, jnp.int32)
    for j in range(pairs.shape[2]):
        note = jnp.where(lane == j, jnp.where(j < kept[0, 0], pairs[0, 0, j], orb), note)
    note = note.astype(jnp.float32).astype(jnp.bfloat16)
    full_ref[size + tiles * BS :] = note
    tail_ref[tiles * height :] = note


def lean_kernel(full_ref, out_ref):
    size = out_ref.shape[0] - NOTE
    out_ref[:size] = full_ref[:size]
    out_ref[size:] = full_ref[full_ref.shape[0] - NOTE :]


def relay_kernel(raw, out_ref):
    lay_blocks(raw[0, 0], out_ref)


def merge_kernel(size, *refs):
    parts, out_ref = refs[:-1], refs[-1]
    at = 0
    for i, part in enumerate(parts):
        first = size if i < len(parts) - 1 else 0
        count = part.shape[0] - NOTE - first
        out_ref[at : at + count] = part[first : first + count]
        at += count


def half_kernel(orb, slots, aux_width, meta_ref, density_ref, own_ref, *refs):
    fulls, (tail, swapped, half_ref, rows) = refs[:-4], refs[-4:]
    me = lax.axis_index("orb")
    parity = core_parity()
    height = BS // 2
    count = density_ref.shape[1] // LANES
    size = slots * aux_width * BS // LANES * BS
    near = pl.multiple_of(parity * height, height)
    far = pl.multiple_of((1 - parity) * height, height)
    rows[me] = density_ref[...]
    for i, full in enumerate(fulls):
        sign = 1 - 2 * parity
        ahead = owner_of(me, i + 1, sign, orb)
        behind = owner_of(me, i + 1, -sign, orb)
        for t in range(count):
            lanes = slice(t * LANES, (t + 1) * LANES)
            at = (i * count + t) * BS
            rows[ahead, :, lanes] = full[size + t * BS : size + (t + 1) * BS]
            rows[behind, :, lanes] = swapped[at : at + BS]
    across = lax.rem(me + orb // 2, orb)
    for t in range(count):
        lanes = slice(t * LANES, (t + 1) * LANES)
        at = len(fulls) * count * BS + t * height
        rows[across, pl.ds(near, height), lanes] = tail[t * height : (t + 1) * height]
        rows[across, pl.ds(far, height), lanes] = swapped[at : at + height]
    rows[orb] = jnp.zeros_like(rows[orb])
    selected = jnp.concatenate([rows[meta_ref[j]] for j in range(slots)], axis=0)
    own = jnp.concatenate([own_ref[at : at + BS] for at in range(0, size, BS)], axis=1)
    left = []
    for p in range(aux_width):
        cuts = [(j * aux_width + p) * BS for j in range(slots)]
        left.append(jnp.concatenate([own[:, cut : cut + BS] for cut in cuts], axis=1))
    left = jnp.concatenate(left, axis=0)
    half = jnp.dot(left, selected, preferred_element_type=jnp.float32).astype(jnp.bfloat16)
    for k in range(orb):
        half_ref[k] = jnp.concatenate(
            [half[p * BS : (p + 1) * BS, k * BS : (k + 1) * BS] for p in range(aux_width)],
            axis=1,
        )
    half_ref[orb] = jnp.zeros_like(half_ref[orb])


def exchange_kernel(orb, slots, aux_width, meta_ref, half_ref, *refs):
    packs, (out_ref, held) = refs[:orb], refs[orb:]
    me = lax.axis_index("orb")
    parity = core_parity()
    per_slot = aux_width * BS // LANES
    sign = 1 - 2 * parity
    owners = [me, lax.rem(me + orb // 2, orb)]
    for i in range(1, orb // 2):
        owners += [owner_of(me, i, sign, orb), owner_of(me, i, -sign, orb)]
    for way in range(orb):
        total = None
        for j in range(slots):
            tiles = [
                packs[way][t * BS : (t + 1) * BS] for t in range(j * per_slot, (j + 1) * per_slot)
            ]
            term = lax.dot_general(
                half_ref[meta_ref[way * slots + j]],
                jnp.concatenate(tiles, axis=1),
                (((1,), (1,)), ((), ())),
                preferred_element_type=jnp.float32,
            )
            total = term if total is None else total + term
        held[owners[way]] = total
    out_ref[...] = jnp.concatenate([held[n] for n in range(orb)], axis=1)


def shards(density, tensor_blocks, pairs, kept):
    full_width = density.shape[1]
    slots = tensor_blocks.shape[2]
    aux_width = tensor_blocks.shape[3]
    orb = lax.axis_size("orb")
    aux = lax.axis_size("aux")
    rows = full_width // LANES * BS
    size = slots * aux_width * BS // LANES * BS
    vmem = pl.BlockSpec(memory_space=pltpu.VMEM)
    smem = pl.BlockSpec(memory_space=pltpu.SMEM)
    hbm = pl.BlockSpec(memory_space=pltpu.HBM)
    params = pltpu.CompilerParams(vmem_limit_bytes=32 * 1024 * 1024)

    def array(height):
        return jax.ShapeDtypeStruct((height, LANES), jnp.bfloat16)

    def shift(x, step, sign):
        perm = [
            (a * orb + o, a * orb + partner(o, step, sign * (1 - 2 * (a % 2)), orb))
            for a in range(aux)
            for o in range(orb)
        ]
        return lax.ppermute(x, ("aux", "orb"), perm)

    full, tail = pl.pallas_call(
        functools.partial(pack_kernel, orb),
        out_shape=[array(size + rows + NOTE), array(rows // 2 + NOTE)],
        in_specs=[smem, hbm, hbm, hbm],
        out_specs=[vmem] * 2,
        scratch_shapes=[
            pltpu.SMEM(pairs.shape, jnp.int32),
            pltpu.VMEM(density.shape, jnp.bfloat16),
            pltpu.VMEM(tensor_blocks.shape, jnp.bfloat16),
            pltpu.SemaphoreType.DMA((3,)),
        ],
        compiler_params=params,
        name="pack",
    )(
        kept,
        *(pltpu.with_memory_space_constraint(a, pltpu.HBM) for a in (pairs, density, tensor_blocks)),
    )
    lean = pl.pallas_call(
        lean_kernel,
        out_shape=array(size + NOTE),
        in_specs=[vmem],
        out_specs=vmem,
        compiler_params=params,
        name="lean",
    )(full)
    across = [(i, (i + orb // 2) % orb) for i in range(orb)]
    raw = lax.ppermute(tensor_blocks, "orb", across)
    tail_in = lax.ppermute(tail, "orb", across)
    fulls = [shift(full, i, 1) for i in range(1, orb // 2)]
    leans = [shift(lean, i, -1) for i in range(1, orb // 2)]

    tail_in, raw = lax.optimization_barrier((tail_in, raw))
    merged = pl.pallas_call(
        functools.partial(merge_kernel, size),
        out_shape=array(len(fulls) * rows + rows // 2),
        in_specs=[vmem] * (len(fulls) + 1),
        out_specs=vmem,
        compiler_params=params,
        name="merge",
    )(*fulls, tail_in)
    swapped = lax.ppermute(merged, "aux", [(i, i ^ 1) for i in range(aux)])
    across = pl.pallas_call(
        relay_kernel,
        out_shape=array(size),
        in_specs=[vmem],
        out_specs=vmem,
        compiler_params=params,
        name="relay",
    )(raw)
    half = pl.pallas_call(
        functools.partial(half_kernel, orb, slots, aux_width),
        out_shape=jax.ShapeDtypeStruct((orb + 1, BS, aux_width * BS), jnp.bfloat16),
        in_specs=[smem] + [vmem] * (len(fulls) + 4),
        out_specs=vmem,
        scratch_shapes=[pltpu.VMEM((orb + 1, BS, full_width), jnp.bfloat16)],
        compiler_params=params,
        name="half",
    )(tail[-NOTE, :slots].astype(jnp.int32), density, full, *fulls, tail_in, swapped)
    half, leans = lax.optimization_barrier((half, leans))
    packs, notes = [full, across], [tail, tail_in]
    for pair in zip(fulls, leans):
        packs += pair
        notes += pair
    codes = jnp.concatenate([n[-NOTE, :slots] for n in notes]).astype(jnp.int32)
    parts = pl.pallas_call(
        functools.partial(exchange_kernel, orb, slots, aux_width),
        out_shape=jax.ShapeDtypeStruct((BS, full_width), jnp.float32),
        in_specs=[smem] + [vmem] * (orb + 1),
        out_specs=vmem,
        scratch_shapes=[pltpu.VMEM((orb, BS, BS), jnp.float32)],
        compiler_params=params,
        name="exchange",
    )(codes, half, *packs)

    step = 1
    while step < aux:
        ways = 2 if step == 1 or step * 4 > aux else 4
        terms = [parts]
        for way in range(1, ways):
            terms.append(lax.ppermute(parts, "aux", [(i, i ^ (way * step)) for i in range(aux)]))
        while len(terms) > 1:
            terms = [terms[i] + terms[i + 1] for i in range(0, len(terms), 2)]
        parts = terms[0]
        step *= ways
    return parts


def solution(mesh):
    return jax.shard_map(
        shards,
        mesh=mesh,
        in_specs=(
            P("orb", None),
            P("orb", "aux", None, None, None),
            P("orb", "aux", None),
            P("orb", "aux"),
        ),
        out_specs=P("orb", None),
        check_vma=False,
    )
```

```python
import functools

import jax
import jax.numpy as jnp
from jax import lax
from jax.experimental import pallas as pl
from jax.experimental.pallas import tpu as pltpu
from jax.sharding import PartitionSpec as P

BS = 64
LANES = 128
NOTE = 16


def lay_blocks(raw, out_ref):
    slots, aux_width = raw.shape[:2]
    square = raw.reshape(slots * aux_width, BS, BS)
    for tile in range(slots * aux_width // 2):
        both = jnp.concatenate([square[2 * tile], square[2 * tile + 1]], axis=1)
        out_ref[tile * BS : (tile + 1) * BS] = both
    return slots * aux_width // 2


def partner(i, step, sign, orb):
    if orb == 4:
        return i ^ (2 - sign)
    return (i + sign * step) % orb


def owner_of(me, step, sign, orb):
    if orb == 4:
        return me ^ (2 - sign)
    return lax.rem(me - sign * step + orb, orb)


def core_parity():
    return lax.rem(lax.axis_index("aux"), 2)


def pack_kernel(
    orb, kept, pairs_hbm, density_hbm, raw_hbm, own_ref, near_ref, tail_ref, pairs, rows, raw, sems
):
    copies = [
        pltpu.make_async_copy(src, dst, sems.at[i])
        for i, (src, dst) in enumerate(((raw_hbm, raw), (density_hbm, rows), (pairs_hbm, pairs)))
    ]
    for copy in copies:
        copy.start()
    for copy in copies:
        copy.wait()
    lay_blocks(raw[0, 0], own_ref)
    height = BS // 2
    near = pl.multiple_of(core_parity() * height, height)
    tiles = rows.shape[1] // LANES
    for t in range(tiles):
        lanes = slice(t * LANES, (t + 1) * LANES)
        near_ref[t * BS : (t + 1) * BS] = rows[:, lanes]
        tail_ref[t * height : (t + 1) * height] = rows[pl.ds(near, height), lanes]
    shape = (NOTE, LANES)
    lane = lax.broadcasted_iota(jnp.int32, shape, 1)
    note = jnp.zeros(shape, jnp.int32)
    for j in range(pairs.shape[2]):
        note = jnp.where(lane == j, jnp.where(j < kept[0, 0], pairs[0, 0, j], orb), note)
    note = note.astype(jnp.float32).astype(jnp.bfloat16)
    near_ref[tiles * BS :] = note
    tail_ref[tiles * height :] = note


def lean_kernel(own_ref, near_ref, mark_ref, out_ref):
    size = own_ref.shape[0]
    out_ref[:size] = own_ref[...]
    out_ref[size:] = near_ref[near_ref.shape[0] - NOTE :]


def relay_kernel(raw, out_ref):
    lay_blocks(raw[0, 0], out_ref)


def merge_kernel(*refs):
    parts, out_ref = refs[:-1], refs[-1]
    at = 0
    for part in parts:
        count = part.shape[0] - NOTE
        out_ref[at : at + count] = part[:count]
        at += count


def half_kernel(orb, slots, aux_width, meta_ref, density_ref, own_ref, *refs):
    nears, (tail, swapped, half_ref, rows) = refs[:-4], refs[-4:]
    me = lax.axis_index("orb")
    parity = core_parity()
    height = BS // 2
    count = density_ref.shape[1] // LANES
    size = slots * aux_width * BS // LANES * BS
    mine = pl.multiple_of(parity * height, height)
    other = pl.multiple_of((1 - parity) * height, height)
    rows[me] = density_ref[...]
    for i, near in enumerate(nears):
        sign = 1 - 2 * parity
        ahead = owner_of(me, i + 1, sign, orb)
        behind = owner_of(me, i + 1, -sign, orb)
        for t in range(count):
            lanes = slice(t * LANES, (t + 1) * LANES)
            at = (i * count + t) * BS
            rows[ahead, :, lanes] = near[t * BS : (t + 1) * BS]
            rows[behind, :, lanes] = swapped[at : at + BS]
    across = lax.rem(me + orb // 2, orb)
    for t in range(count):
        lanes = slice(t * LANES, (t + 1) * LANES)
        at = len(nears) * count * BS + t * height
        rows[across, pl.ds(mine, height), lanes] = tail[t * height : (t + 1) * height]
        rows[across, pl.ds(other, height), lanes] = swapped[at : at + height]
    rows[orb] = jnp.zeros_like(rows[orb])
    selected = jnp.concatenate([rows[meta_ref[j]] for j in range(slots)], axis=0)
    own = jnp.concatenate([own_ref[at : at + BS] for at in range(0, size, BS)], axis=1)
    left = []
    for p in range(aux_width):
        cuts = [(j * aux_width + p) * BS for j in range(slots)]
        left.append(jnp.concatenate([own[:, cut : cut + BS] for cut in cuts], axis=1))
    left = jnp.concatenate(left, axis=0)
    half = jnp.dot(left, selected, preferred_element_type=jnp.float32).astype(jnp.bfloat16)
    for k in range(orb):
        half_ref[k] = jnp.concatenate(
            [half[p * BS : (p + 1) * BS, k * BS : (k + 1) * BS] for p in range(aux_width)],
            axis=1,
        )
    half_ref[orb] = jnp.zeros_like(half_ref[orb])


def exchange_kernel(orb, slots, aux_width, meta_ref, half_ref, *refs):
    packs, (out_ref, held) = refs[:orb], refs[orb:]
    me = lax.axis_index("orb")
    per_slot = aux_width * BS // LANES
    owners = [me, lax.rem(me + orb // 2, orb)]
    for i in range(1, orb // 2):
        owners += [owner_of(me, i, sign, orb) for sign in (1, -1)]
    for way in range(orb):
        total = None
        for j in range(slots):
            tiles = [
                packs[way][t * BS : (t + 1) * BS] for t in range(j * per_slot, (j + 1) * per_slot)
            ]
            term = lax.dot_general(
                half_ref[meta_ref[way * slots + j]],
                jnp.concatenate(tiles, axis=1),
                (((1,), (1,)), ((), ())),
                preferred_element_type=jnp.float32,
            )
            total = term if total is None else total + term
        held[owners[way]] = total
    out_ref[...] = jnp.concatenate([held[n] for n in range(orb)], axis=1)


def shards(density, tensor_blocks, pairs, kept):
    full_width = density.shape[1]
    slots = tensor_blocks.shape[2]
    aux_width = tensor_blocks.shape[3]
    orb = lax.axis_size("orb")
    aux = lax.axis_size("aux")
    rows = full_width // LANES * BS
    size = slots * aux_width * BS // LANES * BS
    vmem = pl.BlockSpec(memory_space=pltpu.VMEM)
    smem = pl.BlockSpec(memory_space=pltpu.SMEM)
    hbm = pl.BlockSpec(memory_space=pltpu.HBM)
    params = pltpu.CompilerParams(vmem_limit_bytes=32 * 1024 * 1024)

    def array(height):
        return jax.ShapeDtypeStruct((height, LANES), jnp.bfloat16)

    own, near, tail = pl.pallas_call(
        functools.partial(pack_kernel, orb),
        out_shape=[array(size), array(rows + NOTE), array(rows // 2 + NOTE)],
        in_specs=[smem, hbm, hbm, hbm],
        out_specs=[vmem] * 3,
        scratch_shapes=[
            pltpu.SMEM(pairs.shape, jnp.int32),
            pltpu.VMEM(density.shape, jnp.bfloat16),
            pltpu.VMEM(tensor_blocks.shape, jnp.bfloat16),
            pltpu.SemaphoreType.DMA((3,)),
        ],
        compiler_params=params,
        name="pack",
    )(
        kept,
        *(pltpu.with_memory_space_constraint(a, pltpu.HBM) for a in (pairs, density, tensor_blocks)),
    )
    mark = lax.ppermute(tail, "aux", [(i, i ^ 1) for i in range(aux)])
    lean = pl.pallas_call(
        lean_kernel,
        out_shape=array(size + NOTE),
        in_specs=[vmem] * 3,
        out_specs=vmem,
        compiler_params=params,
        name="lean",
    )(own, near, mark)
    across = [(i, (i + orb // 2) % orb) for i in range(orb)]
    raw = lax.ppermute(tensor_blocks, "orb", across)
    tail_in = lax.ppermute(tail, "orb", across)
    nears, leans = [], []
    for i in range(1, orb // 2):
        perm = [
            (a * orb + o, a * orb + partner(o, i, 1 - 2 * (a % 2), orb))
            for a in range(aux)
            for o in range(orb)
        ]
        nears.append(lax.ppermute(near, ("aux", "orb"), perm))
        for sign in (1, -1):
            perm = [(o, partner(o, i, sign, orb)) for o in range(orb)]
            leans.append(lax.ppermute(lean, "orb", perm))

    tail_in, raw = lax.optimization_barrier((tail_in, raw))
    merged = pl.pallas_call(
        merge_kernel,
        out_shape=array(len(nears) * rows + rows // 2),
        in_specs=[vmem] * (len(nears) + 1),
        out_specs=vmem,
        compiler_params=params,
        name="merge",
    )(*nears, tail_in)
    swapped = lax.ppermute(merged, "aux", [(i, i ^ 1) for i in range(aux)])
    across = pl.pallas_call(
        relay_kernel,
        out_shape=array(size),
        in_specs=[vmem],
        out_specs=vmem,
        compiler_params=params,
        name="relay",
    )(raw)
    half = pl.pallas_call(
        functools.partial(half_kernel, orb, slots, aux_width),
        out_shape=jax.ShapeDtypeStruct((orb + 1, BS, aux_width * BS), jnp.bfloat16),
        in_specs=[smem] + [vmem] * (len(nears) + 4),
        out_specs=vmem,
        scratch_shapes=[pltpu.VMEM((orb + 1, BS, full_width), jnp.bfloat16)],
        compiler_params=params,
        name="half",
    )(tail[-NOTE, :slots].astype(jnp.int32), density, own, *nears, tail_in, swapped)
    half, leans = lax.optimization_barrier((half, leans))
    packs, notes = [own, across, *leans], [tail, tail_in, *leans]
    codes = jnp.concatenate([n[-NOTE, :slots] for n in notes]).astype(jnp.int32)
    parts = pl.pallas_call(
        functools.partial(exchange_kernel, orb, slots, aux_width),
        out_shape=jax.ShapeDtypeStruct((BS, full_width), jnp.float32),
        in_specs=[smem] + [vmem] * (orb + 1),
        out_specs=vmem,
        scratch_shapes=[pltpu.VMEM((orb, BS, BS), jnp.float32)],
        compiler_params=params,
        name="exchange",
    )(codes, half, *packs)

    step = 1
    while step < aux:
        ways = 2 if step == 1 or step * 4 > aux else 4
        terms = [parts]
        for way in range(1, ways):
            terms.append(lax.ppermute(parts, "aux", [(i, i ^ (way * step)) for i in range(aux)]))
        while len(terms) > 1:
            terms = [terms[i] + terms[i + 1] for i in range(0, len(terms), 2)]
        parts = terms[0]
        step *= ways
    return parts


def solution(mesh):
    return jax.shard_map(
        shards,
        mesh=mesh,
        in_specs=(
            P("orb", None),
            P("orb", "aux", None, None, None),
            P("orb", "aux", None),
            P("orb", "aux"),
        ),
        out_specs=P("orb", None),
        check_vma=False,
    )
```

```python
import functools

import jax
import jax.numpy as jnp
from jax import lax
from jax.experimental import pallas as pl
from jax.experimental.pallas import tpu as pltpu
from jax.sharding import PartitionSpec as P

BS = 64
LANES = 128
NOTE = 16


def lay_blocks(raw, out_ref):
    slots, aux_width = raw.shape[:2]
    square = raw.reshape(slots * aux_width, BS, BS)
    for tile in range(slots * aux_width // 2):
        both = jnp.concatenate([square[2 * tile], square[2 * tile + 1]], axis=1)
        out_ref[tile * BS : (tile + 1) * BS] = both
    return slots * aux_width // 2


def partner(i, step, sign, orb):
    if orb == 4:
        return i ^ (2 - sign)
    return (i + sign * step) % orb


def owner_of(me, step, sign, orb):
    if orb == 4:
        return me ^ (2 - sign)
    return lax.rem(me - sign * step + orb, orb)


def core_parity():
    return lax.rem(lax.axis_index("aux"), 2)


def pack_kernel(
    orb, kept, pairs_hbm, density_hbm, raw_hbm, own_ref, near_ref, tail_ref, pairs, rows, raw, sems
):
    copies = [
        pltpu.make_async_copy(src, dst, sems.at[i])
        for i, (src, dst) in enumerate(((raw_hbm, raw), (density_hbm, rows), (pairs_hbm, pairs)))
    ]
    for copy in copies:
        copy.start()
    for copy in copies:
        copy.wait()
    lay_blocks(raw[0, 0], own_ref)
    height = BS // 2
    near = pl.multiple_of(core_parity() * height, height)
    tiles = rows.shape[1] // LANES
    for t in range(tiles):
        lanes = slice(t * LANES, (t + 1) * LANES)
        near_ref[t * BS : (t + 1) * BS] = rows[:, lanes]
        tail_ref[t * height : (t + 1) * height] = rows[pl.ds(near, height), lanes]
    shape = (NOTE, LANES)
    lane = lax.broadcasted_iota(jnp.int32, shape, 1)
    note = jnp.zeros(shape, jnp.int32)
    for j in range(pairs.shape[2]):
        note = jnp.where(lane == j, jnp.where(j < kept[0, 0], pairs[0, 0, j], orb), note)
    note = note.astype(jnp.float32).astype(jnp.bfloat16)
    near_ref[tiles * BS :] = note
    tail_ref[tiles * height :] = note


def lean_kernel(own_ref, near_ref, mark_ref, out_ref):
    size = own_ref.shape[0]
    out_ref[:size] = own_ref[...]
    out_ref[size:] = near_ref[near_ref.shape[0] - NOTE :]


def relay_kernel(raw, out_ref):
    lay_blocks(raw[0, 0], out_ref)


def merge_kernel(*refs):
    parts, out_ref = refs[:-1], refs[-1]
    at = 0
    for part in parts:
        count = part.shape[0] - NOTE
        out_ref[at : at + count] = part[:count]
        at += count


def half_kernel(orb, slots, aux_width, meta_ref, density_ref, own_ref, *refs):
    nears, (tail, swapped, half_ref, rows) = refs[:-4], refs[-4:]
    me = lax.axis_index("orb")
    parity = core_parity()
    height = BS // 2
    count = density_ref.shape[1] // LANES
    size = slots * aux_width * BS // LANES * BS
    mine = pl.multiple_of(parity * height, height)
    other = pl.multiple_of((1 - parity) * height, height)
    rows[me] = density_ref[...]
    for i, near in enumerate(nears):
        sign = 1 - 2 * parity
        ahead = owner_of(me, i + 1, sign, orb)
        behind = owner_of(me, i + 1, -sign, orb)
        for t in range(count):
            lanes = slice(t * LANES, (t + 1) * LANES)
            at = (i * count + t) * BS
            rows[ahead, :, lanes] = near[t * BS : (t + 1) * BS]
            rows[behind, :, lanes] = swapped[at : at + BS]
    across = lax.rem(me + orb // 2, orb)
    for t in range(count):
        lanes = slice(t * LANES, (t + 1) * LANES)
        at = len(nears) * count * BS + t * height
        rows[across, pl.ds(mine, height), lanes] = tail[t * height : (t + 1) * height]
        rows[across, pl.ds(other, height), lanes] = swapped[at : at + height]
    rows[orb] = jnp.zeros_like(rows[orb])
    selected = jnp.concatenate([rows[meta_ref[j]] for j in range(slots)], axis=0)
    own = jnp.concatenate([own_ref[at : at + BS] for at in range(0, size, BS)], axis=1)
    left = []
    for p in range(aux_width):
        cuts = [(j * aux_width + p) * BS for j in range(slots)]
        left.append(jnp.concatenate([own[:, cut : cut + BS] for cut in cuts], axis=1))
    left = jnp.concatenate(left, axis=0)
    half = jnp.dot(left, selected, preferred_element_type=jnp.float32).astype(jnp.bfloat16)
    for k in range(orb):
        half_ref[k] = jnp.concatenate(
            [half[p * BS : (p + 1) * BS, k * BS : (k + 1) * BS] for p in range(aux_width)],
            axis=1,
        )
    half_ref[orb] = jnp.zeros_like(half_ref[orb])


def exchange_kernel(orb, slots, aux_width, meta_ref, half_ref, *refs):
    packs, (out_ref, held) = refs[:orb], refs[orb:]
    me = lax.axis_index("orb")
    parity = core_parity()
    per_slot = aux_width * BS // LANES
    owners = [me, lax.rem(me + orb // 2, orb)]
    for i in range(1, orb // 2):
        owners += [owner_of(me, i, sign * (1 - 2 * parity), orb) for sign in (-1, 1)]
    for way in range(orb):
        total = None
        for j in range(slots):
            tiles = [
                packs[way][t * BS : (t + 1) * BS] for t in range(j * per_slot, (j + 1) * per_slot)
            ]
            term = lax.dot_general(
                half_ref[meta_ref[way * slots + j]],
                jnp.concatenate(tiles, axis=1),
                (((1,), (1,)), ((), ())),
                preferred_element_type=jnp.float32,
            )
            total = term if total is None else total + term
        held[owners[way]] = total
    out_ref[...] = jnp.concatenate([held[n] for n in range(orb)], axis=1)


def shards(density, tensor_blocks, pairs, kept):
    full_width = density.shape[1]
    slots = tensor_blocks.shape[2]
    aux_width = tensor_blocks.shape[3]
    orb = lax.axis_size("orb")
    aux = lax.axis_size("aux")
    rows = full_width // LANES * BS
    size = slots * aux_width * BS // LANES * BS
    vmem = pl.BlockSpec(memory_space=pltpu.VMEM)
    smem = pl.BlockSpec(memory_space=pltpu.SMEM)
    hbm = pl.BlockSpec(memory_space=pltpu.HBM)
    params = pltpu.CompilerParams(vmem_limit_bytes=32 * 1024 * 1024)

    def array(height):
        return jax.ShapeDtypeStruct((height, LANES), jnp.bfloat16)

    own, near, tail = pl.pallas_call(
        functools.partial(pack_kernel, orb),
        out_shape=[array(size), array(rows + NOTE), array(rows // 2 + NOTE)],
        in_specs=[smem, hbm, hbm, hbm],
        out_specs=[vmem] * 3,
        scratch_shapes=[
            pltpu.SMEM(pairs.shape, jnp.int32),
            pltpu.VMEM(density.shape, jnp.bfloat16),
            pltpu.VMEM(tensor_blocks.shape, jnp.bfloat16),
            pltpu.SemaphoreType.DMA((3,)),
        ],
        compiler_params=params,
        name="pack",
    )(
        kept,
        *(pltpu.with_memory_space_constraint(a, pltpu.HBM) for a in (pairs, density, tensor_blocks)),
    )
    mark = lax.ppermute(tail, "aux", [(i, i ^ 1) for i in range(aux)])
    lean = pl.pallas_call(
        lean_kernel,
        out_shape=array(size + NOTE),
        in_specs=[vmem] * 3,
        out_specs=vmem,
        compiler_params=params,
        name="lean",
    )(own, near, mark)
    across = [(i, (i + orb // 2) % orb) for i in range(orb)]
    raw = lax.ppermute(tensor_blocks, "orb", across)
    tail_in = lax.ppermute(tail, "orb", across)
    nears, leans = [], []
    for i in range(1, orb // 2):
        perm = [
            (a * orb + o, a * orb + partner(o, i, 1 - 2 * (a % 2), orb))
            for a in range(aux)
            for o in range(orb)
        ]
        nears.append(lax.ppermute(near, ("aux", "orb"), perm))
        for sign in (-1, 1):
            perm = [
                (a * orb + o, a * orb + partner(o, i, sign * (1 - 2 * (a % 2)), orb))
                for a in range(aux)
                for o in range(orb)
            ]
            leans.append(lax.ppermute(lean, ("aux", "orb"), perm))

    tail_in, raw = lax.optimization_barrier((tail_in, raw))
    merged = pl.pallas_call(
        merge_kernel,
        out_shape=array(len(nears) * rows + rows // 2),
        in_specs=[vmem] * (len(nears) + 1),
        out_specs=vmem,
        compiler_params=params,
        name="merge",
    )(*nears, tail_in)
    swapped = lax.ppermute(merged, "aux", [(i, i ^ 1) for i in range(aux)])
    across = pl.pallas_call(
        relay_kernel,
        out_shape=array(size),
        in_specs=[vmem],
        out_specs=vmem,
        compiler_params=params,
        name="relay",
    )(raw)
    half = pl.pallas_call(
        functools.partial(half_kernel, orb, slots, aux_width),
        out_shape=jax.ShapeDtypeStruct((orb + 1, BS, aux_width * BS), jnp.bfloat16),
        in_specs=[smem] + [vmem] * (len(nears) + 4),
        out_specs=vmem,
        scratch_shapes=[pltpu.VMEM((orb + 1, BS, full_width), jnp.bfloat16)],
        compiler_params=params,
        name="half",
    )(tail[-NOTE, :slots].astype(jnp.int32), density, own, *nears, tail_in, swapped)
    half, leans = lax.optimization_barrier((half, leans))
    packs, notes = [own, across, *leans], [tail, tail_in, *leans]
    codes = jnp.concatenate([n[-NOTE, :slots] for n in notes]).astype(jnp.int32)
    parts = pl.pallas_call(
        functools.partial(exchange_kernel, orb, slots, aux_width),
        out_shape=jax.ShapeDtypeStruct((BS, full_width), jnp.float32),
        in_specs=[smem] + [vmem] * (orb + 1),
        out_specs=vmem,
        scratch_shapes=[pltpu.VMEM((orb, BS, BS), jnp.float32)],
        compiler_params=params,
        name="exchange",
    )(codes, half, *packs)

    step = 1
    while step < aux:
        ways = 2 if step == 1 or step * 4 > aux else 4
        terms = [parts]
        for way in range(1, ways):
            terms.append(lax.ppermute(parts, "aux", [(i, i ^ (way * step)) for i in range(aux)]))
        while len(terms) > 1:
            terms = [terms[i] + terms[i + 1] for i in range(0, len(terms), 2)]
        parts = terms[0]
        step *= ways
    return parts


def solution(mesh):
    return jax.shard_map(
        shards,
        mesh=mesh,
        in_specs=(
            P("orb", None),
            P("orb", "aux", None, None, None),
            P("orb", "aux", None),
            P("orb", "aux"),
        ),
        out_specs=P("orb", None),
        check_vma=False,
    )
```

```python
import functools

import jax
import jax.numpy as jnp
from jax import lax
from jax.experimental import pallas as pl
from jax.experimental.pallas import tpu as pltpu
from jax.sharding import PartitionSpec as P

BS = 64
LANES = 128
NOTE = 16


def lay_blocks(raw, out_ref):
    slots, aux_width = raw.shape[:2]
    square = raw.reshape(slots * aux_width, BS, BS)
    for tile in range(slots * aux_width // 2):
        both = jnp.concatenate([square[2 * tile], square[2 * tile + 1]], axis=1)
        out_ref[tile * BS : (tile + 1) * BS] = both
    return slots * aux_width // 2


def partner(i, step, sign, orb):
    if orb == 4:
        return i ^ (2 - sign)
    return (i + sign * step) % orb


def owner_of(me, step, sign, orb):
    if orb == 4:
        return me ^ (2 - sign)
    return lax.rem(me - sign * step + orb, orb)


def core_parity():
    return lax.rem(lax.axis_index("aux"), 2)


def pack_kernel(
    orb, kept, pairs_hbm, density_hbm, raw_hbm, own_ref, near_ref, tail_ref, pairs, rows, raw, sems
):
    copies = [
        pltpu.make_async_copy(src, dst, sems.at[i])
        for i, (src, dst) in enumerate(((raw_hbm, raw), (density_hbm, rows), (pairs_hbm, pairs)))
    ]
    for copy in copies:
        copy.start()
    for copy in copies:
        copy.wait()
    lay_blocks(raw[0, 0], own_ref)
    height = BS // 2
    near = pl.multiple_of(core_parity() * height, height)
    tiles = rows.shape[1] // LANES
    for t in range(tiles):
        lanes = slice(t * LANES, (t + 1) * LANES)
        near_ref[t * BS : (t + 1) * BS] = rows[:, lanes]
        tail_ref[t * height : (t + 1) * height] = rows[pl.ds(near, height), lanes]
    shape = (NOTE, LANES)
    lane = lax.broadcasted_iota(jnp.int32, shape, 1)
    note = jnp.zeros(shape, jnp.int32)
    for j in range(pairs.shape[2]):
        note = jnp.where(lane == j, jnp.where(j < kept[0, 0], pairs[0, 0, j], orb), note)
    note = note.astype(jnp.float32).astype(jnp.bfloat16)
    near_ref[tiles * BS :] = note
    tail_ref[tiles * height :] = note


def lean_kernel(own_ref, near_ref, mark_ref, out_ref):
    size = own_ref.shape[0]
    out_ref[:size] = own_ref[...]
    out_ref[size:] = near_ref[near_ref.shape[0] - NOTE :]


def relay_kernel(raw, out_ref):
    lay_blocks(raw[0, 0], out_ref)


def merge_kernel(*refs):
    parts, out_ref = refs[:-1], refs[-1]
    at = 0
    for part in parts:
        count = part.shape[0] - NOTE
        out_ref[at : at + count] = part[:count]
        at += count


def half_kernel(orb, slots, aux_width, meta_ref, density_ref, own_ref, *refs):
    nears, (tail, swapped, half_ref, rows) = refs[:-4], refs[-4:]
    me = lax.axis_index("orb")
    parity = core_parity()
    height = BS // 2
    count = density_ref.shape[1] // LANES
    size = slots * aux_width * BS // LANES * BS
    mine = pl.multiple_of(parity * height, height)
    other = pl.multiple_of((1 - parity) * height, height)
    rows[me] = density_ref[...]
    for i, near in enumerate(nears):
        sign = 1 - 2 * parity
        ahead = owner_of(me, i + 1, sign, orb)
        behind = owner_of(me, i + 1, -sign, orb)
        for t in range(count):
            lanes = slice(t * LANES, (t + 1) * LANES)
            at = (i * count + t) * BS
            rows[ahead, :, lanes] = near[t * BS : (t + 1) * BS]
            rows[behind, :, lanes] = swapped[at : at + BS]
    across = lax.rem(me + orb // 2, orb)
    for t in range(count):
        lanes = slice(t * LANES, (t + 1) * LANES)
        at = len(nears) * count * BS + t * height
        rows[across, pl.ds(mine, height), lanes] = tail[t * height : (t + 1) * height]
        rows[across, pl.ds(other, height), lanes] = swapped[at : at + height]
    rows[orb] = jnp.zeros_like(rows[orb])
    selected = jnp.concatenate([rows[meta_ref[j]] for j in range(slots)], axis=0)
    own = jnp.concatenate([own_ref[at : at + BS] for at in range(0, size, BS)], axis=1)
    left = []
    for p in range(aux_width):
        cuts = [(j * aux_width + p) * BS for j in range(slots)]
        left.append(jnp.concatenate([own[:, cut : cut + BS] for cut in cuts], axis=1))
    left = jnp.concatenate(left, axis=0)
    half = jnp.dot(left, selected, preferred_element_type=jnp.float32).astype(jnp.bfloat16)
    for k in range(orb):
        half_ref[k] = jnp.concatenate(
            [half[p * BS : (p + 1) * BS, k * BS : (k + 1) * BS] for p in range(aux_width)],
            axis=1,
        )
    half_ref[orb] = jnp.zeros_like(half_ref[orb])


def exchange_kernel(orb, slots, aux_width, meta_ref, half_ref, *refs):
    packs, (out_ref, held) = refs[:orb], refs[orb:]
    me = lax.axis_index("orb")
    parity = core_parity()
    per_slot = aux_width * BS // LANES
    owners = [me, lax.rem(me + orb // 2, orb)]
    for i in range(1, orb // 2):
        owners += [owner_of(me, i, sign * (1 - 2 * parity), orb) for sign in (-1, 1)]
    for way in range(orb):
        total = None
        for j in range(slots):
            tiles = [
                packs[way][t * BS : (t + 1) * BS] for t in range(j * per_slot, (j + 1) * per_slot)
            ]
            term = lax.dot_general(
                half_ref[meta_ref[way * slots + j]],
                jnp.concatenate(tiles, axis=1),
                (((1,), (1,)), ((), ())),
                preferred_element_type=jnp.float32,
            )
            total = term if total is None else total + term
        held[owners[way]] = total
    out_ref[...] = jnp.concatenate([held[n] for n in range(orb)], axis=1)


def shards(density, tensor_blocks, pairs, kept):
    full_width = density.shape[1]
    slots = tensor_blocks.shape[2]
    aux_width = tensor_blocks.shape[3]
    orb = lax.axis_size("orb")
    aux = lax.axis_size("aux")
    rows = full_width // LANES * BS
    size = slots * aux_width * BS // LANES * BS
    vmem = pl.BlockSpec(memory_space=pltpu.VMEM)
    smem = pl.BlockSpec(memory_space=pltpu.SMEM)
    hbm = pl.BlockSpec(memory_space=pltpu.HBM)
    params = pltpu.CompilerParams(vmem_limit_bytes=32 * 1024 * 1024)

    def array(height):
        return jax.ShapeDtypeStruct((height, LANES), jnp.bfloat16)

    own, near, tail = pl.pallas_call(
        functools.partial(pack_kernel, orb),
        out_shape=[array(size), array(rows + NOTE), array(rows // 2 + NOTE)],
        in_specs=[smem, hbm, hbm, hbm],
        out_specs=[vmem] * 3,
        scratch_shapes=[
            pltpu.SMEM(pairs.shape, jnp.int32),
            pltpu.VMEM(density.shape, jnp.bfloat16),
            pltpu.VMEM(tensor_blocks.shape, jnp.bfloat16),
            pltpu.SemaphoreType.DMA((3,)),
        ],
        compiler_params=params,
        name="pack",
    )(
        kept,
        *(pltpu.with_memory_space_constraint(a, pltpu.HBM) for a in (pairs, density, tensor_blocks)),
    )
    mark = lax.ppermute(near, "aux", [(i, i ^ 1) for i in range(aux)])
    lean = pl.pallas_call(
        lean_kernel,
        out_shape=array(size + NOTE),
        in_specs=[vmem] * 3,
        out_specs=vmem,
        compiler_params=params,
        name="lean",
    )(own, near, mark)
    across = [(i, (i + orb // 2) % orb) for i in range(orb)]
    raw = lax.ppermute(tensor_blocks, "orb", across)
    tail_in = lax.ppermute(tail, "orb", across)
    nears, leans = [], []
    for i in range(1, orb // 2):
        perm = [
            (a * orb + o, a * orb + partner(o, i, 1 - 2 * (a % 2), orb))
            for a in range(aux)
            for o in range(orb)
        ]
        nears.append(lax.ppermute(near, ("aux", "orb"), perm))
        for sign in (-1, 1):
            perm = [
                (a * orb + o, a * orb + partner(o, i, sign * (1 - 2 * (a % 2)), orb))
                for a in range(aux)
                for o in range(orb)
            ]
            leans.append(lax.ppermute(lean, ("aux", "orb"), perm))

    tail_in, raw = lax.optimization_barrier((tail_in, raw))
    merged = pl.pallas_call(
        merge_kernel,
        out_shape=array(len(nears) * rows + rows // 2),
        in_specs=[vmem] * (len(nears) + 1),
        out_specs=vmem,
        compiler_params=params,
        name="merge",
    )(*nears, tail_in)
    swapped = lax.ppermute(merged, "aux", [(i, i ^ 1) for i in range(aux)])
    across = pl.pallas_call(
        relay_kernel,
        out_shape=array(size),
        in_specs=[vmem],
        out_specs=vmem,
        compiler_params=params,
        name="relay",
    )(raw)
    half = pl.pallas_call(
        functools.partial(half_kernel, orb, slots, aux_width),
        out_shape=jax.ShapeDtypeStruct((orb + 1, BS, aux_width * BS), jnp.bfloat16),
        in_specs=[smem] + [vmem] * (len(nears) + 4),
        out_specs=vmem,
        scratch_shapes=[pltpu.VMEM((orb + 1, BS, full_width), jnp.bfloat16)],
        compiler_params=params,
        name="half",
    )(tail[-NOTE, :slots].astype(jnp.int32), density, own, *nears, tail_in, swapped)
    half, leans = lax.optimization_barrier((half, leans))
    packs, notes = [own, across, *leans], [tail, tail_in, *leans]
    codes = jnp.concatenate([n[-NOTE, :slots] for n in notes]).astype(jnp.int32)
    parts = pl.pallas_call(
        functools.partial(exchange_kernel, orb, slots, aux_width),
        out_shape=jax.ShapeDtypeStruct((BS, full_width), jnp.float32),
        in_specs=[smem] + [vmem] * (orb + 1),
        out_specs=vmem,
        scratch_shapes=[pltpu.VMEM((orb, BS, BS), jnp.float32)],
        compiler_params=params,
        name="exchange",
    )(codes, half, *packs)

    step = 1
    while step < aux:
        ways = 2 if step == 1 or step * 4 > aux else 4
        terms = [parts]
        for way in range(1, ways):
            terms.append(lax.ppermute(parts, "aux", [(i, i ^ (way * step)) for i in range(aux)]))
        while len(terms) > 1:
            terms = [terms[i] + terms[i + 1] for i in range(0, len(terms), 2)]
        parts = terms[0]
        step *= ways
    return parts


def solution(mesh):
    return jax.shard_map(
        shards,
        mesh=mesh,
        in_specs=(
            P("orb", None),
            P("orb", "aux", None, None, None),
            P("orb", "aux", None),
            P("orb", "aux"),
        ),
        out_specs=P("orb", None),
        check_vma=False,
    )
```

```python
import functools

import jax
import jax.numpy as jnp
from jax import lax
from jax.experimental import pallas as pl
from jax.experimental.pallas import tpu as pltpu
from jax.sharding import PartitionSpec as P

BS = 64
LANES = 128
NOTE = 16


def lay_blocks(raw, out_ref):
    slots, aux_width = raw.shape[:2]
    square = raw.reshape(slots * aux_width, BS, BS)
    for tile in range(slots * aux_width // 2):
        both = jnp.concatenate([square[2 * tile], square[2 * tile + 1]], axis=1)
        out_ref[tile * BS : (tile + 1) * BS] = both
    return slots * aux_width // 2


def partner(i, step, sign, orb):
    if orb == 4:
        return i ^ (3 - sign) // 2
    return (i + sign * step) % orb


def owner_of(me, step, sign, orb):
    if orb == 4:
        return me ^ jnp.where(sign > 0, 1, 2)
    return lax.rem(me - sign * step + orb, orb)


def opposite(i, orb):
    return i ^ 3 if orb == 4 else (i + orb // 2) % orb


def core_parity():
    return lax.rem(lax.axis_index("aux"), 2)


def pack_kernel(
    orb, kept, pairs_hbm, density_hbm, raw_hbm, own_ref, near_ref, tail_ref, pairs, rows, raw, sems
):
    copies = [
        pltpu.make_async_copy(src, dst, sems.at[i])
        for i, (src, dst) in enumerate(((raw_hbm, raw), (density_hbm, rows), (pairs_hbm, pairs)))
    ]
    for copy in copies:
        copy.start()
    for copy in copies:
        copy.wait()
    lay_blocks(raw[0, 0], own_ref)
    height = BS // 2
    near = pl.multiple_of(core_parity() * height, height)
    tiles = rows.shape[1] // LANES
    for t in range(tiles):
        lanes = slice(t * LANES, (t + 1) * LANES)
        near_ref[t * BS : (t + 1) * BS] = rows[:, lanes]
        tail_ref[t * height : (t + 1) * height] = rows[pl.ds(near, height), lanes]
    shape = (NOTE, LANES)
    lane = lax.broadcasted_iota(jnp.int32, shape, 1)
    note = jnp.zeros(shape, jnp.int32)
    for j in range(pairs.shape[2]):
        note = jnp.where(lane == j, jnp.where(j < kept[0, 0], pairs[0, 0, j], orb), note)
    note = note.astype(jnp.float32).astype(jnp.bfloat16)
    near_ref[tiles * BS :] = note
    tail_ref[tiles * height :] = note


def lean_kernel(own_ref, near_ref, mark_ref, out_ref):
    size = own_ref.shape[0]
    out_ref[:size] = own_ref[...]
    out_ref[size:] = near_ref[near_ref.shape[0] - NOTE :]


def relay_kernel(raw, out_ref):
    lay_blocks(raw[0, 0], out_ref)


def merge_kernel(*refs):
    parts, out_ref = refs[:-1], refs[-1]
    at = 0
    for part in parts:
        count = part.shape[0] - NOTE
        out_ref[at : at + count] = part[:count]
        at += count


def half_kernel(orb, slots, aux_width, meta_ref, density_ref, own_ref, *refs):
    nears, (tail, swapped, half_ref, rows) = refs[:-4], refs[-4:]
    me = lax.axis_index("orb")
    parity = core_parity()
    height = BS // 2
    count = density_ref.shape[1] // LANES
    size = slots * aux_width * BS // LANES * BS
    mine = pl.multiple_of(parity * height, height)
    other = pl.multiple_of((1 - parity) * height, height)
    rows[me] = density_ref[...]
    for i, near in enumerate(nears):
        sign = 1 - 2 * parity
        ahead = owner_of(me, i + 1, sign, orb)
        behind = owner_of(me, i + 1, -sign, orb)
        for t in range(count):
            lanes = slice(t * LANES, (t + 1) * LANES)
            at = (i * count + t) * BS
            rows[ahead, :, lanes] = near[t * BS : (t + 1) * BS]
            rows[behind, :, lanes] = swapped[at : at + BS]
    across = opposite(me, orb)
    for t in range(count):
        lanes = slice(t * LANES, (t + 1) * LANES)
        at = len(nears) * count * BS + t * height
        rows[across, pl.ds(mine, height), lanes] = tail[t * height : (t + 1) * height]
        rows[across, pl.ds(other, height), lanes] = swapped[at : at + height]
    rows[orb] = jnp.zeros_like(rows[orb])
    selected = jnp.concatenate([rows[meta_ref[j]] for j in range(slots)], axis=0)
    own = jnp.concatenate([own_ref[at : at + BS] for at in range(0, size, BS)], axis=1)
    left = []
    for p in range(aux_width):
        cuts = [(j * aux_width + p) * BS for j in range(slots)]
        left.append(jnp.concatenate([own[:, cut : cut + BS] for cut in cuts], axis=1))
    left = jnp.concatenate(left, axis=0)
    half = jnp.dot(left, selected, preferred_element_type=jnp.float32).astype(jnp.bfloat16)
    for k in range(orb):
        half_ref[k] = jnp.concatenate(
            [half[p * BS : (p + 1) * BS, k * BS : (k + 1) * BS] for p in range(aux_width)],
            axis=1,
        )
    half_ref[orb] = jnp.zeros_like(half_ref[orb])


def exchange_kernel(orb, slots, aux_width, meta_ref, half_ref, *refs):
    packs, (out_ref, held) = refs[:orb], refs[orb:]
    me = lax.axis_index("orb")
    parity = core_parity()
    per_slot = aux_width * BS // LANES
    owners = [me, opposite(me, orb)]
    for i in range(1, orb // 2):
        owners += [owner_of(me, i, sign * (1 - 2 * parity), orb) for sign in (-1, 1)]
    for way in range(orb):
        total = None
        for j in range(slots):
            tiles = [
                packs[way][t * BS : (t + 1) * BS] for t in range(j * per_slot, (j + 1) * per_slot)
            ]
            term = lax.dot_general(
                half_ref[meta_ref[way * slots + j]],
                jnp.concatenate(tiles, axis=1),
                (((1,), (1,)), ((), ())),
                preferred_element_type=jnp.float32,
            )
            total = term if total is None else total + term
        held[owners[way]] = total
    out_ref[...] = jnp.concatenate([held[n] for n in range(orb)], axis=1)


def shards(density, tensor_blocks, pairs, kept):
    full_width = density.shape[1]
    slots = tensor_blocks.shape[2]
    aux_width = tensor_blocks.shape[3]
    orb = lax.axis_size("orb")
    aux = lax.axis_size("aux")
    rows = full_width // LANES * BS
    size = slots * aux_width * BS // LANES * BS
    vmem = pl.BlockSpec(memory_space=pltpu.VMEM)
    smem = pl.BlockSpec(memory_space=pltpu.SMEM)
    hbm = pl.BlockSpec(memory_space=pltpu.HBM)
    params = pltpu.CompilerParams(vmem_limit_bytes=32 * 1024 * 1024)

    def array(height):
        return jax.ShapeDtypeStruct((height, LANES), jnp.bfloat16)

    own, near, tail = pl.pallas_call(
        functools.partial(pack_kernel, orb),
        out_shape=[array(size), array(rows + NOTE), array(rows // 2 + NOTE)],
        in_specs=[smem, hbm, hbm, hbm],
        out_specs=[vmem] * 3,
        scratch_shapes=[
            pltpu.SMEM(pairs.shape, jnp.int32),
            pltpu.VMEM(density.shape, jnp.bfloat16),
            pltpu.VMEM(tensor_blocks.shape, jnp.bfloat16),
            pltpu.SemaphoreType.DMA((3,)),
        ],
        compiler_params=params,
        name="pack",
    )(
        kept,
        *(pltpu.with_memory_space_constraint(a, pltpu.HBM) for a in (pairs, density, tensor_blocks)),
    )
    mark = lax.ppermute(near, "aux", [(i, i ^ 1) for i in range(aux)])
    lean = pl.pallas_call(
        lean_kernel,
        out_shape=array(size + NOTE),
        in_specs=[vmem] * 3,
        out_specs=vmem,
        compiler_params=params,
        name="lean",
    )(own, near, mark)
    across = [(i, opposite(i, orb)) for i in range(orb)]
    raw = lax.ppermute(tensor_blocks, "orb", across)
    tail_in = lax.ppermute(tail, "orb", across)
    nears, leans = [], []
    for i in range(1, orb // 2):
        perm = [
            (a * orb + o, a * orb + partner(o, i, 1 - 2 * (a % 2), orb))
            for a in range(aux)
            for o in range(orb)
        ]
        nears.append(lax.ppermute(near, ("aux", "orb"), perm))
        for sign in (-1, 1):
            perm = [
                (a * orb + o, a * orb + partner(o, i, sign * (1 - 2 * (a % 2)), orb))
                for a in range(aux)
                for o in range(orb)
            ]
            leans.append(lax.ppermute(lean, ("aux", "orb"), perm))

    tail_in, raw = lax.optimization_barrier((tail_in, raw))
    merged = pl.pallas_call(
        merge_kernel,
        out_shape=array(len(nears) * rows + rows // 2),
        in_specs=[vmem] * (len(nears) + 1),
        out_specs=vmem,
        compiler_params=params,
        name="merge",
    )(*nears, tail_in)
    swapped = lax.ppermute(merged, "aux", [(i, i ^ 1) for i in range(aux)])
    across = pl.pallas_call(
        relay_kernel,
        out_shape=array(size),
        in_specs=[vmem],
        out_specs=vmem,
        compiler_params=params,
        name="relay",
    )(raw)
    half = pl.pallas_call(
        functools.partial(half_kernel, orb, slots, aux_width),
        out_shape=jax.ShapeDtypeStruct((orb + 1, BS, aux_width * BS), jnp.bfloat16),
        in_specs=[smem] + [vmem] * (len(nears) + 4),
        out_specs=vmem,
        scratch_shapes=[pltpu.VMEM((orb + 1, BS, full_width), jnp.bfloat16)],
        compiler_params=params,
        name="half",
    )(tail[-NOTE, :slots].astype(jnp.int32), density, own, *nears, tail_in, swapped)
    half, leans = lax.optimization_barrier((half, leans))
    packs, notes = [own, across, *leans], [tail, tail_in, *leans]
    codes = jnp.concatenate([n[-NOTE, :slots] for n in notes]).astype(jnp.int32)
    parts = pl.pallas_call(
        functools.partial(exchange_kernel, orb, slots, aux_width),
        out_shape=jax.ShapeDtypeStruct((BS, full_width), jnp.float32),
        in_specs=[smem] + [vmem] * (orb + 1),
        out_specs=vmem,
        scratch_shapes=[pltpu.VMEM((orb, BS, BS), jnp.float32)],
        compiler_params=params,
        name="exchange",
    )(codes, half, *packs)

    step = 1
    while step < aux:
        ways = 2 if step == 1 or step * 4 > aux else 4
        terms = [parts]
        for way in range(1, ways):
            terms.append(lax.ppermute(parts, "aux", [(i, i ^ (way * step)) for i in range(aux)]))
        while len(terms) > 1:
            terms = [terms[i] + terms[i + 1] for i in range(0, len(terms), 2)]
        parts = terms[0]
        step *= ways
    return parts


def solution(mesh):
    return jax.shard_map(
        shards,
        mesh=mesh,
        in_specs=(
            P("orb", None),
            P("orb", "aux", None, None, None),
            P("orb", "aux", None),
            P("orb", "aux"),
        ),
        out_specs=P("orb", None),
        check_vma=False,
    )
```

```python
import functools

import jax
import jax.numpy as jnp
from jax import lax
from jax.experimental import pallas as pl
from jax.experimental.pallas import tpu as pltpu
from jax.sharding import PartitionSpec as P

BS = 64
LANES = 128
NOTE = 16


def lay_blocks(raw, out_ref):
    slots, aux_width = raw.shape[:2]
    square = raw.reshape(slots * aux_width, BS, BS)
    for tile in range(slots * aux_width // 2):
        both = jnp.concatenate([square[2 * tile], square[2 * tile + 1]], axis=1)
        out_ref[tile * BS : (tile + 1) * BS] = both
    return slots * aux_width // 2


def partner(i, step, sign, orb):
    if orb == 4:
        return i ^ (2 - sign)
    return (i + sign * step) % orb


def owner_of(me, step, sign, orb):
    if orb == 4:
        return me ^ (2 - sign)
    return lax.rem(me - sign * step + orb, orb)


def core_parity():
    return lax.rem(lax.axis_index("aux"), 2)


def pack_kernel(
    orb, kept, pairs_hbm, density_hbm, raw_hbm, full_ref, tail_ref, pairs, rows, raw, sems
):
    copies = [
        pltpu.make_async_copy(src, dst, sems.at[i])
        for i, (src, dst) in enumerate(((raw_hbm, raw), (density_hbm, rows), (pairs_hbm, pairs)))
    ]
    for copy in copies:
        copy.start()
    for copy in copies:
        copy.wait()
    size = lay_blocks(raw[0, 0], full_ref) * BS
    height = BS // 2
    near = pl.multiple_of(core_parity() * height, height)
    tiles = rows.shape[1] // LANES
    for t in range(tiles):
        lanes = slice(t * LANES, (t + 1) * LANES)
        full_ref[size + t * BS : size + (t + 1) * BS] = rows[:, lanes]
        tail_ref[t * height : (t + 1) * height] = rows[pl.ds(near, height), lanes]
    shape = (NOTE, LANES)
    lane = lax.broadcasted_iota(jnp.int32, shape, 1)
    note = jnp.zeros(shape, jnp.int32)
    for j in range(pairs.shape[2]):
        note = jnp.where(lane == j, jnp.where(j < kept[0, 0], pairs[0, 0, j], orb), note)
    note = note.astype(jnp.float32).astype(jnp.bfloat16)
    full_ref[size + tiles * BS :] = note
    tail_ref[tiles * height :] = note


def lean_kernel(full_ref, out_ref):
    size = out_ref.shape[0] - NOTE
    out_ref[:size] = full_ref[:size]
    out_ref[size:] = full_ref[full_ref.shape[0] - NOTE :]


def relay_kernel(raw, out_ref):
    lay_blocks(raw[0, 0], out_ref)


def merge_kernel(size, *refs):
    parts, out_ref = refs[:-1], refs[-1]
    at = 0
    for i, part in enumerate(parts):
        first = size if i < len(parts) - 1 else 0
        count = part.shape[0] - NOTE - first
        out_ref[at : at + count] = part[first : first + count]
        at += count


def half_kernel(orb, slots, aux_width, meta_ref, density_ref, own_ref, *refs):
    fulls, (tail, swapped, half_ref, rows) = refs[:-4], refs[-4:]
    me = lax.axis_index("orb")
    parity = core_parity()
    height = BS // 2
    count = density_ref.shape[1] // LANES
    size = slots * aux_width * BS // LANES * BS
    near = pl.multiple_of(parity * height, height)
    far = pl.multiple_of((1 - parity) * height, height)
    rows[me] = density_ref[...]
    for i, full in enumerate(fulls):
        sign = 1 - 2 * parity
        ahead = owner_of(me, i + 1, sign, orb)
        behind = owner_of(me, i + 1, -sign, orb)
        for t in range(count):
            lanes = slice(t * LANES, (t + 1) * LANES)
            at = (i * count + t) * BS
            rows[ahead, :, lanes] = full[size + t * BS : size + (t + 1) * BS]
            rows[behind, :, lanes] = swapped[at : at + BS]
    across = lax.rem(me + orb // 2, orb)
    for t in range(count):
        lanes = slice(t * LANES, (t + 1) * LANES)
        at = len(fulls) * count * BS + t * height
        rows[across, pl.ds(near, height), lanes] = tail[t * height : (t + 1) * height]
        rows[across, pl.ds(far, height), lanes] = swapped[at : at + height]
    rows[orb] = jnp.zeros_like(rows[orb])
    selected = jnp.concatenate([rows[meta_ref[j]] for j in range(slots)], axis=0)
    own = jnp.concatenate([own_ref[at : at + BS] for at in range(0, size, BS)], axis=1)
    left = []
    for p in range(aux_width):
        cuts = [(j * aux_width + p) * BS for j in range(slots)]
        left.append(jnp.concatenate([own[:, cut : cut + BS] for cut in cuts], axis=1))
    left = jnp.concatenate(left, axis=0)
    half = jnp.dot(left, selected, preferred_element_type=jnp.float32).astype(jnp.bfloat16)
    for k in range(orb):
        half_ref[k] = jnp.concatenate(
            [half[p * BS : (p + 1) * BS, k * BS : (k + 1) * BS] for p in range(aux_width)],
            axis=1,
        )
    half_ref[orb] = jnp.zeros_like(half_ref[orb])


def exchange_kernel(orb, slots, aux_width, meta_ref, half_ref, *refs):
    packs, (out_ref, held) = refs[:orb], refs[orb:]
    me = lax.axis_index("orb")
    parity = core_parity()
    per_slot = aux_width * BS // LANES
    sign = 1 - 2 * parity
    owners = [me, lax.rem(me + orb // 2, orb)]
    for i in range(1, orb // 2):
        owners += [owner_of(me, i, sign, orb), owner_of(me, i, -sign, orb)]
    for way in range(orb):
        total = None
        for j in range(slots):
            tiles = [
                packs[way][t * BS : (t + 1) * BS] for t in range(j * per_slot, (j + 1) * per_slot)
            ]
            term = lax.dot_general(
                half_ref[meta_ref[way * slots + j]],
                jnp.concatenate(tiles, axis=1),
                (((1,), (1,)), ((), ())),
                preferred_element_type=jnp.float32,
            )
            total = term if total is None else total + term
        held[owners[way]] = total
    out_ref[...] = jnp.concatenate([held[n] for n in range(orb)], axis=1)


def shards(density, tensor_blocks, pairs, kept):
    full_width = density.shape[1]
    slots = tensor_blocks.shape[2]
    aux_width = tensor_blocks.shape[3]
    orb = lax.axis_size("orb")
    aux = lax.axis_size("aux")
    rows = full_width // LANES * BS
    size = slots * aux_width * BS // LANES * BS
    vmem = pl.BlockSpec(memory_space=pltpu.VMEM)
    smem = pl.BlockSpec(memory_space=pltpu.SMEM)
    hbm = pl.BlockSpec(memory_space=pltpu.HBM)
    params = pltpu.CompilerParams(vmem_limit_bytes=32 * 1024 * 1024)

    def array(height):
        return jax.ShapeDtypeStruct((height, LANES), jnp.bfloat16)

    def shift(x, step, sign):
        perm = [
            (a * orb + o, a * orb + partner(o, step, sign * (1 - 2 * (a % 2)), orb))
            for a in range(aux)
            for o in range(orb)
        ]
        return lax.ppermute(x, ("aux", "orb"), perm)

    full, tail = pl.pallas_call(
        functools.partial(pack_kernel, orb),
        out_shape=[array(size + rows + NOTE), array(rows // 2 + NOTE)],
        in_specs=[smem, hbm, hbm, hbm],
        out_specs=[vmem] * 2,
        scratch_shapes=[
            pltpu.SMEM(pairs.shape, jnp.int32),
            pltpu.VMEM(density.shape, jnp.bfloat16),
            pltpu.VMEM(tensor_blocks.shape, jnp.bfloat16),
            pltpu.SemaphoreType.DMA((3,)),
        ],
        compiler_params=params,
        name="pack",
    )(
        kept,
        *(pltpu.with_memory_space_constraint(a, pltpu.HBM) for a in (pairs, density, tensor_blocks)),
    )
    lean = pl.pallas_call(
        lean_kernel,
        out_shape=array(size + NOTE),
        in_specs=[vmem],
        out_specs=vmem,
        compiler_params=params,
        name="lean",
    )(full)
    across = [(i, (i + orb // 2) % orb) for i in range(orb)]
    raw = lax.ppermute(tensor_blocks, "orb", across)
    tail_in = lax.ppermute(tail, "orb", across)
    fulls = [shift(full, i, 1) for i in range(1, orb // 2)]
    leans = [shift(lean, i, -1) for i in range(1, orb // 2)]

    tail_in, raw = lax.optimization_barrier((tail_in, raw))
    merged = pl.pallas_call(
        functools.partial(merge_kernel, size),
        out_shape=array(len(fulls) * rows + rows // 2),
        in_specs=[vmem] * (len(fulls) + 1),
        out_specs=vmem,
        compiler_params=params,
        name="merge",
    )(*fulls, tail_in)
    swapped = lax.ppermute(merged, "aux", [(i, i ^ 1) for i in range(aux)])
    across = pl.pallas_call(
        relay_kernel,
        out_shape=array(size),
        in_specs=[vmem],
        out_specs=vmem,
        compiler_params=params,
        name="relay",
    )(raw)
    half = pl.pallas_call(
        functools.partial(half_kernel, orb, slots, aux_width),
        out_shape=jax.ShapeDtypeStruct((orb + 1, BS, aux_width * BS), jnp.bfloat16),
        in_specs=[smem] + [vmem] * (len(fulls) + 4),
        out_specs=vmem,
        scratch_shapes=[pltpu.VMEM((orb + 1, BS, full_width), jnp.bfloat16)],
        compiler_params=params,
        name="half",
    )(tail[-NOTE, :slots].astype(jnp.int32), density, full, *fulls, tail_in, swapped)
    half, leans = lax.optimization_barrier((half, leans))
    packs, notes = [full, across], [tail, tail_in]
    for pair in zip(fulls, leans):
        packs += pair
        notes += pair
    codes = jnp.concatenate([n[-NOTE, :slots] for n in notes]).astype(jnp.int32)
    parts = pl.pallas_call(
        functools.partial(exchange_kernel, orb, slots, aux_width),
        out_shape=jax.ShapeDtypeStruct((BS, full_width), jnp.float32),
        in_specs=[smem] + [vmem] * (orb + 1),
        out_specs=vmem,
        scratch_shapes=[pltpu.VMEM((orb, BS, BS), jnp.float32)],
        compiler_params=params,
        name="exchange",
    )(codes, half, *packs)

    odd = core_parity() == 1
    parts = parts + lax.ppermute(parts, "aux", [(i, i ^ 1) for i in range(aux)])
    step = 2
    while step < aux:
        if step * 4 > aux:
            parts = parts + lax.ppermute(parts, "aux", [(i, i ^ step) for i in range(aux)])
            break
        first = [(i, i ^ (2 * step if i % 2 else step)) for i in range(aux)]
        second = [(i, i ^ (3 * step)) for i in range(aux) if i % 2]
        one = lax.ppermute(parts, "aux", first)
        two = lax.ppermute(parts, "aux", second)
        parts = one + jnp.where(odd, two, parts)
        parts = parts + lax.ppermute(parts, "aux", [(i, i ^ 1) for i in range(aux)])
        step *= 4
    return parts


def solution(mesh):
    return jax.shard_map(
        shards,
        mesh=mesh,
        in_specs=(
            P("orb", None),
            P("orb", "aux", None, None, None),
            P("orb", "aux", None),
            P("orb", "aux"),
        ),
        out_specs=P("orb", None),
        check_vma=False,
    )
```

```python
import functools

import jax
import jax.numpy as jnp
from jax import lax
from jax.experimental import pallas as pl
from jax.experimental.pallas import tpu as pltpu
from jax.sharding import PartitionSpec as P

BS = 64
LANES = 128
NOTE = 16


def lay_blocks(raw, out_ref):
    slots, aux_width = raw.shape[:2]
    square = raw.reshape(slots * aux_width, BS, BS)
    for tile in range(slots * aux_width // 2):
        both = jnp.concatenate([square[2 * tile], square[2 * tile + 1]], axis=1)
        out_ref[tile * BS : (tile + 1) * BS] = both
    return slots * aux_width // 2


def partner(i, step, sign, orb):
    if orb == 4:
        return i ^ (3 - sign) // 2
    return (i + sign * step) % orb


def owner_of(me, step, sign, orb):
    if orb == 4:
        return me ^ jnp.where(sign > 0, 1, 2)
    return lax.rem(me - sign * step + orb, orb)


def opposite(i, orb):
    return i ^ 3 if orb == 4 else (i + orb // 2) % orb


def core_parity():
    return lax.rem(lax.axis_index("aux"), 2)


def pack_kernel(
    orb, kept, pairs_hbm, density_hbm, raw_hbm, own_ref, near_ref, pairs, rows, raw, sems
):
    copies = [
        pltpu.make_async_copy(src, dst, sems.at[i])
        for i, (src, dst) in enumerate(((raw_hbm, raw), (density_hbm, rows), (pairs_hbm, pairs)))
    ]
    for copy in copies:
        copy.start()
    for copy in copies:
        copy.wait()
    lay_blocks(raw[0, 0], own_ref)
    tiles = rows.shape[1] // LANES
    for t in range(tiles):
        near_ref[t * BS : (t + 1) * BS] = rows[:, t * LANES : (t + 1) * LANES]
    shape = (NOTE, LANES)
    lane = lax.broadcasted_iota(jnp.int32, shape, 1)
    note = jnp.zeros(shape, jnp.int32)
    for j in range(pairs.shape[2]):
        note = jnp.where(lane == j, jnp.where(j < kept[0, 0], pairs[0, 0, j], orb), note)
    near_ref[tiles * BS :] = note.astype(jnp.float32).astype(jnp.bfloat16)


def relay_kernel(raw, out_ref):
    lay_blocks(raw[0, 0], out_ref)


def join_kernel(own_ref, near_ref, met_ref, out_ref):
    size = own_ref.shape[0]
    out_ref[:size] = own_ref[...]
    out_ref[size : size + NOTE] = near_ref[near_ref.shape[0] - NOTE :]
    out_ref[size + NOTE :] = met_ref[...]


def exchange_kernel(orb, slots, aux_width, meta_ref, density_ref, own_ref, far_ref, last_ref, *refs):
    out_ref, rows, half_ref, held = refs[-4:]
    count = (len(refs) - 4) // 4
    met, swapped, first, second = (refs[i * count : (i + 1) * count] for i in range(4))
    me = lax.axis_index("orb")
    sign = 1 - 2 * core_parity()
    size = own_ref.shape[0]
    tiles = density_ref.shape[1] // LANES
    owners = [me, opposite(me, orb)]
    packs = [own_ref, far_ref]
    rows[me] = density_ref[...]
    parts = [(owners[1], last_ref, last_ref.shape[0] - tiles * BS - NOTE)]
    for i in range(count):
        owners += [owner_of(me, i + 1, sign, orb), owner_of(me, i + 1, -sign, orb)]
        packs += [first[i], second[i]]
        parts += [(owners[-2], met[i], 0), (owners[-1], swapped[i], 0)]
    for owner, part, at in parts:
        for t in range(tiles):
            rows[owner, :, t * LANES : (t + 1) * LANES] = part[at + t * BS : at + (t + 1) * BS]
    rows[orb] = jnp.zeros_like(rows[orb])
    selected = jnp.concatenate([rows[meta_ref[j]] for j in range(slots)], axis=0)
    own = jnp.concatenate([own_ref[at : at + BS] for at in range(0, size, BS)], axis=1)
    left = []
    for p in range(aux_width):
        cuts = [(j * aux_width + p) * BS for j in range(slots)]
        left.append(jnp.concatenate([own[:, cut : cut + BS] for cut in cuts], axis=1))
    left = jnp.concatenate(left, axis=0)
    half = jnp.dot(left, selected, preferred_element_type=jnp.float32).astype(jnp.bfloat16)
    for k in range(orb):
        half_ref[k] = jnp.concatenate(
            [half[p * BS : (p + 1) * BS, k * BS : (k + 1) * BS] for p in range(aux_width)],
            axis=1,
        )
    half_ref[orb] = jnp.zeros_like(half_ref[orb])
    for way in range(orb):
        codes = [meta_ref[way * slots + j] for j in range(slots)]
        held[owners[way]] = lax.dot_general(
            jnp.concatenate([half_ref[code] for code in codes], axis=1),
            jnp.concatenate([packs[way][at : at + BS] for at in range(0, size, BS)], axis=1),
            (((1,), (1,)), ((), ())),
            preferred_element_type=jnp.float32,
        )
    out_ref[...] = jnp.concatenate([held[n] for n in range(orb)], axis=1)


def shards(density, tensor_blocks, pairs, kept):
    full_width = density.shape[1]
    slots = tensor_blocks.shape[2]
    aux_width = tensor_blocks.shape[3]
    orb = lax.axis_size("orb")
    aux = lax.axis_size("aux")
    rows = full_width // LANES * BS
    size = slots * aux_width * BS // LANES * BS
    vmem = pl.BlockSpec(memory_space=pltpu.VMEM)
    smem = pl.BlockSpec(memory_space=pltpu.SMEM)
    hbm = pl.BlockSpec(memory_space=pltpu.HBM)
    params = pltpu.CompilerParams(vmem_limit_bytes=32 * 1024 * 1024)

    def array(height):
        return jax.ShapeDtypeStruct((height, LANES), jnp.bfloat16)

    def shift(x, step, sign):
        perm = [
            (a * orb + o, a * orb + partner(o, step, sign * (1 - 2 * (a % 2)), orb))
            for a in range(aux)
            for o in range(orb)
        ]
        return lax.ppermute(x, ("aux", "orb"), perm)

    own, near = pl.pallas_call(
        functools.partial(pack_kernel, orb),
        out_shape=[array(size), array(rows + NOTE)],
        in_specs=[smem, hbm, hbm, hbm],
        out_specs=[vmem] * 2,
        scratch_shapes=[
            pltpu.SMEM(pairs.shape, jnp.int32),
            pltpu.VMEM(density.shape, jnp.bfloat16),
            pltpu.VMEM(tensor_blocks.shape, jnp.bfloat16),
            pltpu.SemaphoreType.DMA((3,)),
        ],
        compiler_params=params,
        name="pack",
    )(
        kept,
        *(pltpu.with_memory_space_constraint(a, pltpu.HBM) for a in (pairs, density, tensor_blocks)),
    )
    across = [(i, opposite(i, orb)) for i in range(orb)]
    raw = lax.ppermute(tensor_blocks, "orb", across)
    steps = range(1, orb // 2)
    met = [shift(near, i, 1) for i in steps]
    first = [shift(own, i, 1) for i in steps]
    met, raw = lax.optimization_barrier((met, raw))
    second = []
    for i in steps:
        joined = pl.pallas_call(
            join_kernel,
            out_shape=array(size + NOTE + rows + NOTE),
            in_specs=[vmem] * 3,
            out_specs=vmem,
            compiler_params=params,
            name="join",
        )(own, near, met[i - 1])
        second.append(shift(joined, i, -1))
    last = second[0] if orb == 4 else lax.ppermute(near, "orb", across)
    swapped = [lax.ppermute(x, "aux", [(i, i ^ 1) for i in range(aux)]) for x in met]
    far = pl.pallas_call(
        relay_kernel,
        out_shape=array(size),
        in_specs=[vmem],
        out_specs=vmem,
        compiler_params=params,
        name="relay",
    )(raw)
    notes = [near[-NOTE], last[-NOTE]]
    for i in range(len(met)):
        notes += [met[i][-NOTE], second[i][size]]
    codes = jnp.concatenate([note[:slots] for note in notes]).astype(jnp.int32)
    parts = pl.pallas_call(
        functools.partial(exchange_kernel, orb, slots, aux_width),
        out_shape=jax.ShapeDtypeStruct((BS, full_width), jnp.float32),
        in_specs=[smem] + [vmem] * (4 + 4 * len(met)),
        out_specs=vmem,
        scratch_shapes=[
            pltpu.VMEM((orb + 1, BS, full_width), jnp.bfloat16),
            pltpu.VMEM((orb + 1, BS, aux_width * BS), jnp.bfloat16),
            pltpu.VMEM((orb, BS, BS), jnp.float32),
        ],
        compiler_params=params,
        name="exchange",
    )(codes, density, own, far, last, *met, *swapped, *first, *second)

    parts = parts + lax.ppermute(parts, "aux", [(i, i ^ 1) for i in range(aux)])
    step = 2
    while step < aux:
        ways = 2 if step * 4 > aux else 4
        terms = [parts]
        for way in range(1, ways):
            terms.append(lax.ppermute(parts, "aux", [(i, i ^ (way * step)) for i in range(aux)]))
        while len(terms) > 1:
            terms = [terms[i] + terms[i + 1] for i in range(0, len(terms), 2)]
        parts = terms[0]
        step *= ways
    return parts


def solution(mesh):
    return jax.shard_map(
        shards,
        mesh=mesh,
        in_specs=(
            P("orb", None),
            P("orb", "aux", None, None, None),
            P("orb", "aux", None),
            P("orb", "aux"),
        ),
        out_specs=P("orb", None),
        check_vma=False,
    )
```

```python
import functools

import jax
import jax.numpy as jnp
from jax import lax
from jax.experimental import pallas as pl
from jax.experimental.pallas import tpu as pltpu
from jax.sharding import PartitionSpec as P

BS = 64
LANES = 128
NOTE = 16


def lay_blocks(raw, out_ref):
    slots, aux_width = raw.shape[:2]
    square = raw.reshape(slots * aux_width, BS, BS)
    for tile in range(slots * aux_width // 2):
        both = jnp.concatenate([square[2 * tile], square[2 * tile + 1]], axis=1)
        out_ref[tile * BS : (tile + 1) * BS] = both
    return slots * aux_width // 2


def partner(i, step, sign, orb):
    if orb == 4:
        return i ^ (3 - sign) // 2
    return (i + sign * step) % orb


def owner_of(me, step, sign, orb):
    if orb == 4:
        return me ^ jnp.where(sign > 0, 1, 2)
    return lax.rem(me - sign * step + orb, orb)


def opposite(i, orb):
    return i ^ 3 if orb == 4 else (i + orb // 2) % orb


def core_parity():
    return lax.rem(lax.axis_index("aux"), 2)


def pack_kernel(
    orb, kept, pairs_hbm, density_hbm, raw_hbm, full_ref, tail_ref, pairs, rows, raw, sems
):
    copies = [
        pltpu.make_async_copy(src, dst, sems.at[i])
        for i, (src, dst) in enumerate(((raw_hbm, raw), (density_hbm, rows), (pairs_hbm, pairs)))
    ]
    for copy in copies:
        copy.start()
    for copy in copies:
        copy.wait()
    size = lay_blocks(raw[0, 0], full_ref) * BS
    height = BS // 2
    near = pl.multiple_of(core_parity() * height, height)
    tiles = rows.shape[1] // LANES
    for t in range(tiles):
        lanes = slice(t * LANES, (t + 1) * LANES)
        full_ref[size + t * BS : size + (t + 1) * BS] = rows[:, lanes]
        tail_ref[t * height : (t + 1) * height] = rows[pl.ds(near, height), lanes]
    shape = (NOTE, LANES)
    lane = lax.broadcasted_iota(jnp.int32, shape, 1)
    note = jnp.zeros(shape, jnp.int32)
    for j in range(pairs.shape[2]):
        note = jnp.where(lane == j, jnp.where(j < kept[0, 0], pairs[0, 0, j], orb), note)
    note = note.astype(jnp.float32).astype(jnp.bfloat16)
    full_ref[size + tiles * BS :] = note
    tail_ref[tiles * height :] = note


def lean_kernel(full_ref, out_ref):
    size = out_ref.shape[0] - NOTE
    out_ref[:size] = full_ref[:size]
    out_ref[size:] = full_ref[full_ref.shape[0] - NOTE :]


def relay_kernel(raw, out_ref):
    lay_blocks(raw[0, 0], out_ref)


def merge_kernel(size, *refs):
    parts, out_ref = refs[:-1], refs[-1]
    at = 0
    for i, part in enumerate(parts):
        first = size if i < len(parts) - 1 else 0
        count = part.shape[0] - NOTE - first
        out_ref[at : at + count] = part[first : first + count]
        at += count


def half_kernel(orb, slots, aux_width, meta_ref, density_ref, own_ref, *refs):
    fulls, (tail, swapped, half_ref, rows) = refs[:-4], refs[-4:]
    me = lax.axis_index("orb")
    parity = core_parity()
    height = BS // 2
    count = density_ref.shape[1] // LANES
    size = slots * aux_width * BS // LANES * BS
    near = pl.multiple_of(parity * height, height)
    far = pl.multiple_of((1 - parity) * height, height)
    rows[me] = density_ref[...]
    for i, full in enumerate(fulls):
        sign = 1 - 2 * parity
        ahead = owner_of(me, i + 1, sign, orb)
        behind = owner_of(me, i + 1, -sign, orb)
        for t in range(count):
            lanes = slice(t * LANES, (t + 1) * LANES)
            at = (i * count + t) * BS
            rows[ahead, :, lanes] = full[size + t * BS : size + (t + 1) * BS]
            rows[behind, :, lanes] = swapped[at : at + BS]
    across = opposite(me, orb)
    for t in range(count):
        lanes = slice(t * LANES, (t + 1) * LANES)
        at = len(fulls) * count * BS + t * height
        rows[across, pl.ds(near, height), lanes] = tail[t * height : (t + 1) * height]
        rows[across, pl.ds(far, height), lanes] = swapped[at : at + height]
    rows[orb] = jnp.zeros_like(rows[orb])
    selected = jnp.concatenate([rows[meta_ref[j]] for j in range(slots)], axis=0)
    own = jnp.concatenate([own_ref[at : at + BS] for at in range(0, size, BS)], axis=1)
    left = []
    for p in range(aux_width):
        cuts = [(j * aux_width + p) * BS for j in range(slots)]
        left.append(jnp.concatenate([own[:, cut : cut + BS] for cut in cuts], axis=1))
    left = jnp.concatenate(left, axis=0)
    half = jnp.dot(left, selected, preferred_element_type=jnp.float32).astype(jnp.bfloat16)
    for k in range(orb):
        half_ref[k] = jnp.concatenate(
            [half[p * BS : (p + 1) * BS, k * BS : (k + 1) * BS] for p in range(aux_width)],
            axis=1,
        )
    half_ref[orb] = jnp.zeros_like(half_ref[orb])


def exchange_kernel(orb, slots, aux_width, meta_ref, half_ref, *refs):
    packs, (out_ref, held) = refs[:orb], refs[orb:]
    me = lax.axis_index("orb")
    parity = core_parity()
    per_slot = aux_width * BS // LANES
    sign = 1 - 2 * parity
    owners = [me, opposite(me, orb)]
    for i in range(1, orb // 2):
        owners += [owner_of(me, i, sign, orb), owner_of(me, i, -sign, orb)]
    for way in range(orb):
        total = None
        for j in range(slots):
            tiles = [
                packs[way][t * BS : (t + 1) * BS] for t in range(j * per_slot, (j + 1) * per_slot)
            ]
            term = lax.dot_general(
                half_ref[meta_ref[way * slots + j]],
                jnp.concatenate(tiles, axis=1),
                (((1,), (1,)), ((), ())),
                preferred_element_type=jnp.float32,
            )
            total = term if total is None else total + term
        held[owners[way]] = total
    out_ref[...] = jnp.concatenate([held[n] for n in range(orb)], axis=1)


def shards(density, tensor_blocks, pairs, kept):
    full_width = density.shape[1]
    slots = tensor_blocks.shape[2]
    aux_width = tensor_blocks.shape[3]
    orb = lax.axis_size("orb")
    aux = lax.axis_size("aux")
    rows = full_width // LANES * BS
    size = slots * aux_width * BS // LANES * BS
    vmem = pl.BlockSpec(memory_space=pltpu.VMEM)
    smem = pl.BlockSpec(memory_space=pltpu.SMEM)
    hbm = pl.BlockSpec(memory_space=pltpu.HBM)
    params = pltpu.CompilerParams(vmem_limit_bytes=32 * 1024 * 1024)

    def array(height):
        return jax.ShapeDtypeStruct((height, LANES), jnp.bfloat16)

    def shift(x, step, sign):
        perm = [
            (a * orb + o, a * orb + partner(o, step, sign * (1 - 2 * (a % 2)), orb))
            for a in range(aux)
            for o in range(orb)
        ]
        return lax.ppermute(x, ("aux", "orb"), perm)

    full, tail = pl.pallas_call(
        functools.partial(pack_kernel, orb),
        out_shape=[array(size + rows + NOTE), array(rows // 2 + NOTE)],
        in_specs=[smem, hbm, hbm, hbm],
        out_specs=[vmem] * 2,
        scratch_shapes=[
            pltpu.SMEM(pairs.shape, jnp.int32),
            pltpu.VMEM(density.shape, jnp.bfloat16),
            pltpu.VMEM(tensor_blocks.shape, jnp.bfloat16),
            pltpu.SemaphoreType.DMA((3,)),
        ],
        compiler_params=params,
        name="pack",
    )(
        kept,
        *(pltpu.with_memory_space_constraint(a, pltpu.HBM) for a in (pairs, density, tensor_blocks)),
    )
    lean = pl.pallas_call(
        lean_kernel,
        out_shape=array(size + NOTE),
        in_specs=[vmem],
        out_specs=vmem,
        compiler_params=params,
        name="lean",
    )(full)
    across = [(i, opposite(i, orb)) for i in range(orb)]
    raw = lax.ppermute(tensor_blocks, "orb", across)
    tail_in = lax.ppermute(tail, "orb", across)
    fulls = [shift(full, i, 1) for i in range(1, orb // 2)]
    leans = [shift(lean, i, -1) for i in range(1, orb // 2)]

    tail_in, raw = lax.optimization_barrier((tail_in, raw))
    merged = pl.pallas_call(
        functools.partial(merge_kernel, size),
        out_shape=array(len(fulls) * rows + rows // 2),
        in_specs=[vmem] * (len(fulls) + 1),
        out_specs=vmem,
        compiler_params=params,
        name="merge",
    )(*fulls, tail_in)
    swapped = lax.ppermute(merged, "aux", [(i, i ^ 1) for i in range(aux)])
    across = pl.pallas_call(
        relay_kernel,
        out_shape=array(size),
        in_specs=[vmem],
        out_specs=vmem,
        compiler_params=params,
        name="relay",
    )(raw)
    half = pl.pallas_call(
        functools.partial(half_kernel, orb, slots, aux_width),
        out_shape=jax.ShapeDtypeStruct((orb + 1, BS, aux_width * BS), jnp.bfloat16),
        in_specs=[smem] + [vmem] * (len(fulls) + 4),
        out_specs=vmem,
        scratch_shapes=[pltpu.VMEM((orb + 1, BS, full_width), jnp.bfloat16)],
        compiler_params=params,
        name="half",
    )(tail[-NOTE, :slots].astype(jnp.int32), density, full, *fulls, tail_in, swapped)
    half, leans = lax.optimization_barrier((half, leans))
    packs, notes = [full, across], [tail, tail_in]
    for pair in zip(fulls, leans):
        packs += pair
        notes += pair
    codes = jnp.concatenate([n[-NOTE, :slots] for n in notes]).astype(jnp.int32)
    parts = pl.pallas_call(
        functools.partial(exchange_kernel, orb, slots, aux_width),
        out_shape=jax.ShapeDtypeStruct((BS, full_width), jnp.float32),
        in_specs=[smem] + [vmem] * (orb + 1),
        out_specs=vmem,
        scratch_shapes=[pltpu.VMEM((orb, BS, BS), jnp.float32)],
        compiler_params=params,
        name="exchange",
    )(codes, half, *packs)

    step = 1
    while step < aux:
        ways = 2 if step == 1 or step * 4 > aux else 4
        terms = [parts]
        for way in range(1, ways):
            terms.append(lax.ppermute(parts, "aux", [(i, i ^ (way * step)) for i in range(aux)]))
        while len(terms) > 1:
            terms = [terms[i] + terms[i + 1] for i in range(0, len(terms), 2)]
        parts = terms[0]
        step *= ways
    return parts


def solution(mesh):
    return jax.shard_map(
        shards,
        mesh=mesh,
        in_specs=(
            P("orb", None),
            P("orb", "aux", None, None, None),
            P("orb", "aux", None),
            P("orb", "aux"),
        ),
        out_specs=P("orb", None),
        check_vma=False,
    )
```

```python
import functools

import jax
import jax.numpy as jnp
from jax import lax
from jax.experimental import pallas as pl
from jax.experimental.pallas import tpu as pltpu
from jax.sharding import PartitionSpec as P

BS = 64
LANES = 128
NOTE = 16


def lay_blocks(raw, out_ref):
    slots, aux_width = raw.shape[:2]
    square = raw.reshape(slots * aux_width, BS, BS)
    for tile in range(slots * aux_width // 2):
        both = jnp.concatenate([square[2 * tile], square[2 * tile + 1]], axis=1)
        out_ref[tile * BS : (tile + 1) * BS] = both
    return slots * aux_width // 2


def partner(i, step, sign, orb):
    if orb == 4:
        return i ^ (2 + sign)
    return (i + sign * step) % orb


def owner_of(me, step, sign, orb):
    if orb == 4:
        return me ^ (2 + sign)
    return lax.rem(me - sign * step + orb, orb)


def core_parity():
    return lax.rem(lax.axis_index("aux"), 2)


def pack_kernel(
    orb, kept, pairs_hbm, density_hbm, raw_hbm, full_ref, tail_ref, pairs, rows, raw, sems
):
    copies = [
        pltpu.make_async_copy(src, dst, sems.at[i])
        for i, (src, dst) in enumerate(((raw_hbm, raw), (density_hbm, rows), (pairs_hbm, pairs)))
    ]
    for copy in copies:
        copy.start()
    for copy in copies:
        copy.wait()
    size = lay_blocks(raw[0, 0], full_ref) * BS
    height = BS // 2
    near = pl.multiple_of(core_parity() * height, height)
    tiles = rows.shape[1] // LANES
    for t in range(tiles):
        lanes = slice(t * LANES, (t + 1) * LANES)
        full_ref[size + t * BS : size + (t + 1) * BS] = rows[:, lanes]
        tail_ref[t * height : (t + 1) * height] = rows[pl.ds(near, height), lanes]
    shape = (NOTE, LANES)
    lane = lax.broadcasted_iota(jnp.int32, shape, 1)
    note = jnp.zeros(shape, jnp.int32)
    for j in range(pairs.shape[2]):
        note = jnp.where(lane == j, jnp.where(j < kept[0, 0], pairs[0, 0, j], orb), note)
    note = note.astype(jnp.float32).astype(jnp.bfloat16)
    full_ref[size + tiles * BS :] = note
    tail_ref[tiles * height :] = note


def lean_kernel(full_ref, out_ref):
    size = out_ref.shape[0] - NOTE
    out_ref[:size] = full_ref[:size]
    out_ref[size:] = full_ref[full_ref.shape[0] - NOTE :]


def relay_kernel(raw, out_ref):
    lay_blocks(raw[0, 0], out_ref)


def merge_kernel(size, *refs):
    parts, out_ref = refs[:-1], refs[-1]
    at = 0
    for i, part in enumerate(parts):
        first = size if i < len(parts) - 1 else 0
        count = part.shape[0] - NOTE - first
        out_ref[at : at + count] = part[first : first + count]
        at += count


def half_kernel(orb, slots, aux_width, meta_ref, density_ref, own_ref, *refs):
    fulls, (tail, swapped, half_ref, rows) = refs[:-4], refs[-4:]
    me = lax.axis_index("orb")
    parity = core_parity()
    height = BS // 2
    count = density_ref.shape[1] // LANES
    size = slots * aux_width * BS // LANES * BS
    near = pl.multiple_of(parity * height, height)
    far = pl.multiple_of((1 - parity) * height, height)
    rows[me] = density_ref[...]
    for i, full in enumerate(fulls):
        sign = 1 - 2 * parity
        ahead = owner_of(me, i + 1, sign, orb)
        behind = owner_of(me, i + 1, -sign, orb)
        for t in range(count):
            lanes = slice(t * LANES, (t + 1) * LANES)
            at = (i * count + t) * BS
            rows[ahead, :, lanes] = full[size + t * BS : size + (t + 1) * BS]
            rows[behind, :, lanes] = swapped[at : at + BS]
    across = lax.rem(me + orb // 2, orb)
    for t in range(count):
        lanes = slice(t * LANES, (t + 1) * LANES)
        at = len(fulls) * count * BS + t * height
        rows[across, pl.ds(near, height), lanes] = tail[t * height : (t + 1) * height]
        rows[across, pl.ds(far, height), lanes] = swapped[at : at + height]
    rows[orb] = jnp.zeros_like(rows[orb])
    selected = jnp.concatenate([rows[meta_ref[j]] for j in range(slots)], axis=0)
    own = jnp.concatenate([own_ref[at : at + BS] for at in range(0, size, BS)], axis=1)
    left = []
    for p in range(aux_width):
        cuts = [(j * aux_width + p) * BS for j in range(slots)]
        left.append(jnp.concatenate([own[:, cut : cut + BS] for cut in cuts], axis=1))
    left = jnp.concatenate(left, axis=0)
    half = jnp.dot(left, selected, preferred_element_type=jnp.float32).astype(jnp.bfloat16)
    for k in range(orb):
        half_ref[k] = jnp.concatenate(
            [half[p * BS : (p + 1) * BS, k * BS : (k + 1) * BS] for p in range(aux_width)],
            axis=1,
        )
    half_ref[orb] = jnp.zeros_like(half_ref[orb])


def exchange_kernel(orb, slots, aux_width, meta_ref, half_ref, *refs):
    packs, (out_ref, held) = refs[:orb], refs[orb:]
    me = lax.axis_index("orb")
    parity = core_parity()
    per_slot = aux_width * BS // LANES
    sign = 1 - 2 * parity
    owners = [me, lax.rem(me + orb // 2, orb)]
    for i in range(1, orb // 2):
        owners += [owner_of(me, i, sign, orb), owner_of(me, i, -sign, orb)]
    for way in range(orb):
        total = None
        for j in range(slots):
            tiles = [
                packs[way][t * BS : (t + 1) * BS] for t in range(j * per_slot, (j + 1) * per_slot)
            ]
            term = lax.dot_general(
                half_ref[meta_ref[way * slots + j]],
                jnp.concatenate(tiles, axis=1),
                (((1,), (1,)), ((), ())),
                preferred_element_type=jnp.float32,
            )
            total = term if total is None else total + term
        held[owners[way]] = total
    out_ref[...] = jnp.concatenate([held[n] for n in range(orb)], axis=1)


def shards(density, tensor_blocks, pairs, kept):
    full_width = density.shape[1]
    slots = tensor_blocks.shape[2]
    aux_width = tensor_blocks.shape[3]
    orb = lax.axis_size("orb")
    aux = lax.axis_size("aux")
    rows = full_width // LANES * BS
    size = slots * aux_width * BS // LANES * BS
    vmem = pl.BlockSpec(memory_space=pltpu.VMEM)
    smem = pl.BlockSpec(memory_space=pltpu.SMEM)
    hbm = pl.BlockSpec(memory_space=pltpu.HBM)
    params = pltpu.CompilerParams(vmem_limit_bytes=32 * 1024 * 1024)

    def array(height):
        return jax.ShapeDtypeStruct((height, LANES), jnp.bfloat16)

    def shift(x, step, sign):
        perm = [
            (a * orb + o, a * orb + partner(o, step, sign * (1 - 2 * (a % 2)), orb))
            for a in range(aux)
            for o in range(orb)
        ]
        return lax.ppermute(x, ("aux", "orb"), perm)

    full, tail = pl.pallas_call(
        functools.partial(pack_kernel, orb),
        out_shape=[array(size + rows + NOTE), array(rows // 2 + NOTE)],
        in_specs=[smem, hbm, hbm, hbm],
        out_specs=[vmem] * 2,
        scratch_shapes=[
            pltpu.SMEM(pairs.shape, jnp.int32),
            pltpu.VMEM(density.shape, jnp.bfloat16),
            pltpu.VMEM(tensor_blocks.shape, jnp.bfloat16),
            pltpu.SemaphoreType.DMA((3,)),
        ],
        compiler_params=params,
        name="pack",
    )(
        kept,
        *(pltpu.with_memory_space_constraint(a, pltpu.HBM) for a in (pairs, density, tensor_blocks)),
    )
    lean = pl.pallas_call(
        lean_kernel,
        out_shape=array(size + NOTE),
        in_specs=[vmem],
        out_specs=vmem,
        compiler_params=params,
        name="lean",
    )(full)
    across = [(i, (i + orb // 2) % orb) for i in range(orb)]
    raw = lax.ppermute(tensor_blocks, "orb", across)
    tail_in = lax.ppermute(tail, "orb", across)
    fulls = [shift(full, i, 1) for i in range(1, orb // 2)]
    leans = [shift(lean, i, -1) for i in range(1, orb // 2)]

    tail_in, raw = lax.optimization_barrier((tail_in, raw))
    merged = pl.pallas_call(
        functools.partial(merge_kernel, size),
        out_shape=array(len(fulls) * rows + rows // 2),
        in_specs=[vmem] * (len(fulls) + 1),
        out_specs=vmem,
        compiler_params=params,
        name="merge",
    )(*fulls, tail_in)
    swapped = lax.ppermute(merged, "aux", [(i, i ^ 1) for i in range(aux)])
    across = pl.pallas_call(
        relay_kernel,
        out_shape=array(size),
        in_specs=[vmem],
        out_specs=vmem,
        compiler_params=params,
        name="relay",
    )(raw)
    half = pl.pallas_call(
        functools.partial(half_kernel, orb, slots, aux_width),
        out_shape=jax.ShapeDtypeStruct((orb + 1, BS, aux_width * BS), jnp.bfloat16),
        in_specs=[smem] + [vmem] * (len(fulls) + 4),
        out_specs=vmem,
        scratch_shapes=[pltpu.VMEM((orb + 1, BS, full_width), jnp.bfloat16)],
        compiler_params=params,
        name="half",
    )(tail[-NOTE, :slots].astype(jnp.int32), density, full, *fulls, tail_in, swapped)
    half, leans = lax.optimization_barrier((half, leans))
    packs, notes = [full, across], [tail, tail_in]
    for pair in zip(fulls, leans):
        packs += pair
        notes += pair
    codes = jnp.concatenate([n[-NOTE, :slots] for n in notes]).astype(jnp.int32)
    parts = pl.pallas_call(
        functools.partial(exchange_kernel, orb, slots, aux_width),
        out_shape=jax.ShapeDtypeStruct((BS, full_width), jnp.float32),
        in_specs=[smem] + [vmem] * (orb + 1),
        out_specs=vmem,
        scratch_shapes=[pltpu.VMEM((orb, BS, BS), jnp.float32)],
        compiler_params=params,
        name="exchange",
    )(codes, half, *packs)

    step = 1
    while step < aux:
        ways = 2 if step == 1 or step * 4 > aux else 4
        terms = [parts]
        for way in range(1, ways):
            terms.append(lax.ppermute(parts, "aux", [(i, i ^ (way * step)) for i in range(aux)]))
        while len(terms) > 1:
            terms = [terms[i] + terms[i + 1] for i in range(0, len(terms), 2)]
        parts = terms[0]
        step *= ways
    return parts


def solution(mesh):
    return jax.shard_map(
        shards,
        mesh=mesh,
        in_specs=(
            P("orb", None),
            P("orb", "aux", None, None, None),
            P("orb", "aux", None),
            P("orb", "aux"),
        ),
        out_specs=P("orb", None),
        check_vma=False,
    )
```

```python
import functools

import jax
import jax.numpy as jnp
from jax import lax
from jax.experimental import pallas as pl
from jax.experimental.pallas import tpu as pltpu
from jax.sharding import PartitionSpec as P

BS = 64
LANES = 128
NOTE = 16


def lay_blocks(raw, out_ref):
    slots, aux_width = raw.shape[:2]
    square = raw.reshape(slots * aux_width, BS, BS)
    for tile in range(slots * aux_width // 2):
        both = jnp.concatenate([square[2 * tile], square[2 * tile + 1]], axis=1)
        out_ref[tile * BS : (tile + 1) * BS] = both
    return slots * aux_width // 2


def partner(i, step, sign, orb):
    if orb == 4:
        return i ^ (2 - sign)
    return (i + sign * step) % orb


def owner_of(me, step, sign, orb):
    if orb == 4:
        return me ^ (2 - sign)
    return lax.rem(me - sign * step + orb, orb)


def core_parity():
    return lax.rem(lax.axis_index("aux"), 2)


def pack_kernel(
    orb, kept, pairs_hbm, density_hbm, raw_hbm, full_ref, tail_ref, pairs, rows, raw, sems
):
    copies = [
        pltpu.make_async_copy(src, dst, sems.at[i])
        for i, (src, dst) in enumerate(((raw_hbm, raw), (density_hbm, rows), (pairs_hbm, pairs)))
    ]
    for copy in copies:
        copy.start()
    for copy in copies[1:]:
        copy.wait()
    height = BS // 2
    near = pl.multiple_of(core_parity() * height, height)
    tiles = rows.shape[1] // LANES
    size = full_ref.shape[0] - tiles * BS - NOTE
    for t in range(tiles):
        lanes = slice(t * LANES, (t + 1) * LANES)
        full_ref[size + t * BS : size + (t + 1) * BS] = rows[:, lanes]
        tail_ref[t * height : (t + 1) * height] = rows[pl.ds(near, height), lanes]
    shape = (NOTE, LANES)
    lane = lax.broadcasted_iota(jnp.int32, shape, 1)
    note = jnp.zeros(shape, jnp.int32)
    for j in range(pairs.shape[2]):
        note = jnp.where(lane == j, jnp.where(j < kept[0, 0], pairs[0, 0, j], orb), note)
    note = note.astype(jnp.float32).astype(jnp.bfloat16)
    full_ref[size + tiles * BS :] = note
    tail_ref[tiles * height :] = note
    copies[0].wait()
    lay_blocks(raw[0, 0], full_ref)


def lean_kernel(full_ref, out_ref):
    size = out_ref.shape[0] - NOTE
    out_ref[:size] = full_ref[:size]
    out_ref[size:] = full_ref[full_ref.shape[0] - NOTE :]


def relay_kernel(slots, aux_width, raw, full_ref, out_ref, left_ref):
    lay_blocks(raw[0, 0], out_ref)
    size = out_ref.shape[0]
    own = jnp.concatenate([full_ref[at : at + BS] for at in range(0, size, BS)], axis=1)
    for p in range(aux_width):
        cuts = [(j * aux_width + p) * BS for j in range(slots)]
        left_ref[p * BS : (p + 1) * BS] = jnp.concatenate(
            [own[:, cut : cut + BS] for cut in cuts], axis=1
        )


def merge_kernel(size, *refs):
    parts, out_ref = refs[:-1], refs[-1]
    at = 0
    for i, part in enumerate(parts):
        first = size if i < len(parts) - 1 else 0
        count = part.shape[0] - NOTE - first
        out_ref[at : at + count] = part[first : first + count]
        at += count


def exchange_kernel(
    orb, slots, aux_width, meta_ref, density_ref, left_ref, tail, swapped, *refs
):
    packs, (out_ref, rows, half_ref, held) = refs[:orb], refs[orb:]
    fulls = packs[2::2]
    me = lax.axis_index("orb")
    parity = core_parity()
    sign = 1 - 2 * parity
    height = BS // 2
    count = density_ref.shape[1] // LANES
    size = slots * aux_width * BS // LANES * BS
    near = pl.multiple_of(parity * height, height)
    far = pl.multiple_of((1 - parity) * height, height)
    across = lax.rem(me + orb // 2, orb)
    owners = [me, across]
    rows[me] = density_ref[...]
    for i, full in enumerate(fulls):
        owners += [owner_of(me, i + 1, sign, orb), owner_of(me, i + 1, -sign, orb)]
        for t in range(count):
            lanes = slice(t * LANES, (t + 1) * LANES)
            at = (i * count + t) * BS
            rows[owners[-2], :, lanes] = full[size + t * BS : size + (t + 1) * BS]
            rows[owners[-1], :, lanes] = swapped[at : at + BS]
    for t in range(count):
        lanes = slice(t * LANES, (t + 1) * LANES)
        at = len(fulls) * count * BS + t * height
        rows[across, pl.ds(near, height), lanes] = tail[t * height : (t + 1) * height]
        rows[across, pl.ds(far, height), lanes] = swapped[at : at + height]
    rows[orb] = jnp.zeros_like(rows[orb])
    selected = jnp.concatenate([rows[meta_ref[j]] for j in range(slots)], axis=0)
    half = jnp.dot(left_ref[...], selected, preferred_element_type=jnp.float32)
    half = half.astype(jnp.bfloat16)
    for k in range(orb):
        half_ref[k] = jnp.concatenate(
            [half[p * BS : (p + 1) * BS, k * BS : (k + 1) * BS] for p in range(aux_width)],
            axis=1,
        )
    half_ref[orb] = jnp.zeros_like(half_ref[orb])
    for way in range(orb):
        codes = [meta_ref[way * slots + j] for j in range(slots)]
        held[owners[way]] = lax.dot_general(
            jnp.concatenate([half_ref[code] for code in codes], axis=1),
            jnp.concatenate([packs[way][at : at + BS] for at in range(0, size, BS)], axis=1),
            (((1,), (1,)), ((), ())),
            preferred_element_type=jnp.float32,
        )
    out_ref[...] = jnp.concatenate([held[n] for n in range(orb)], axis=1)


def shards(density, tensor_blocks, pairs, kept):
    full_width = density.shape[1]
    slots = tensor_blocks.shape[2]
    aux_width = tensor_blocks.shape[3]
    orb = lax.axis_size("orb")
    aux = lax.axis_size("aux")
    rows = full_width // LANES * BS
    size = slots * aux_width * BS // LANES * BS
    vmem = pl.BlockSpec(memory_space=pltpu.VMEM)
    smem = pl.BlockSpec(memory_space=pltpu.SMEM)
    hbm = pl.BlockSpec(memory_space=pltpu.HBM)
    params = pltpu.CompilerParams(vmem_limit_bytes=32 * 1024 * 1024)

    def array(height):
        return jax.ShapeDtypeStruct((height, LANES), jnp.bfloat16)

    def shift(x, step, sign):
        perm = [
            (a * orb + o, a * orb + partner(o, step, sign * (1 - 2 * (a % 2)), orb))
            for a in range(aux)
            for o in range(orb)
        ]
        return lax.ppermute(x, ("aux", "orb"), perm)

    full, tail = pl.pallas_call(
        functools.partial(pack_kernel, orb),
        out_shape=[array(size + rows + NOTE), array(rows // 2 + NOTE)],
        in_specs=[smem, hbm, hbm, hbm],
        out_specs=[vmem] * 2,
        scratch_shapes=[
            pltpu.SMEM(pairs.shape, jnp.int32),
            pltpu.VMEM(density.shape, jnp.bfloat16),
            pltpu.VMEM(tensor_blocks.shape, jnp.bfloat16),
            pltpu.SemaphoreType.DMA((3,)),
        ],
        compiler_params=params,
        name="pack",
    )(
        kept,
        *(pltpu.with_memory_space_constraint(a, pltpu.HBM) for a in (pairs, density, tensor_blocks)),
    )
    lean = pl.pallas_call(
        lean_kernel,
        out_shape=array(size + NOTE),
        in_specs=[vmem],
        out_specs=vmem,
        compiler_params=params,
        name="lean",
    )(full)
    across = [(i, (i + orb // 2) % orb) for i in range(orb)]
    raw = lax.ppermute(tensor_blocks, "orb", across)
    tail_in = lax.ppermute(tail, "orb", across)
    fulls = [shift(full, i, 1) for i in range(1, orb // 2)]
    leans = [shift(lean, i, -1) for i in range(1, orb // 2)]

    tail_in, raw = lax.optimization_barrier((tail_in, raw))
    merged = pl.pallas_call(
        functools.partial(merge_kernel, size),
        out_shape=array(len(fulls) * rows + rows // 2),
        in_specs=[vmem] * (len(fulls) + 1),
        out_specs=vmem,
        compiler_params=params,
        name="merge",
    )(*fulls, tail_in)
    swapped = lax.ppermute(merged, "aux", [(i, i ^ 1) for i in range(aux)])
    across, left = pl.pallas_call(
        functools.partial(relay_kernel, slots, aux_width),
        out_shape=[
            array(size),
            jax.ShapeDtypeStruct((aux_width * BS, slots * BS), jnp.bfloat16),
        ],
        in_specs=[vmem] * 2,
        out_specs=[vmem] * 2,
        compiler_params=params,
        name="relay",
    )(raw, full)
    swapped, leans = lax.optimization_barrier((swapped, leans))
    packs, notes = [full, across], [tail, tail_in]
    for pair in zip(fulls, leans):
        packs += pair
        notes += pair
    codes = jnp.concatenate([n[-NOTE, :slots] for n in notes]).astype(jnp.int32)
    parts = pl.pallas_call(
        functools.partial(exchange_kernel, orb, slots, aux_width),
        out_shape=jax.ShapeDtypeStruct((BS, full_width), jnp.float32),
        in_specs=[smem] + [vmem] * (orb + 4),
        out_specs=vmem,
        scratch_shapes=[
            pltpu.VMEM((orb + 1, BS, full_width), jnp.bfloat16),
            pltpu.VMEM((orb + 1, BS, aux_width * BS), jnp.bfloat16),
            pltpu.VMEM((orb, BS, BS), jnp.float32),
        ],
        compiler_params=params,
        name="exchange",
    )(codes, density, left, tail_in, swapped, *packs)

    step = 1
    while step < aux:
        ways = 2 if step == 1 or step * 4 > aux else 4
        terms = [parts]
        for way in range(1, ways):
            terms.append(lax.ppermute(parts, "aux", [(i, i ^ (way * step)) for i in range(aux)]))
        while len(terms) > 1:
            terms = [terms[i] + terms[i + 1] for i in range(0, len(terms), 2)]
        parts = terms[0]
        step *= ways
    return parts


def solution(mesh):
    return jax.shard_map(
        shards,
        mesh=mesh,
        in_specs=(
            P("orb", None),
            P("orb", "aux", None, None, None),
            P("orb", "aux", None),
            P("orb", "aux"),
        ),
        out_specs=P("orb", None),
        check_vma=False,
    )
```

```python
import functools

import jax
import jax.numpy as jnp
from jax import lax
from jax.experimental import pallas as pl
from jax.experimental.pallas import tpu as pltpu
from jax.sharding import PartitionSpec as P

BS = 64
LANES = 128
NOTE = 8


def lay_blocks(raw, out_ref):
    slots, aux_width = raw.shape[:2]
    square = raw.reshape(slots * aux_width, BS, BS)
    for tile in range(slots * aux_width // 2):
        both = jnp.concatenate([square[2 * tile], square[2 * tile + 1]], axis=1)
        out_ref[tile * BS : (tile + 1) * BS] = both
    return slots * aux_width // 2


def partner(i, step, sign, orb):
    if orb == 4:
        return i ^ (2 - sign)
    return (i + sign * step) % orb


def owner_of(me, step, sign, orb):
    if orb == 4:
        return me ^ (2 - sign)
    return lax.rem(me - sign * step + orb, orb)


def core_parity():
    return lax.rem(lax.axis_index("aux"), 2)


def pack_kernel(
    orb, kept, pairs_hbm, density_hbm, raw_hbm, full_ref, tail_ref, pairs, rows, raw, sems
):
    copies = [
        pltpu.make_async_copy(src, dst, sems.at[i])
        for i, (src, dst) in enumerate(((raw_hbm, raw), (density_hbm, rows), (pairs_hbm, pairs)))
    ]
    for copy in copies:
        copy.start()
    for copy in copies[1:]:
        copy.wait()
    height = BS // 2
    near = pl.multiple_of(core_parity() * height, height)
    tiles = rows.shape[1] // LANES
    size = full_ref.shape[0] - tiles * BS - NOTE
    for t in range(tiles):
        lanes = slice(t * LANES, (t + 1) * LANES)
        full_ref[size + t * BS : size + (t + 1) * BS] = rows[:, lanes]
        tail_ref[t * height : (t + 1) * height] = rows[pl.ds(near, height), lanes]
    shape = (NOTE, LANES)
    lane = lax.broadcasted_iota(jnp.int32, shape, 1)
    note = jnp.zeros(shape, jnp.int32)
    for j in range(pairs.shape[2]):
        note = jnp.where(lane == j, jnp.where(j < kept[0, 0], pairs[0, 0, j], orb), note)
    note = note.astype(jnp.float32).astype(jnp.bfloat16)
    full_ref[size + tiles * BS :] = note
    tail_ref[tiles * height :] = note
    copies[0].wait()
    lay_blocks(raw[0, 0], full_ref)


def lean_kernel(full_ref, out_ref):
    size = out_ref.shape[0] - NOTE
    out_ref[:size] = full_ref[:size]
    out_ref[size:] = full_ref[full_ref.shape[0] - NOTE :]


def relay_kernel(slots, aux_width, raw, full_ref, out_ref, left_ref):
    lay_blocks(raw[0, 0], out_ref)
    size = out_ref.shape[0]
    own = jnp.concatenate([full_ref[at : at + BS] for at in range(0, size, BS)], axis=1)
    for p in range(aux_width):
        cuts = [(j * aux_width + p) * BS for j in range(slots)]
        left_ref[p * BS : (p + 1) * BS] = jnp.concatenate(
            [own[:, cut : cut + BS] for cut in cuts], axis=1
        )


def merge_kernel(size, *refs):
    parts, out_ref = refs[:-1], refs[-1]
    at = 0
    for i, part in enumerate(parts):
        first = size if i < len(parts) - 1 else 0
        count = part.shape[0] - NOTE - first
        out_ref[at : at + count] = part[first : first + count]
        at += count


def exchange_kernel(
    orb, slots, aux_width, meta_ref, density_ref, left_ref, tail, swapped, *refs
):
    packs, (out_ref, rows, half_ref, held) = refs[:orb], refs[orb:]
    fulls = packs[2::2]
    me = lax.axis_index("orb")
    parity = core_parity()
    sign = 1 - 2 * parity
    height = BS // 2
    count = density_ref.shape[1] // LANES
    size = slots * aux_width * BS // LANES * BS
    near = pl.multiple_of(parity * height, height)
    far = pl.multiple_of((1 - parity) * height, height)
    across = lax.rem(me + orb // 2, orb)
    owners = [me, across]
    rows[me] = density_ref[...]
    for i, full in enumerate(fulls):
        owners += [owner_of(me, i + 1, sign, orb), owner_of(me, i + 1, -sign, orb)]
        for t in range(count):
            lanes = slice(t * LANES, (t + 1) * LANES)
            at = (i * count + t) * BS
            rows[owners[-2], :, lanes] = full[size + t * BS : size + (t + 1) * BS]
            rows[owners[-1], :, lanes] = swapped[at : at + BS]
    for t in range(count):
        lanes = slice(t * LANES, (t + 1) * LANES)
        at = len(fulls) * count * BS + t * height
        rows[across, pl.ds(near, height), lanes] = tail[t * height : (t + 1) * height]
        rows[across, pl.ds(far, height), lanes] = swapped[at : at + height]
    rows[orb] = jnp.zeros_like(rows[orb])
    selected = jnp.concatenate([rows[meta_ref[j]] for j in range(slots)], axis=0)
    half = jnp.dot(left_ref[...], selected, preferred_element_type=jnp.float32)
    half = half.astype(jnp.bfloat16)
    for k in range(orb):
        half_ref[k] = jnp.concatenate(
            [half[p * BS : (p + 1) * BS, k * BS : (k + 1) * BS] for p in range(aux_width)],
            axis=1,
        )
    half_ref[orb] = jnp.zeros_like(half_ref[orb])
    for way in range(orb):
        codes = [meta_ref[way * slots + j] for j in range(slots)]
        held[owners[way]] = lax.dot_general(
            jnp.concatenate([half_ref[code] for code in codes], axis=1),
            jnp.concatenate([packs[way][at : at + BS] for at in range(0, size, BS)], axis=1),
            (((1,), (1,)), ((), ())),
            preferred_element_type=jnp.float32,
        )
    out_ref[...] = jnp.concatenate([held[n] for n in range(orb)], axis=1)


def shards(density, tensor_blocks, pairs, kept):
    full_width = density.shape[1]
    slots = tensor_blocks.shape[2]
    aux_width = tensor_blocks.shape[3]
    orb = lax.axis_size("orb")
    aux = lax.axis_size("aux")
    rows = full_width // LANES * BS
    size = slots * aux_width * BS // LANES * BS
    vmem = pl.BlockSpec(memory_space=pltpu.VMEM)
    smem = pl.BlockSpec(memory_space=pltpu.SMEM)
    hbm = pl.BlockSpec(memory_space=pltpu.HBM)
    params = pltpu.CompilerParams(vmem_limit_bytes=32 * 1024 * 1024)

    def array(height):
        return jax.ShapeDtypeStruct((height, LANES), jnp.bfloat16)

    def shift(x, step, sign):
        perm = [
            (a * orb + o, a * orb + partner(o, step, sign * (1 - 2 * (a % 2)), orb))
            for a in range(aux)
            for o in range(orb)
        ]
        return lax.ppermute(x, ("aux", "orb"), perm)

    full, tail = pl.pallas_call(
        functools.partial(pack_kernel, orb),
        out_shape=[array(size + rows + NOTE), array(rows // 2 + NOTE)],
        in_specs=[smem, hbm, hbm, hbm],
        out_specs=[vmem] * 2,
        scratch_shapes=[
            pltpu.SMEM(pairs.shape, jnp.int32),
            pltpu.VMEM(density.shape, jnp.bfloat16),
            pltpu.VMEM(tensor_blocks.shape, jnp.bfloat16),
            pltpu.SemaphoreType.DMA((3,)),
        ],
        compiler_params=params,
        name="pack",
    )(
        kept,
        *(pltpu.with_memory_space_constraint(a, pltpu.HBM) for a in (pairs, density, tensor_blocks)),
    )
    lean = pl.pallas_call(
        lean_kernel,
        out_shape=array(size + NOTE),
        in_specs=[vmem],
        out_specs=vmem,
        compiler_params=params,
        name="lean",
    )(full)
    across = [(i, (i + orb // 2) % orb) for i in range(orb)]
    raw = lax.ppermute(tensor_blocks, "orb", across)
    tail_in = lax.ppermute(tail, "orb", across)
    fulls = [shift(full, i, 1) for i in range(1, orb // 2)]
    leans = [shift(lean, i, -1) for i in range(1, orb // 2)]

    tail_in, raw = lax.optimization_barrier((tail_in, raw))
    merged = pl.pallas_call(
        functools.partial(merge_kernel, size),
        out_shape=array(len(fulls) * rows + rows // 2),
        in_specs=[vmem] * (len(fulls) + 1),
        out_specs=vmem,
        compiler_params=params,
        name="merge",
    )(*fulls, tail_in)
    swapped = lax.ppermute(merged, "aux", [(i, i ^ 1) for i in range(aux)])
    across, left = pl.pallas_call(
        functools.partial(relay_kernel, slots, aux_width),
        out_shape=[
            array(size),
            jax.ShapeDtypeStruct((aux_width * BS, slots * BS), jnp.bfloat16),
        ],
        in_specs=[vmem] * 2,
        out_specs=[vmem] * 2,
        compiler_params=params,
        name="relay",
    )(raw, full)
    swapped, leans = lax.optimization_barrier((swapped, leans))
    packs, notes = [full, across], [tail, tail_in]
    for pair in zip(fulls, leans):
        packs += pair
        notes += pair
    codes = jnp.concatenate([n[-NOTE, :slots] for n in notes]).astype(jnp.int32)
    parts = pl.pallas_call(
        functools.partial(exchange_kernel, orb, slots, aux_width),
        out_shape=jax.ShapeDtypeStruct((BS, full_width), jnp.float32),
        in_specs=[smem] + [vmem] * (orb + 4),
        out_specs=vmem,
        scratch_shapes=[
            pltpu.VMEM((orb + 1, BS, full_width), jnp.bfloat16),
            pltpu.VMEM((orb + 1, BS, aux_width * BS), jnp.bfloat16),
            pltpu.VMEM((orb, BS, BS), jnp.float32),
        ],
        compiler_params=params,
        name="exchange",
    )(codes, density, left, tail_in, swapped, *packs)

    step = 1
    while step < aux:
        ways = 2 if step == 1 or step * 4 > aux else 4
        terms = [parts]
        for way in range(1, ways):
            terms.append(lax.ppermute(parts, "aux", [(i, i ^ (way * step)) for i in range(aux)]))
        while len(terms) > 1:
            terms = [terms[i] + terms[i + 1] for i in range(0, len(terms), 2)]
        parts = terms[0]
        step *= ways
    return parts


def solution(mesh):
    return jax.shard_map(
        shards,
        mesh=mesh,
        in_specs=(
            P("orb", None),
            P("orb", "aux", None, None, None),
            P("orb", "aux", None),
            P("orb", "aux"),
        ),
        out_specs=P("orb", None),
        check_vma=False,
    )
```

```python
import functools

import jax
import jax.numpy as jnp
from jax import lax
from jax.experimental import pallas as pl
from jax.experimental.pallas import tpu as pltpu
from jax.sharding import PartitionSpec as P

BS = 64
LANES = 128
NOTE = 8


def lay_blocks(raw, out_ref):
    slots, aux_width = raw.shape[:2]
    square = raw.reshape(slots * aux_width, BS, BS)
    for tile in range(slots * aux_width // 2):
        both = jnp.concatenate([square[2 * tile], square[2 * tile + 1]], axis=1)
        out_ref[tile * BS : (tile + 1) * BS] = both
    return slots * aux_width // 2


def partner(i, step, sign, orb):
    if orb == 4:
        return i ^ (2 - sign)
    return (i + sign * step) % orb


def owner_of(me, step, sign, orb):
    if orb == 4:
        return me ^ (2 - sign)
    return lax.rem(me - sign * step + orb, orb)


def core_parity():
    return lax.rem(lax.axis_index("aux"), 2)


def pack_kernel(
    orb, kept, pairs_hbm, density_hbm, raw_hbm, full_ref, pairs, rows, raw, sems
):
    copies = [
        pltpu.make_async_copy(src, dst, sems.at[i])
        for i, (src, dst) in enumerate(((raw_hbm, raw), (density_hbm, rows), (pairs_hbm, pairs)))
    ]
    for copy in copies:
        copy.start()
    for copy in copies[1:]:
        copy.wait()
    tiles = rows.shape[1] // LANES
    size = full_ref.shape[0] - tiles * BS - NOTE
    for t in range(tiles):
        lanes = slice(t * LANES, (t + 1) * LANES)
        full_ref[size + t * BS : size + (t + 1) * BS] = rows[:, lanes]
    shape = (NOTE, LANES)
    lane = lax.broadcasted_iota(jnp.int32, shape, 1)
    note = jnp.zeros(shape, jnp.int32)
    for j in range(pairs.shape[2]):
        note = jnp.where(lane == j, jnp.where(j < kept[0, 0], pairs[0, 0, j], orb), note)
    full_ref[size + tiles * BS :] = note.astype(jnp.float32).astype(jnp.bfloat16)
    copies[0].wait()
    lay_blocks(raw[0, 0], full_ref)


def tail_kernel(size, full_ref, out_ref):
    height = BS // 2
    tiles = (out_ref.shape[0] - NOTE) // height
    for t in range(tiles):
        first = pl.multiple_of(size + t * BS + core_parity() * height, height)
        out_ref[t * height : (t + 1) * height] = full_ref[pl.ds(first, height)]
    out_ref[tiles * height :] = full_ref[full_ref.shape[0] - NOTE :]


def lean_kernel(full_ref, tail_ref, out_ref):
    size = out_ref.shape[0] - NOTE
    out_ref[:size] = full_ref[:size]
    out_ref[size:] = tail_ref[tail_ref.shape[0] - NOTE :]


def relay_kernel(slots, aux_width, raw, full_ref, out_ref, left_ref):
    lay_blocks(raw[0, 0], out_ref)
    size = out_ref.shape[0]
    own = jnp.concatenate([full_ref[at : at + BS] for at in range(0, size, BS)], axis=1)
    for p in range(aux_width):
        cuts = [(j * aux_width + p) * BS for j in range(slots)]
        left_ref[p * BS : (p + 1) * BS] = jnp.concatenate(
            [own[:, cut : cut + BS] for cut in cuts], axis=1
        )


def merge_kernel(size, *refs):
    parts, out_ref = refs[:-1], refs[-1]
    at = 0
    for i, part in enumerate(parts):
        first = size if i < len(parts) - 1 else 0
        count = part.shape[0] - NOTE - first
        out_ref[at : at + count] = part[first : first + count]
        at += count


def exchange_kernel(
    orb, slots, aux_width, meta_ref, density_ref, left_ref, tail, swapped, *refs
):
    packs, (out_ref, rows, half_ref, held) = refs[:orb], refs[orb:]
    fulls = packs[2::2]
    me = lax.axis_index("orb")
    parity = core_parity()
    sign = 1 - 2 * parity
    height = BS // 2
    count = density_ref.shape[1] // LANES
    size = slots * aux_width * BS // LANES * BS
    near = pl.multiple_of(parity * height, height)
    far = pl.multiple_of((1 - parity) * height, height)
    across = lax.rem(me + orb // 2, orb)
    owners = [me, across]
    rows[me] = density_ref[...]
    for i, full in enumerate(fulls):
        owners += [owner_of(me, i + 1, sign, orb), owner_of(me, i + 1, -sign, orb)]
        for t in range(count):
            lanes = slice(t * LANES, (t + 1) * LANES)
            at = (i * count + t) * BS
            rows[owners[-2], :, lanes] = full[size + t * BS : size + (t + 1) * BS]
            rows[owners[-1], :, lanes] = swapped[at : at + BS]
    for t in range(count):
        lanes = slice(t * LANES, (t + 1) * LANES)
        at = len(fulls) * count * BS + t * height
        rows[across, pl.ds(near, height), lanes] = tail[t * height : (t + 1) * height]
        rows[across, pl.ds(far, height), lanes] = swapped[at : at + height]
    rows[orb] = jnp.zeros_like(rows[orb])
    selected = jnp.concatenate([rows[meta_ref[j]] for j in range(slots)], axis=0)
    half = jnp.dot(left_ref[...], selected, preferred_element_type=jnp.float32)
    half = half.astype(jnp.bfloat16)
    for k in range(orb):
        half_ref[k] = jnp.concatenate(
            [half[p * BS : (p + 1) * BS, k * BS : (k + 1) * BS] for p in range(aux_width)],
            axis=1,
        )
    half_ref[orb] = jnp.zeros_like(half_ref[orb])
    for way in range(orb):
        codes = [meta_ref[way * slots + j] for j in range(slots)]
        held[owners[way]] = lax.dot_general(
            jnp.concatenate([half_ref[code] for code in codes], axis=1),
            jnp.concatenate([packs[way][at : at + BS] for at in range(0, size, BS)], axis=1),
            (((1,), (1,)), ((), ())),
            preferred_element_type=jnp.float32,
        )
    out_ref[...] = jnp.concatenate([held[n] for n in range(orb)], axis=1)


def shards(density, tensor_blocks, pairs, kept):
    full_width = density.shape[1]
    slots = tensor_blocks.shape[2]
    aux_width = tensor_blocks.shape[3]
    orb = lax.axis_size("orb")
    aux = lax.axis_size("aux")
    rows = full_width // LANES * BS
    size = slots * aux_width * BS // LANES * BS
    vmem = pl.BlockSpec(memory_space=pltpu.VMEM)
    smem = pl.BlockSpec(memory_space=pltpu.SMEM)
    hbm = pl.BlockSpec(memory_space=pltpu.HBM)
    params = pltpu.CompilerParams(vmem_limit_bytes=32 * 1024 * 1024)

    def array(height):
        return jax.ShapeDtypeStruct((height, LANES), jnp.bfloat16)

    def shift(x, step, sign):
        perm = [
            (a * orb + o, a * orb + partner(o, step, sign * (1 - 2 * (a % 2)), orb))
            for a in range(aux)
            for o in range(orb)
        ]
        return lax.ppermute(x, ("aux", "orb"), perm)

    full = pl.pallas_call(
        functools.partial(pack_kernel, orb),
        out_shape=array(size + rows + NOTE),
        in_specs=[smem, hbm, hbm, hbm],
        out_specs=vmem,
        scratch_shapes=[
            pltpu.SMEM(pairs.shape, jnp.int32),
            pltpu.VMEM(density.shape, jnp.bfloat16),
            pltpu.VMEM(tensor_blocks.shape, jnp.bfloat16),
            pltpu.SemaphoreType.DMA((3,)),
        ],
        compiler_params=params,
        name="pack",
    )(
        kept,
        *(pltpu.with_memory_space_constraint(a, pltpu.HBM) for a in (pairs, density, tensor_blocks)),
    )
    tail = pl.pallas_call(
        functools.partial(tail_kernel, size),
        out_shape=array(rows // 2 + NOTE),
        in_specs=[vmem],
        out_specs=vmem,
        compiler_params=params,
        name="tail",
    )(full)
    lean = pl.pallas_call(
        lean_kernel,
        out_shape=array(size + NOTE),
        in_specs=[vmem] * 2,
        out_specs=vmem,
        compiler_params=params,
        name="lean",
    )(full, tail)
    across = [(i, (i + orb // 2) % orb) for i in range(orb)]
    raw = lax.ppermute(tensor_blocks, "orb", across)
    tail_in = lax.ppermute(tail, "orb", across)
    fulls = [shift(full, i, 1) for i in range(1, orb // 2)]
    leans = [shift(lean, i, -1) for i in range(1, orb // 2)]

    tail_in, raw = lax.optimization_barrier((tail_in, raw))
    merged = pl.pallas_call(
        functools.partial(merge_kernel, size),
        out_shape=array(len(fulls) * rows + rows // 2),
        in_specs=[vmem] * (len(fulls) + 1),
        out_specs=vmem,
        compiler_params=params,
        name="merge",
    )(*fulls, tail_in)
    swapped = lax.ppermute(merged, "aux", [(i, i ^ 1) for i in range(aux)])
    across, left = pl.pallas_call(
        functools.partial(relay_kernel, slots, aux_width),
        out_shape=[
            array(size),
            jax.ShapeDtypeStruct((aux_width * BS, slots * BS), jnp.bfloat16),
        ],
        in_specs=[vmem] * 2,
        out_specs=[vmem] * 2,
        compiler_params=params,
        name="relay",
    )(raw, full)
    swapped, leans = lax.optimization_barrier((swapped, leans))
    packs, notes = [full, across], [tail, tail_in]
    for pair in zip(fulls, leans):
        packs += pair
        notes += pair
    codes = jnp.concatenate([n[-NOTE, :slots] for n in notes]).astype(jnp.int32)
    parts = pl.pallas_call(
        functools.partial(exchange_kernel, orb, slots, aux_width),
        out_shape=jax.ShapeDtypeStruct((BS, full_width), jnp.float32),
        in_specs=[smem] + [vmem] * (orb + 4),
        out_specs=vmem,
        scratch_shapes=[
            pltpu.VMEM((orb + 1, BS, full_width), jnp.bfloat16),
            pltpu.VMEM((orb + 1, BS, aux_width * BS), jnp.bfloat16),
            pltpu.VMEM((orb, BS, BS), jnp.float32),
        ],
        compiler_params=params,
        name="exchange",
    )(codes, density, left, tail_in, swapped, *packs)

    step = 1
    while step < aux:
        ways = 2 if step == 1 or step * 4 > aux else 4
        terms = [parts]
        for way in range(1, ways):
            terms.append(lax.ppermute(parts, "aux", [(i, i ^ (way * step)) for i in range(aux)]))
        while len(terms) > 1:
            terms = [terms[i] + terms[i + 1] for i in range(0, len(terms), 2)]
        parts = terms[0]
        step *= ways
    return parts


def solution(mesh):
    return jax.shard_map(
        shards,
        mesh=mesh,
        in_specs=(
            P("orb", None),
            P("orb", "aux", None, None, None),
            P("orb", "aux", None),
            P("orb", "aux"),
        ),
        out_specs=P("orb", None),
        check_vma=False,
    )
```

```python
import functools

import jax
import jax.numpy as jnp
from jax import lax
from jax.experimental import pallas as pl
from jax.experimental.pallas import tpu as pltpu
from jax.sharding import PartitionSpec as P

BS = 64
LANES = 128
NOTE = 8


def lay_blocks(raw, out_ref):
    slots, aux_width = raw.shape[:2]
    square = raw.reshape(slots * aux_width, BS, BS)
    for tile in range(slots * aux_width // 2):
        both = jnp.concatenate([square[2 * tile], square[2 * tile + 1]], axis=1)
        out_ref[tile * BS : (tile + 1) * BS] = both
    return slots * aux_width // 2


def partner(i, step, sign, orb):
    if orb == 4:
        return i ^ (2 - sign)
    return (i + sign * step) % orb


def owner_of(me, step, sign, orb):
    if orb == 4:
        return me ^ (2 - sign)
    return lax.rem(me - sign * step + orb, orb)


def core_parity():
    return lax.rem(lax.axis_index("aux"), 2)


def pack_kernel(
    orb, kept, pairs_hbm, density_hbm, raw_hbm, full_ref, pairs, rows, raw, sems
):
    copies = [
        pltpu.make_async_copy(src, dst, sems.at[i])
        for i, (src, dst) in enumerate(((raw_hbm, raw), (density_hbm, rows), (pairs_hbm, pairs)))
    ]
    for copy in copies:
        copy.start()
    for copy in copies[1:]:
        copy.wait()
    tiles = rows.shape[1] // LANES
    size = full_ref.shape[0] - tiles * BS - NOTE
    for t in range(tiles):
        lanes = slice(t * LANES, (t + 1) * LANES)
        full_ref[size + t * BS : size + (t + 1) * BS] = rows[:, lanes]
    shape = (NOTE, LANES)
    lane = lax.broadcasted_iota(jnp.int32, shape, 1)
    note = jnp.zeros(shape, jnp.int32)
    for j in range(pairs.shape[2]):
        note = jnp.where(lane == j, jnp.where(j < kept[0, 0], pairs[0, 0, j], orb), note)
    full_ref[size + tiles * BS :] = note.astype(jnp.float32).astype(jnp.bfloat16)
    copies[0].wait()
    lay_blocks(raw[0, 0], full_ref)


def lean_kernel(full_ref, out_ref):
    size = out_ref.shape[0] - NOTE
    out_ref[:size] = full_ref[:size]
    out_ref[size:] = full_ref[full_ref.shape[0] - NOTE :]


def tail_kernel(full_ref, lean_ref, out_ref):
    height = BS // 2
    size = lean_ref.shape[0] - NOTE
    tiles = (out_ref.shape[0] - NOTE) // height
    for t in range(tiles):
        first = pl.multiple_of(size + t * BS + core_parity() * height, height)
        out_ref[t * height : (t + 1) * height] = full_ref[pl.ds(first, height)]
    out_ref[tiles * height :] = lean_ref[size:]


def relay_kernel(slots, aux_width, raw, full_ref, out_ref, left_ref):
    lay_blocks(raw[0, 0], out_ref)
    size = out_ref.shape[0]
    own = jnp.concatenate([full_ref[at : at + BS] for at in range(0, size, BS)], axis=1)
    for p in range(aux_width):
        cuts = [(j * aux_width + p) * BS for j in range(slots)]
        left_ref[p * BS : (p + 1) * BS] = jnp.concatenate(
            [own[:, cut : cut + BS] for cut in cuts], axis=1
        )


def merge_kernel(size, *refs):
    parts, out_ref = refs[:-1], refs[-1]
    at = 0
    for i, part in enumerate(parts):
        first = size if i < len(parts) - 1 else 0
        count = part.shape[0] - NOTE - first
        out_ref[at : at + count] = part[first : first + count]
        at += count


def exchange_kernel(
    orb, slots, aux_width, meta_ref, density_ref, left_ref, tail, swapped, *refs
):
    packs, (out_ref, rows, half_ref, held) = refs[:orb], refs[orb:]
    fulls = packs[2::2]
    me = lax.axis_index("orb")
    parity = core_parity()
    sign = 1 - 2 * parity
    height = BS // 2
    count = density_ref.shape[1] // LANES
    size = slots * aux_width * BS // LANES * BS
    near = pl.multiple_of(parity * height, height)
    far = pl.multiple_of((1 - parity) * height, height)
    across = lax.rem(me + orb // 2, orb)
    owners = [me, across]
    rows[me] = density_ref[...]
    for i, full in enumerate(fulls):
        owners += [owner_of(me, i + 1, sign, orb), owner_of(me, i + 1, -sign, orb)]
        for t in range(count):
            lanes = slice(t * LANES, (t + 1) * LANES)
            at = (i * count + t) * BS
            rows[owners[-2], :, lanes] = full[size + t * BS : size + (t + 1) * BS]
            rows[owners[-1], :, lanes] = swapped[at : at + BS]
    for t in range(count):
        lanes = slice(t * LANES, (t + 1) * LANES)
        at = len(fulls) * count * BS + t * height
        rows[across, pl.ds(near, height), lanes] = tail[t * height : (t + 1) * height]
        rows[across, pl.ds(far, height), lanes] = swapped[at : at + height]
    rows[orb] = jnp.zeros_like(rows[orb])
    selected = jnp.concatenate([rows[meta_ref[j]] for j in range(slots)], axis=0)
    half = jnp.dot(left_ref[...], selected, preferred_element_type=jnp.float32)
    half = half.astype(jnp.bfloat16)
    for k in range(orb):
        half_ref[k] = jnp.concatenate(
            [half[p * BS : (p + 1) * BS, k * BS : (k + 1) * BS] for p in range(aux_width)],
            axis=1,
        )
    half_ref[orb] = jnp.zeros_like(half_ref[orb])
    for way in range(orb):
        codes = [meta_ref[way * slots + j] for j in range(slots)]
        held[owners[way]] = lax.dot_general(
            jnp.concatenate([half_ref[code] for code in codes], axis=1),
            jnp.concatenate([packs[way][at : at + BS] for at in range(0, size, BS)], axis=1),
            (((1,), (1,)), ((), ())),
            preferred_element_type=jnp.float32,
        )
    out_ref[...] = jnp.concatenate([held[n] for n in range(orb)], axis=1)


def shards(density, tensor_blocks, pairs, kept):
    full_width = density.shape[1]
    slots = tensor_blocks.shape[2]
    aux_width = tensor_blocks.shape[3]
    orb = lax.axis_size("orb")
    aux = lax.axis_size("aux")
    rows = full_width // LANES * BS
    size = slots * aux_width * BS // LANES * BS
    vmem = pl.BlockSpec(memory_space=pltpu.VMEM)
    smem = pl.BlockSpec(memory_space=pltpu.SMEM)
    hbm = pl.BlockSpec(memory_space=pltpu.HBM)
    params = pltpu.CompilerParams(vmem_limit_bytes=32 * 1024 * 1024)

    def array(height):
        return jax.ShapeDtypeStruct((height, LANES), jnp.bfloat16)

    def shift(x, step, sign):
        perm = [
            (a * orb + o, a * orb + partner(o, step, sign * (1 - 2 * (a % 2)), orb))
            for a in range(aux)
            for o in range(orb)
        ]
        return lax.ppermute(x, ("aux", "orb"), perm)

    full = pl.pallas_call(
        functools.partial(pack_kernel, orb),
        out_shape=array(size + rows + NOTE),
        in_specs=[smem, hbm, hbm, hbm],
        out_specs=vmem,
        scratch_shapes=[
            pltpu.SMEM(pairs.shape, jnp.int32),
            pltpu.VMEM(density.shape, jnp.bfloat16),
            pltpu.VMEM(tensor_blocks.shape, jnp.bfloat16),
            pltpu.SemaphoreType.DMA((3,)),
        ],
        compiler_params=params,
        name="pack",
    )(
        kept,
        *(pltpu.with_memory_space_constraint(a, pltpu.HBM) for a in (pairs, density, tensor_blocks)),
    )
    lean = pl.pallas_call(
        lean_kernel,
        out_shape=array(size + NOTE),
        in_specs=[vmem],
        out_specs=vmem,
        compiler_params=params,
        name="lean",
    )(full)
    tail = pl.pallas_call(
        tail_kernel,
        out_shape=array(rows // 2 + NOTE),
        in_specs=[vmem] * 2,
        out_specs=vmem,
        compiler_params=params,
        name="tail",
    )(full, lean)
    across = [(i, (i + orb // 2) % orb) for i in range(orb)]
    raw = lax.ppermute(tensor_blocks, "orb", across)
    tail_in = lax.ppermute(tail, "orb", across)
    fulls = [shift(full, i, 1) for i in range(1, orb // 2)]
    leans = [shift(lean, i, -1) for i in range(1, orb // 2)]

    tail_in, raw = lax.optimization_barrier((tail_in, raw))
    merged = pl.pallas_call(
        functools.partial(merge_kernel, size),
        out_shape=array(len(fulls) * rows + rows // 2),
        in_specs=[vmem] * (len(fulls) + 1),
        out_specs=vmem,
        compiler_params=params,
        name="merge",
    )(*fulls, tail_in)
    swapped = lax.ppermute(merged, "aux", [(i, i ^ 1) for i in range(aux)])
    across, left = pl.pallas_call(
        functools.partial(relay_kernel, slots, aux_width),
        out_shape=[
            array(size),
            jax.ShapeDtypeStruct((aux_width * BS, slots * BS), jnp.bfloat16),
        ],
        in_specs=[vmem] * 2,
        out_specs=[vmem] * 2,
        compiler_params=params,
        name="relay",
    )(raw, full)
    swapped, leans = lax.optimization_barrier((swapped, leans))
    packs, notes = [full, across], [tail, tail_in]
    for pair in zip(fulls, leans):
        packs += pair
        notes += pair
    codes = jnp.concatenate([n[-NOTE, :slots] for n in notes]).astype(jnp.int32)
    parts = pl.pallas_call(
        functools.partial(exchange_kernel, orb, slots, aux_width),
        out_shape=jax.ShapeDtypeStruct((BS, full_width), jnp.float32),
        in_specs=[smem] + [vmem] * (orb + 4),
        out_specs=vmem,
        scratch_shapes=[
            pltpu.VMEM((orb + 1, BS, full_width), jnp.bfloat16),
            pltpu.VMEM((orb + 1, BS, aux_width * BS), jnp.bfloat16),
            pltpu.VMEM((orb, BS, BS), jnp.float32),
        ],
        compiler_params=params,
        name="exchange",
    )(codes, density, left, tail_in, swapped, *packs)

    step = 1
    while step < aux:
        ways = 2 if step == 1 or step * 4 > aux else 4
        terms = [parts]
        for way in range(1, ways):
            terms.append(lax.ppermute(parts, "aux", [(i, i ^ (way * step)) for i in range(aux)]))
        while len(terms) > 1:
            terms = [terms[i] + terms[i + 1] for i in range(0, len(terms), 2)]
        parts = terms[0]
        step *= ways
    return parts


def solution(mesh):
    return jax.shard_map(
        shards,
        mesh=mesh,
        in_specs=(
            P("orb", None),
            P("orb", "aux", None, None, None),
            P("orb", "aux", None),
            P("orb", "aux"),
        ),
        out_specs=P("orb", None),
        check_vma=False,
    )
```

```python
import functools

import jax
import jax.numpy as jnp
from jax import lax
from jax.experimental import pallas as pl
from jax.experimental.pallas import tpu as pltpu
from jax.sharding import PartitionSpec as P

BS = 64
LANES = 128
NOTE = 8


def lay_blocks(raw, out_ref):
    slots, aux_width = raw.shape[:2]
    square = raw.reshape(slots * aux_width, BS, BS)
    for tile in range(slots * aux_width // 2):
        both = jnp.concatenate([square[2 * tile], square[2 * tile + 1]], axis=1)
        out_ref[tile * BS : (tile + 1) * BS] = both
    return slots * aux_width // 2


def partner(i, step, sign, orb):
    if orb == 4:
        return i ^ (2 - sign)
    return (i + sign * step) % orb


def owner_of(me, step, sign, orb):
    if orb == 4:
        return me ^ (2 - sign)
    return lax.rem(me - sign * step + orb, orb)


def core_parity():
    return lax.rem(lax.axis_index("aux"), 2)


def pack_kernel(
    orb, kept, pairs_hbm, density_hbm, raw_hbm, full_ref, pairs, rows, raw, sems
):
    copies = [
        pltpu.make_async_copy(src, dst, sems.at[i])
        for i, (src, dst) in enumerate(((raw_hbm, raw), (density_hbm, rows), (pairs_hbm, pairs)))
    ]
    for copy in copies:
        copy.start()
    for copy in copies[1:]:
        copy.wait()
    tiles = rows.shape[1] // LANES
    size = full_ref.shape[0] - tiles * BS - NOTE
    for t in range(tiles):
        lanes = slice(t * LANES, (t + 1) * LANES)
        full_ref[size + t * BS : size + (t + 1) * BS] = rows[:, lanes]
    shape = (NOTE, LANES)
    lane = lax.broadcasted_iota(jnp.int32, shape, 1)
    note = jnp.zeros(shape, jnp.int32)
    for j in range(pairs.shape[2]):
        note = jnp.where(lane == j, jnp.where(j < kept[0, 0], pairs[0, 0, j], orb), note)
    full_ref[size + tiles * BS :] = note.astype(jnp.float32).astype(jnp.bfloat16)
    copies[0].wait()
    lay_blocks(raw[0, 0], full_ref)


def tail_kernel(size, full_ref, out_ref):
    height = BS // 2
    tiles = (out_ref.shape[0] - NOTE) // height
    for t in range(tiles):
        first = pl.multiple_of(size + t * BS + core_parity() * height, height)
        out_ref[t * height : (t + 1) * height] = full_ref[pl.ds(first, height)]
    out_ref[tiles * height :] = full_ref[full_ref.shape[0] - NOTE :]


def lean_kernel(full_ref, tail_ref, out_ref):
    size = out_ref.shape[0] - NOTE
    out_ref[:size] = full_ref[:size]
    out_ref[size:] = tail_ref[tail_ref.shape[0] - NOTE :]


def relay_kernel(slots, aux_width, raw, full_ref, out_ref, left_ref):
    lay_blocks(raw[0, 0], out_ref)
    size = out_ref.shape[0]
    own = jnp.concatenate([full_ref[at : at + BS] for at in range(0, size, BS)], axis=1)
    for p in range(aux_width):
        cuts = [(j * aux_width + p) * BS for j in range(slots)]
        left_ref[p * BS : (p + 1) * BS] = jnp.concatenate(
            [own[:, cut : cut + BS] for cut in cuts], axis=1
        )


def merge_kernel(size, *refs):
    parts, out_ref = refs[:-1], refs[-1]
    at = 0
    for i, part in enumerate(parts):
        first = size if i < len(parts) - 1 else 0
        count = part.shape[0] - NOTE - first
        out_ref[at : at + count] = part[first : first + count]
        at += count


def exchange_kernel(
    orb, slots, aux_width, meta_ref, density_ref, left_ref, tail, swapped, *refs
):
    packs, (out_ref, rows, half_ref, held) = refs[:orb], refs[orb:]
    fulls = packs[2::2]
    notes = meta_ref[...]
    meta = [notes[i] for i in range(orb * slots)]
    me = lax.axis_index("orb")
    parity = core_parity()
    sign = 1 - 2 * parity
    height = BS // 2
    count = density_ref.shape[1] // LANES
    size = slots * aux_width * BS // LANES * BS
    near = pl.multiple_of(parity * height, height)
    far = pl.multiple_of((1 - parity) * height, height)
    across = lax.rem(me + orb // 2, orb)
    owners = [me, across]
    rows[me] = density_ref[...]
    for i, full in enumerate(fulls):
        owners += [owner_of(me, i + 1, sign, orb), owner_of(me, i + 1, -sign, orb)]
        for t in range(count):
            lanes = slice(t * LANES, (t + 1) * LANES)
            at = (i * count + t) * BS
            rows[owners[-2], :, lanes] = full[size + t * BS : size + (t + 1) * BS]
            rows[owners[-1], :, lanes] = swapped[at : at + BS]
    for t in range(count):
        lanes = slice(t * LANES, (t + 1) * LANES)
        at = len(fulls) * count * BS + t * height
        rows[across, pl.ds(near, height), lanes] = tail[t * height : (t + 1) * height]
        rows[across, pl.ds(far, height), lanes] = swapped[at : at + height]
    rows[orb] = jnp.zeros_like(rows[orb])
    selected = jnp.concatenate([rows[meta[j]] for j in range(slots)], axis=0)
    half = jnp.dot(left_ref[...], selected, preferred_element_type=jnp.float32)
    half = half.astype(jnp.bfloat16)
    for k in range(orb):
        half_ref[k] = jnp.concatenate(
            [half[p * BS : (p + 1) * BS, k * BS : (k + 1) * BS] for p in range(aux_width)],
            axis=1,
        )
    half_ref[orb] = jnp.zeros_like(half_ref[orb])
    for way in range(orb):
        codes = meta[way * slots : (way + 1) * slots]
        held[owners[way]] = lax.dot_general(
            jnp.concatenate([half_ref[code] for code in codes], axis=1),
            jnp.concatenate([packs[way][at : at + BS] for at in range(0, size, BS)], axis=1),
            (((1,), (1,)), ((), ())),
            preferred_element_type=jnp.float32,
        )
    out_ref[...] = jnp.concatenate([held[n] for n in range(orb)], axis=1)


def shards(density, tensor_blocks, pairs, kept):
    full_width = density.shape[1]
    slots = tensor_blocks.shape[2]
    aux_width = tensor_blocks.shape[3]
    orb = lax.axis_size("orb")
    aux = lax.axis_size("aux")
    rows = full_width // LANES * BS
    size = slots * aux_width * BS // LANES * BS
    vmem = pl.BlockSpec(memory_space=pltpu.VMEM)
    smem = pl.BlockSpec(memory_space=pltpu.SMEM)
    hbm = pl.BlockSpec(memory_space=pltpu.HBM)
    params = pltpu.CompilerParams(vmem_limit_bytes=32 * 1024 * 1024)

    def array(height):
        return jax.ShapeDtypeStruct((height, LANES), jnp.bfloat16)

    def shift(x, step, sign):
        perm = [
            (a * orb + o, a * orb + partner(o, step, sign * (1 - 2 * (a % 2)), orb))
            for a in range(aux)
            for o in range(orb)
        ]
        return lax.ppermute(x, ("aux", "orb"), perm)

    full = pl.pallas_call(
        functools.partial(pack_kernel, orb),
        out_shape=array(size + rows + NOTE),
        in_specs=[smem, hbm, hbm, hbm],
        out_specs=vmem,
        scratch_shapes=[
            pltpu.SMEM(pairs.shape, jnp.int32),
            pltpu.VMEM(density.shape, jnp.bfloat16),
            pltpu.VMEM(tensor_blocks.shape, jnp.bfloat16),
            pltpu.SemaphoreType.DMA((3,)),
        ],
        compiler_params=params,
        name="pack",
    )(
        kept,
        *(pltpu.with_memory_space_constraint(a, pltpu.HBM) for a in (pairs, density, tensor_blocks)),
    )
    tail = pl.pallas_call(
        functools.partial(tail_kernel, size),
        out_shape=array(rows // 2 + NOTE),
        in_specs=[vmem],
        out_specs=vmem,
        compiler_params=params,
        name="tail",
    )(full)
    lean = pl.pallas_call(
        lean_kernel,
        out_shape=array(size + NOTE),
        in_specs=[vmem] * 2,
        out_specs=vmem,
        compiler_params=params,
        name="lean",
    )(full, tail)
    across = [(i, (i + orb // 2) % orb) for i in range(orb)]
    raw = lax.ppermute(tensor_blocks, "orb", across)
    tail_in = lax.ppermute(tail, "orb", across)
    fulls = [shift(full, i, 1) for i in range(1, orb // 2)]
    leans = [shift(lean, i, -1) for i in range(1, orb // 2)]

    tail_in, raw = lax.optimization_barrier((tail_in, raw))
    merged = pl.pallas_call(
        functools.partial(merge_kernel, size),
        out_shape=array(len(fulls) * rows + rows // 2),
        in_specs=[vmem] * (len(fulls) + 1),
        out_specs=vmem,
        compiler_params=params,
        name="merge",
    )(*fulls, tail_in)
    swapped = lax.ppermute(merged, "aux", [(i, i ^ 1) for i in range(aux)])
    across, left = pl.pallas_call(
        functools.partial(relay_kernel, slots, aux_width),
        out_shape=[
            array(size),
            jax.ShapeDtypeStruct((aux_width * BS, slots * BS), jnp.bfloat16),
        ],
        in_specs=[vmem] * 2,
        out_specs=[vmem] * 2,
        compiler_params=params,
        name="relay",
    )(raw, full)
    swapped, leans = lax.optimization_barrier((swapped, leans))
    packs, notes = [full, across], [tail, tail_in]
    for pair in zip(fulls, leans):
        packs += pair
        notes += pair
    codes = jnp.concatenate([n[-NOTE, :slots] for n in notes]).astype(jnp.int32)
    parts = pl.pallas_call(
        functools.partial(exchange_kernel, orb, slots, aux_width),
        out_shape=jax.ShapeDtypeStruct((BS, full_width), jnp.float32),
        in_specs=[vmem] * (orb + 5),
        out_specs=vmem,
        scratch_shapes=[
            pltpu.VMEM((orb + 1, BS, full_width), jnp.bfloat16),
            pltpu.VMEM((orb + 1, BS, aux_width * BS), jnp.bfloat16),
            pltpu.VMEM((orb, BS, BS), jnp.float32),
        ],
        compiler_params=params,
        name="exchange",
    )(codes, density, left, tail_in, swapped, *packs)

    step = 1
    while step < aux:
        ways = 2 if step == 1 or step * 4 > aux else 4
        terms = [parts]
        for way in range(1, ways):
            terms.append(lax.ppermute(parts, "aux", [(i, i ^ (way * step)) for i in range(aux)]))
        while len(terms) > 1:
            terms = [terms[i] + terms[i + 1] for i in range(0, len(terms), 2)]
        parts = terms[0]
        step *= ways
    return parts


def solution(mesh):
    return jax.shard_map(
        shards,
        mesh=mesh,
        in_specs=(
            P("orb", None),
            P("orb", "aux", None, None, None),
            P("orb", "aux", None),
            P("orb", "aux"),
        ),
        out_specs=P("orb", None),
        check_vma=False,
    )
```

```python
import functools

import jax
import jax.numpy as jnp
from jax import lax
from jax.experimental import pallas as pl
from jax.experimental.pallas import tpu as pltpu
from jax.sharding import PartitionSpec as P

BS = 64
LANES = 128
NOTE = 8


def lay_blocks(raw, out_ref):
    slots, aux_width = raw.shape[:2]
    square = raw.reshape(slots * aux_width, BS, BS)
    for tile in range(slots * aux_width // 2):
        both = jnp.concatenate([square[2 * tile], square[2 * tile + 1]], axis=1)
        out_ref[tile * BS : (tile + 1) * BS] = both
    return slots * aux_width // 2


def partner(i, step, sign, orb):
    if orb == 4:
        return i ^ (2 - sign)
    return (i + sign * step) % orb


def owner_of(me, step, sign, orb):
    if orb == 4:
        return me ^ (2 - sign)
    return lax.rem(me - sign * step + orb, orb)


def core_parity():
    return lax.rem(lax.axis_index("aux"), 2)


def pack_kernel(
    orb, kept, pairs_hbm, density_hbm, raw_hbm, full_ref, pairs, rows, raw, sems
):
    copies = [
        pltpu.make_async_copy(src, dst, sems.at[i])
        for i, (src, dst) in enumerate(((raw_hbm, raw), (density_hbm, rows), (pairs_hbm, pairs)))
    ]
    for copy in copies:
        copy.start()
    for copy in copies[1:]:
        copy.wait()
    tiles = rows.shape[1] // LANES
    size = full_ref.shape[0] - tiles * BS - NOTE
    for t in range(tiles):
        lanes = slice(t * LANES, (t + 1) * LANES)
        full_ref[size + t * BS : size + (t + 1) * BS] = rows[:, lanes]
    shape = (NOTE, LANES)
    lane = lax.broadcasted_iota(jnp.int32, shape, 1)
    note = jnp.zeros(shape, jnp.int32)
    named = pairs[0]
    for j in range(pairs.shape[2]):
        note = jnp.where(lane == j, jnp.where(j < kept[0, 0], named[0, j], orb), note)
    full_ref[size + tiles * BS :] = note.astype(jnp.float32).astype(jnp.bfloat16)
    copies[0].wait()
    lay_blocks(raw[0, 0], full_ref)


def tail_kernel(size, full_ref, out_ref):
    height = BS // 2
    tiles = (out_ref.shape[0] - NOTE) // height
    for t in range(tiles):
        first = pl.multiple_of(size + t * BS + core_parity() * height, height)
        out_ref[t * height : (t + 1) * height] = full_ref[pl.ds(first, height)]
    out_ref[tiles * height :] = full_ref[full_ref.shape[0] - NOTE :]


def lean_kernel(full_ref, tail_ref, out_ref):
    size = out_ref.shape[0] - NOTE
    out_ref[:size] = full_ref[:size]
    out_ref[size:] = tail_ref[tail_ref.shape[0] - NOTE :]


def relay_kernel(slots, aux_width, raw, full_ref, out_ref, left_ref):
    lay_blocks(raw[0, 0], out_ref)
    size = out_ref.shape[0]
    own = jnp.concatenate([full_ref[at : at + BS] for at in range(0, size, BS)], axis=1)
    for p in range(aux_width):
        cuts = [(j * aux_width + p) * BS for j in range(slots)]
        left_ref[p * BS : (p + 1) * BS] = jnp.concatenate(
            [own[:, cut : cut + BS] for cut in cuts], axis=1
        )


def merge_kernel(size, *refs):
    parts, out_ref = refs[:-1], refs[-1]
    at = 0
    for i, part in enumerate(parts):
        first = size if i < len(parts) - 1 else 0
        count = part.shape[0] - NOTE - first
        out_ref[at : at + count] = part[first : first + count]
        at += count


def exchange_kernel(
    orb, slots, aux_width, meta_ref, density_ref, left_ref, tail, swapped, *refs
):
    packs, (out_ref, rows, half_ref, held) = refs[:orb], refs[orb:]
    fulls = packs[2::2]
    notes = meta_ref[...]
    meta = [notes[i] for i in range(orb * slots)]
    me = lax.axis_index("orb")
    parity = core_parity()
    sign = 1 - 2 * parity
    height = BS // 2
    count = density_ref.shape[1] // LANES
    size = slots * aux_width * BS // LANES * BS
    near = pl.multiple_of(parity * height, height)
    far = pl.multiple_of((1 - parity) * height, height)
    across = lax.rem(me + orb // 2, orb)
    owners = [me, across]
    rows[me] = density_ref[...]
    for i, full in enumerate(fulls):
        owners += [owner_of(me, i + 1, sign, orb), owner_of(me, i + 1, -sign, orb)]
        for t in range(count):
            lanes = slice(t * LANES, (t + 1) * LANES)
            at = (i * count + t) * BS
            rows[owners[-2], :, lanes] = full[size + t * BS : size + (t + 1) * BS]
            rows[owners[-1], :, lanes] = swapped[at : at + BS]
    for t in range(count):
        lanes = slice(t * LANES, (t + 1) * LANES)
        at = len(fulls) * count * BS + t * height
        rows[across, pl.ds(near, height), lanes] = tail[t * height : (t + 1) * height]
        rows[across, pl.ds(far, height), lanes] = swapped[at : at + height]
    rows[orb] = jnp.zeros_like(rows[orb])
    selected = jnp.concatenate([rows[meta[j]] for j in range(slots)], axis=0)
    half = jnp.dot(left_ref[...], selected, preferred_element_type=jnp.float32)
    half = half.astype(jnp.bfloat16)
    for k in range(orb):
        half_ref[k] = jnp.concatenate(
            [half[p * BS : (p + 1) * BS, k * BS : (k + 1) * BS] for p in range(aux_width)],
            axis=1,
        )
    half_ref[orb] = jnp.zeros_like(half_ref[orb])
    for way in range(orb):
        codes = meta[way * slots : (way + 1) * slots]
        held[owners[way]] = lax.dot_general(
            jnp.concatenate([half_ref[code] for code in codes], axis=1),
            jnp.concatenate([packs[way][at : at + BS] for at in range(0, size, BS)], axis=1),
            (((1,), (1,)), ((), ())),
            preferred_element_type=jnp.float32,
        )
    out_ref[...] = jnp.concatenate([held[n] for n in range(orb)], axis=1)


def shards(density, tensor_blocks, pairs, kept):
    full_width = density.shape[1]
    slots = tensor_blocks.shape[2]
    aux_width = tensor_blocks.shape[3]
    orb = lax.axis_size("orb")
    aux = lax.axis_size("aux")
    rows = full_width // LANES * BS
    size = slots * aux_width * BS // LANES * BS
    vmem = pl.BlockSpec(memory_space=pltpu.VMEM)
    smem = pl.BlockSpec(memory_space=pltpu.SMEM)
    hbm = pl.BlockSpec(memory_space=pltpu.HBM)
    params = pltpu.CompilerParams(vmem_limit_bytes=32 * 1024 * 1024)

    def array(height):
        return jax.ShapeDtypeStruct((height, LANES), jnp.bfloat16)

    def shift(x, step, sign):
        perm = [
            (a * orb + o, a * orb + partner(o, step, sign * (1 - 2 * (a % 2)), orb))
            for a in range(aux)
            for o in range(orb)
        ]
        return lax.ppermute(x, ("aux", "orb"), perm)

    full = pl.pallas_call(
        functools.partial(pack_kernel, orb),
        out_shape=array(size + rows + NOTE),
        in_specs=[smem, hbm, hbm, hbm],
        out_specs=vmem,
        scratch_shapes=[
            pltpu.VMEM(pairs.shape, jnp.int32),
            pltpu.VMEM(density.shape, jnp.bfloat16),
            pltpu.VMEM(tensor_blocks.shape, jnp.bfloat16),
            pltpu.SemaphoreType.DMA((3,)),
        ],
        compiler_params=params,
        name="pack",
    )(
        kept,
        *(pltpu.with_memory_space_constraint(a, pltpu.HBM) for a in (pairs, density, tensor_blocks)),
    )
    tail = pl.pallas_call(
        functools.partial(tail_kernel, size),
        out_shape=array(rows // 2 + NOTE),
        in_specs=[vmem],
        out_specs=vmem,
        compiler_params=params,
        name="tail",
    )(full)
    lean = pl.pallas_call(
        lean_kernel,
        out_shape=array(size + NOTE),
        in_specs=[vmem] * 2,
        out_specs=vmem,
        compiler_params=params,
        name="lean",
    )(full, tail)
    across = [(i, (i + orb // 2) % orb) for i in range(orb)]
    raw = lax.ppermute(tensor_blocks, "orb", across)
    tail_in = lax.ppermute(tail, "orb", across)
    fulls = [shift(full, i, 1) for i in range(1, orb // 2)]
    leans = [shift(lean, i, -1) for i in range(1, orb // 2)]

    tail_in, raw = lax.optimization_barrier((tail_in, raw))
    merged = pl.pallas_call(
        functools.partial(merge_kernel, size),
        out_shape=array(len(fulls) * rows + rows // 2),
        in_specs=[vmem] * (len(fulls) + 1),
        out_specs=vmem,
        compiler_params=params,
        name="merge",
    )(*fulls, tail_in)
    swapped = lax.ppermute(merged, "aux", [(i, i ^ 1) for i in range(aux)])
    across, left = pl.pallas_call(
        functools.partial(relay_kernel, slots, aux_width),
        out_shape=[
            array(size),
            jax.ShapeDtypeStruct((aux_width * BS, slots * BS), jnp.bfloat16),
        ],
        in_specs=[vmem] * 2,
        out_specs=[vmem] * 2,
        compiler_params=params,
        name="relay",
    )(raw, full)
    swapped, leans = lax.optimization_barrier((swapped, leans))
    packs, notes = [full, across], [tail, tail_in]
    for pair in zip(fulls, leans):
        packs += pair
        notes += pair
    codes = jnp.concatenate([n[-NOTE, :slots] for n in notes]).astype(jnp.int32)
    parts = pl.pallas_call(
        functools.partial(exchange_kernel, orb, slots, aux_width),
        out_shape=jax.ShapeDtypeStruct((BS, full_width), jnp.float32),
        in_specs=[vmem] * (orb + 5),
        out_specs=vmem,
        scratch_shapes=[
            pltpu.VMEM((orb + 1, BS, full_width), jnp.bfloat16),
            pltpu.VMEM((orb + 1, BS, aux_width * BS), jnp.bfloat16),
            pltpu.VMEM((orb, BS, BS), jnp.float32),
        ],
        compiler_params=params,
        name="exchange",
    )(codes, density, left, tail_in, swapped, *packs)

    step = 1
    while step < aux:
        ways = 2 if step == 1 or step * 4 > aux else 4
        terms = [parts]
        for way in range(1, ways):
            terms.append(lax.ppermute(parts, "aux", [(i, i ^ (way * step)) for i in range(aux)]))
        while len(terms) > 1:
            terms = [terms[i] + terms[i + 1] for i in range(0, len(terms), 2)]
        parts = terms[0]
        step *= ways
    return parts


def solution(mesh):
    return jax.shard_map(
        shards,
        mesh=mesh,
        in_specs=(
            P("orb", None),
            P("orb", "aux", None, None, None),
            P("orb", "aux", None),
            P("orb", "aux"),
        ),
        out_specs=P("orb", None),
        check_vma=False,
    )
```

```python
import functools

import jax
import jax.numpy as jnp
from jax import lax
from jax.experimental import pallas as pl
from jax.experimental.pallas import tpu as pltpu
from jax.sharding import PartitionSpec as P

BS = 64
LANES = 128
NOTE = 8


def lay_blocks(raw, out_ref):
    slots, aux_width = raw.shape[:2]
    square = raw.reshape(slots * aux_width, BS, BS)
    for tile in range(slots * aux_width // 2):
        both = jnp.concatenate([square[2 * tile], square[2 * tile + 1]], axis=1)
        out_ref[tile * BS : (tile + 1) * BS] = both
    return slots * aux_width // 2


def partner(i, step, sign, orb):
    if orb == 4:
        return i ^ (2 - sign)
    return (i + sign * step) % orb


def owner_of(me, step, sign, orb):
    if orb == 4:
        return me ^ (2 - sign)
    return lax.rem(me - sign * step + orb, orb)


def core_parity():
    return lax.rem(lax.axis_index("aux"), 2)


def pack_kernel(
    orb, kept, pairs_hbm, density_hbm, raw_hbm, full_ref, pairs, rows, raw, sems
):
    copies = [
        pltpu.make_async_copy(src, dst, sems.at[i])
        for i, (src, dst) in enumerate(((raw_hbm, raw), (density_hbm, rows), (pairs_hbm, pairs)))
    ]
    for copy in copies:
        copy.start()
    for copy in copies[1:]:
        copy.wait()
    tiles = rows.shape[1] // LANES
    size = full_ref.shape[0] - tiles * BS - NOTE
    for t in range(tiles):
        lanes = slice(t * LANES, (t + 1) * LANES)
        full_ref[size + t * BS : size + (t + 1) * BS] = rows[:, lanes]
    shape = (NOTE, LANES)
    lane = lax.broadcasted_iota(jnp.int32, shape, 1)
    note = jnp.zeros(shape, jnp.int32)
    for j in range(pairs.shape[2]):
        note = jnp.where(lane == j, jnp.where(j < kept[0, 0], pairs[0, 0, j], orb), note)
    full_ref[size + tiles * BS :] = note.astype(jnp.float32).astype(jnp.bfloat16)
    copies[0].wait()
    lay_blocks(raw[0, 0], full_ref)


def tail_kernel(size, full_ref, out_ref):
    height = BS // 2
    tiles = (out_ref.shape[0] - NOTE) // height
    for t in range(tiles):
        first = pl.multiple_of(size + t * BS + core_parity() * height, height)
        out_ref[t * height : (t + 1) * height] = full_ref[pl.ds(first, height)]
    out_ref[tiles * height :] = full_ref[full_ref.shape[0] - NOTE :]


def lean_kernel(full_ref, tail_ref, out_ref):
    size = out_ref.shape[0] - NOTE
    out_ref[:size] = full_ref[:size]
    out_ref[size:] = tail_ref[tail_ref.shape[0] - NOTE :]


def relay_kernel(slots, aux_width, raw, full_ref, out_ref, left_ref):
    lay_blocks(raw[0, 0], out_ref)
    size = out_ref.shape[0]
    own = jnp.concatenate([full_ref[at : at + BS] for at in range(0, size, BS)], axis=1)
    for p in range(aux_width):
        cuts = [(j * aux_width + p) * BS for j in range(slots)]
        left_ref[p * BS : (p + 1) * BS] = jnp.concatenate(
            [own[:, cut : cut + BS] for cut in cuts], axis=1
        )


def merge_kernel(size, *refs):
    parts, out_ref = refs[:-1], refs[-1]
    at = 0
    for i, part in enumerate(parts):
        first = size if i < len(parts) - 1 else 0
        count = part.shape[0] - NOTE - first
        out_ref[at : at + count] = part[first : first + count]
        at += count


def exchange_kernel(
    orb, slots, aux_width, meta_ref, density_ref, left_ref, tail, swapped, *refs
):
    packs, (out_ref, rows, half_ref, held) = refs[:orb], refs[orb:]
    fulls = packs[2::2]
    notes = meta_ref[...]
    meta = [notes[i] for i in range(orb * slots)]
    me = lax.axis_index("orb")
    parity = core_parity()
    sign = 1 - 2 * parity
    height = BS // 2
    count = density_ref.shape[1] // LANES
    size = slots * aux_width * BS // LANES * BS
    near = pl.multiple_of(parity * height, height)
    far = pl.multiple_of((1 - parity) * height, height)
    across = lax.rem(me + orb // 2, orb)
    owners = [me, across]
    rows[me] = density_ref[...]
    for i, full in enumerate(fulls):
        owners += [owner_of(me, i + 1, sign, orb), owner_of(me, i + 1, -sign, orb)]
        for t in range(count):
            lanes = slice(t * LANES, (t + 1) * LANES)
            at = (i * count + t) * BS
            rows[owners[-2], :, lanes] = full[size + t * BS : size + (t + 1) * BS]
            rows[owners[-1], :, lanes] = swapped[at : at + BS]
    for t in range(count):
        lanes = slice(t * LANES, (t + 1) * LANES)
        at = len(fulls) * count * BS + t * height
        rows[across, pl.ds(near, height), lanes] = tail[t * height : (t + 1) * height]
        rows[across, pl.ds(far, height), lanes] = swapped[at : at + height]
    rows[orb] = jnp.zeros_like(rows[orb])
    selected = jnp.concatenate([rows[meta[j]] for j in range(slots)], axis=0)
    half = jnp.dot(left_ref[...], selected, preferred_element_type=jnp.float32)
    half = half.astype(jnp.bfloat16)
    for k in range(orb):
        half_ref[k] = jnp.concatenate(
            [half[p * BS : (p + 1) * BS, k * BS : (k + 1) * BS] for p in range(aux_width)],
            axis=1,
        )
    half_ref[orb] = jnp.zeros_like(half_ref[orb])
    for way in range(orb):
        codes = meta[way * slots : (way + 1) * slots]
        held[owners[way]] = lax.dot_general(
            jnp.concatenate([half_ref[code] for code in codes], axis=1),
            jnp.concatenate([packs[way][at : at + BS] for at in range(0, size, BS)], axis=1),
            (((1,), (1,)), ((), ())),
            preferred_element_type=jnp.float32,
        )
    out_ref[...] = jnp.concatenate([held[n] for n in range(orb)], axis=1)


def shards(density, tensor_blocks, pairs, kept):
    full_width = density.shape[1]
    slots = tensor_blocks.shape[2]
    aux_width = tensor_blocks.shape[3]
    orb = lax.axis_size("orb")
    aux = lax.axis_size("aux")
    rows = full_width // LANES * BS
    size = slots * aux_width * BS // LANES * BS
    vmem = pl.BlockSpec(memory_space=pltpu.VMEM)
    smem = pl.BlockSpec(memory_space=pltpu.SMEM)
    hbm = pl.BlockSpec(memory_space=pltpu.HBM)
    params = pltpu.CompilerParams(vmem_limit_bytes=32 * 1024 * 1024)

    def array(height):
        return jax.ShapeDtypeStruct((height, LANES), jnp.bfloat16)

    def shift(x, step, sign):
        perm = [
            (a * orb + o, a * orb + partner(o, step, sign * (1 - 2 * (a % 2)), orb))
            for a in range(aux)
            for o in range(orb)
        ]
        return lax.ppermute(x, ("aux", "orb"), perm)

    full = pl.pallas_call(
        functools.partial(pack_kernel, orb),
        out_shape=array(size + rows + NOTE),
        in_specs=[smem, hbm, hbm, hbm],
        out_specs=vmem,
        scratch_shapes=[
            pltpu.SMEM(pairs.shape, jnp.int32),
            pltpu.VMEM(density.shape, jnp.bfloat16),
            pltpu.VMEM(tensor_blocks.shape, jnp.bfloat16),
            pltpu.SemaphoreType.DMA((3,)),
        ],
        compiler_params=params,
        name="pack",
    )(
        kept,
        *(pltpu.with_memory_space_constraint(a, pltpu.HBM) for a in (pairs, density, tensor_blocks)),
    )
    tail = pl.pallas_call(
        functools.partial(tail_kernel, size),
        out_shape=array(rows // 2 + NOTE),
        in_specs=[vmem],
        out_specs=vmem,
        compiler_params=params,
        name="tail",
    )(full)
    lean = pl.pallas_call(
        lean_kernel,
        out_shape=array(size + NOTE),
        in_specs=[vmem] * 2,
        out_specs=vmem,
        compiler_params=params,
        name="lean",
    )(full, tail)
    across = [(i, (i + orb // 2) % orb) for i in range(orb)]
    raw = lax.ppermute(tensor_blocks, "orb", across)
    tail_in = lax.ppermute(tail, "orb", across)
    fulls = [shift(full, i, 1) for i in range(1, orb // 2)]
    leans = [shift(lean, i, -1) for i in range(1, orb // 2)]

    tail_in, raw = lax.optimization_barrier((tail_in, raw))
    merged = pl.pallas_call(
        functools.partial(merge_kernel, size),
        out_shape=array(len(fulls) * rows + rows // 2),
        in_specs=[vmem] * (len(fulls) + 1),
        out_specs=vmem,
        compiler_params=params,
        name="merge",
    )(*fulls, tail_in)
    swapped = lax.ppermute(merged, "aux", [(i, i ^ 1) for i in range(aux)])
    across, left = pl.pallas_call(
        functools.partial(relay_kernel, slots, aux_width),
        out_shape=[
            array(size),
            jax.ShapeDtypeStruct((aux_width * BS, slots * BS), jnp.bfloat16),
        ],
        in_specs=[vmem] * 2,
        out_specs=[vmem] * 2,
        compiler_params=params,
        name="relay",
    )(raw, full)
    swapped, leans = lax.optimization_barrier((swapped, leans))
    packs, notes = [full, across], [tail, tail_in]
    for pair in zip(fulls, leans):
        packs += pair
        notes += pair
    codes = jnp.concatenate([n[-NOTE, :slots] for n in notes]).astype(jnp.int32)
    parts = pl.pallas_call(
        functools.partial(exchange_kernel, orb, slots, aux_width),
        out_shape=jax.ShapeDtypeStruct((BS, full_width), jnp.float32),
        in_specs=[vmem] * (orb + 5),
        out_specs=vmem,
        scratch_shapes=[
            pltpu.VMEM((orb + 1, BS, full_width), jnp.bfloat16),
            pltpu.VMEM((orb + 1, BS, aux_width * BS), jnp.bfloat16),
            pltpu.VMEM((orb, BS, BS), jnp.float32),
        ],
        compiler_params=params,
        name="exchange",
    )(codes, density, left, tail_in, swapped, *packs)

    step = 1
    while step < aux:
        ways = 2 if step == 1 or step * 4 > aux else 4
        if step == 2:
            parts = parts.astype(jnp.bfloat16)
        terms = [parts]
        for way in range(1, ways):
            terms.append(lax.ppermute(parts, "aux", [(i, i ^ (way * step)) for i in range(aux)]))
        terms = [term.astype(jnp.float32) for term in terms]
        while len(terms) > 1:
            terms = [terms[i] + terms[i + 1] for i in range(0, len(terms), 2)]
        parts = terms[0]
        step *= ways
    return parts


def solution(mesh):
    return jax.shard_map(
        shards,
        mesh=mesh,
        in_specs=(
            P("orb", None),
            P("orb", "aux", None, None, None),
            P("orb", "aux", None),
            P("orb", "aux"),
        ),
        out_specs=P("orb", None),
        check_vma=False,
    )
```

```python
import functools

import jax
import jax.numpy as jnp
from jax import lax
from jax.experimental import pallas as pl
from jax.experimental.pallas import tpu as pltpu
from jax.sharding import PartitionSpec as P

BS = 64
LANES = 128
NOTE = 8


def lay_blocks(raw, out_ref):
    slots, aux_width = raw.shape[:2]
    square = raw.reshape(slots * aux_width, BS, BS)
    for tile in range(slots * aux_width // 2):
        both = jnp.concatenate([square[2 * tile], square[2 * tile + 1]], axis=1)
        out_ref[tile * BS : (tile + 1) * BS] = both
    return slots * aux_width // 2


def partner(i, step, sign, orb):
    if orb == 4:
        return i ^ (2 - sign)
    return (i + sign * step) % orb


def owner_of(me, step, sign, orb):
    if orb == 4:
        return me ^ (2 - sign)
    return lax.rem(me - sign * step + orb, orb)


def core_parity():
    return lax.rem(lax.axis_index("aux"), 2)


def pack_kernel(
    orb, kept, pairs_hbm, density_hbm, raw_hbm, full_ref, pairs, rows, raw, sems
):
    copies = [
        pltpu.make_async_copy(src, dst, sems.at[i])
        for i, (src, dst) in enumerate(((raw_hbm, raw), (density_hbm, rows), (pairs_hbm, pairs)))
    ]
    for copy in copies:
        copy.start()
    for copy in copies[1:]:
        copy.wait()
    tiles = rows.shape[1] // LANES
    size = full_ref.shape[0] - tiles * BS - NOTE
    for t in range(tiles):
        lanes = slice(t * LANES, (t + 1) * LANES)
        full_ref[size + t * BS : size + (t + 1) * BS] = rows[:, lanes]
    shape = (NOTE, LANES)
    lane = lax.broadcasted_iota(jnp.int32, shape, 1)
    note = jnp.zeros(shape, jnp.int32)
    for j in range(pairs.shape[2]):
        note = jnp.where(lane == j, jnp.where(j < kept[0, 0], pairs[0, 0, j], orb), note)
    full_ref[size + tiles * BS :] = note.astype(jnp.float32).astype(jnp.bfloat16)
    copies[0].wait()
    lay_blocks(raw[0, 0], full_ref)


def tail_kernel(size, full_ref, out_ref):
    height = BS // 2
    tiles = (out_ref.shape[0] - NOTE) // height
    for t in range(tiles):
        first = pl.multiple_of(size + t * BS + core_parity() * height, height)
        out_ref[t * height : (t + 1) * height] = full_ref[pl.ds(first, height)]
    out_ref[tiles * height :] = full_ref[full_ref.shape[0] - NOTE :]


def lean_kernel(full_ref, tail_ref, out_ref):
    size = out_ref.shape[0] - NOTE
    out_ref[:size] = full_ref[:size]
    out_ref[size:] = tail_ref[tail_ref.shape[0] - NOTE :]


def relay_kernel(slots, aux_width, raw, full_ref, out_ref, left_ref):
    lay_blocks(raw[0, 0], out_ref)
    size = out_ref.shape[0]
    own = jnp.concatenate([full_ref[at : at + BS] for at in range(0, size, BS)], axis=1)
    for p in range(aux_width):
        cuts = [(j * aux_width + p) * BS for j in range(slots)]
        left_ref[p * BS : (p + 1) * BS] = jnp.concatenate(
            [own[:, cut : cut + BS] for cut in cuts], axis=1
        )


def merge_kernel(size, *refs):
    parts, out_ref = refs[:-1], refs[-1]
    at = 0
    for i, part in enumerate(parts):
        first = size if i < len(parts) - 1 else 0
        count = part.shape[0] - NOTE - first
        out_ref[at : at + count] = part[first : first + count]
        at += count


def exchange_kernel(
    orb, slots, aux_width, meta_ref, density_ref, left_ref, tail, swapped, *refs
):
    packs, (out_ref, rows, half_ref, held) = refs[:orb], refs[orb:]
    fulls = packs[2::2]
    notes = meta_ref[...]
    meta = [notes[i] for i in range(orb * slots)]
    me = lax.axis_index("orb")
    parity = core_parity()
    sign = 1 - 2 * parity
    height = BS // 2
    count = density_ref.shape[1] // LANES
    size = slots * aux_width * BS // LANES * BS
    near = pl.multiple_of(parity * height, height)
    far = pl.multiple_of((1 - parity) * height, height)
    across = lax.rem(me + orb // 2, orb)
    owners = [me, across]
    rows[me] = density_ref[...]
    for i, full in enumerate(fulls):
        owners += [owner_of(me, i + 1, sign, orb), owner_of(me, i + 1, -sign, orb)]
        for t in range(count):
            lanes = slice(t * LANES, (t + 1) * LANES)
            at = (i * count + t) * BS
            rows[owners[-2], :, lanes] = full[size + t * BS : size + (t + 1) * BS]
            rows[owners[-1], :, lanes] = swapped[at : at + BS]
    for t in range(count):
        lanes = slice(t * LANES, (t + 1) * LANES)
        at = len(fulls) * count * BS + t * height
        rows[across, pl.ds(near, height), lanes] = tail[t * height : (t + 1) * height]
        rows[across, pl.ds(far, height), lanes] = swapped[at : at + height]
    rows[orb] = jnp.zeros_like(rows[orb])
    selected = jnp.concatenate([rows[meta[j]] for j in range(slots)], axis=0)
    half = jnp.dot(left_ref[...], selected, preferred_element_type=jnp.float32)
    half = half.astype(jnp.bfloat16)
    for k in range(orb):
        half_ref[k] = jnp.concatenate(
            [half[p * BS : (p + 1) * BS, k * BS : (k + 1) * BS] for p in range(aux_width)],
            axis=1,
        )
    half_ref[orb] = jnp.zeros_like(half_ref[orb])
    for way in range(orb):
        codes = meta[way * slots : (way + 1) * slots]
        held[owners[way]] = lax.dot_general(
            jnp.concatenate([half_ref[code] for code in codes], axis=1),
            jnp.concatenate([packs[way][at : at + BS] for at in range(0, size, BS)], axis=1),
            (((1,), (1,)), ((), ())),
            preferred_element_type=jnp.float32,
        )
    out_ref[...] = jnp.concatenate([held[n] for n in range(orb)], axis=1)


def shards(density, tensor_blocks, pairs, kept):
    full_width = density.shape[1]
    slots = tensor_blocks.shape[2]
    aux_width = tensor_blocks.shape[3]
    orb = lax.axis_size("orb")
    aux = lax.axis_size("aux")
    rows = full_width // LANES * BS
    size = slots * aux_width * BS // LANES * BS
    vmem = pl.BlockSpec(memory_space=pltpu.VMEM)
    smem = pl.BlockSpec(memory_space=pltpu.SMEM)
    hbm = pl.BlockSpec(memory_space=pltpu.HBM)
    params = pltpu.CompilerParams(vmem_limit_bytes=32 * 1024 * 1024)

    def array(height):
        return jax.ShapeDtypeStruct((height, LANES), jnp.bfloat16)

    def shift(x, step, sign):
        perm = [
            (a * orb + o, a * orb + partner(o, step, sign * (1 - 2 * (a % 2)), orb))
            for a in range(aux)
            for o in range(orb)
        ]
        return lax.ppermute(x, ("aux", "orb"), perm)

    full = pl.pallas_call(
        functools.partial(pack_kernel, orb),
        out_shape=array(size + rows + NOTE),
        in_specs=[smem, hbm, hbm, hbm],
        out_specs=vmem,
        scratch_shapes=[
            pltpu.SMEM(pairs.shape, jnp.int32),
            pltpu.VMEM(density.shape, jnp.bfloat16),
            pltpu.VMEM(tensor_blocks.shape, jnp.bfloat16),
            pltpu.SemaphoreType.DMA((3,)),
        ],
        compiler_params=params,
        name="pack",
    )(
        kept,
        *(pltpu.with_memory_space_constraint(a, pltpu.HBM) for a in (pairs, density, tensor_blocks)),
    )
    tail = pl.pallas_call(
        functools.partial(tail_kernel, size),
        out_shape=array(rows // 2 + NOTE),
        in_specs=[vmem],
        out_specs=vmem,
        compiler_params=params,
        name="tail",
    )(full)
    lean = pl.pallas_call(
        lean_kernel,
        out_shape=array(size + NOTE),
        in_specs=[vmem] * 2,
        out_specs=vmem,
        compiler_params=params,
        name="lean",
    )(full, tail)
    across = [(i, (i + orb // 2) % orb) for i in range(orb)]
    raw = lax.ppermute(tensor_blocks, "orb", across)
    tail_in = lax.ppermute(tail, "orb", across)
    fulls = [shift(full, i, 1) for i in range(1, orb // 2)]
    leans = [shift(lean, i, -1) for i in range(1, orb // 2)]

    tail_in, raw = lax.optimization_barrier((tail_in, raw))
    merged = pl.pallas_call(
        functools.partial(merge_kernel, size),
        out_shape=array(len(fulls) * rows + rows // 2),
        in_specs=[vmem] * (len(fulls) + 1),
        out_specs=vmem,
        compiler_params=params,
        name="merge",
    )(*fulls, tail_in)
    swapped = lax.ppermute(merged, "aux", [(i, i ^ 1) for i in range(aux)])
    across, left = pl.pallas_call(
        functools.partial(relay_kernel, slots, aux_width),
        out_shape=[
            array(size),
            jax.ShapeDtypeStruct((aux_width * BS, slots * BS), jnp.bfloat16),
        ],
        in_specs=[vmem] * 2,
        out_specs=[vmem] * 2,
        compiler_params=params,
        name="relay",
    )(raw, full)
    swapped, leans = lax.optimization_barrier((swapped, leans))
    packs, notes = [full, across], [tail, tail_in]
    for pair in zip(fulls, leans):
        packs += pair
        notes += pair
    codes = jnp.concatenate([n[-NOTE, :slots] for n in notes]).astype(jnp.int32)
    parts = pl.pallas_call(
        functools.partial(exchange_kernel, orb, slots, aux_width),
        out_shape=jax.ShapeDtypeStruct((BS, full_width), jnp.float32),
        in_specs=[vmem] * (orb + 5),
        out_specs=vmem,
        scratch_shapes=[
            pltpu.VMEM((orb + 1, BS, full_width), jnp.bfloat16),
            pltpu.VMEM((orb + 1, BS, aux_width * BS), jnp.bfloat16),
            pltpu.VMEM((orb, BS, BS), jnp.float32),
        ],
        compiler_params=params,
        name="exchange",
    )(codes, density, left, tail_in, swapped, *packs)

    odd = core_parity() == 1
    beside = [(i, i ^ 1) for i in range(aux)]
    parts = parts + lax.ppermute(parts, "aux", beside)
    step = 2
    while step < aux:
        if step * 4 > aux:
            parts = parts + lax.ppermute(parts, "aux", [(i, i ^ step) for i in range(aux)])
            break
        if step == 2:
            parts = parts.astype(jnp.bfloat16)
        mid = BS // 2
        straight = [(i, i ^ (2 * step if i % 2 else step)) for i in range(aux)]
        diagonal = [(i, i ^ (3 * step)) for i in range(aux)]
        one = lax.ppermute(parts, "aux", straight)
        two = lax.ppermute(jnp.where(odd, parts[mid:], parts[:mid]), "aux", diagonal)
        got = jnp.concatenate([one, two], axis=0)
        other = lax.ppermute(got, "aux", beside)
        first = jnp.where(odd, other, got).astype(jnp.float32)
        second = jnp.where(odd, got, other).astype(jnp.float32)
        corner = jnp.concatenate([first[BS:], second[BS:]], axis=0)
        parts = (parts.astype(jnp.float32) + first[:BS]) + (second[:BS] + corner)
        step *= 4
    return parts


def solution(mesh):
    return jax.shard_map(
        shards,
        mesh=mesh,
        in_specs=(
            P("orb", None),
            P("orb", "aux", None, None, None),
            P("orb", "aux", None),
            P("orb", "aux"),
        ),
        out_specs=P("orb", None),
        check_vma=False,
    )
```

```python
import functools

import jax
import jax.numpy as jnp
from jax import lax
from jax.experimental import pallas as pl
from jax.experimental.pallas import tpu as pltpu
from jax.sharding import PartitionSpec as P

BS = 64
LANES = 128
NOTE = 8


def lay_blocks(raw, out_ref):
    slots, aux_width = raw.shape[:2]
    square = raw.reshape(slots * aux_width, BS, BS)
    for tile in range(slots * aux_width // 2):
        both = jnp.concatenate([square[2 * tile], square[2 * tile + 1]], axis=1)
        out_ref[tile * BS : (tile + 1) * BS] = both
    return slots * aux_width // 2


def partner(i, step, sign, orb):
    if orb == 4:
        return i ^ (5 - sign) // 2
    return (i + sign * step) % orb


def owner_of(me, step, sign, orb):
    if orb == 4:
        return me ^ jnp.where(sign > 0, 2, 3)
    return lax.rem(me - sign * step + orb, orb)


def opposite(i, orb):
    return i ^ 1 if orb == 4 else (i + orb // 2) % orb


def core_parity():
    return lax.rem(lax.axis_index("aux"), 2)


def pack_kernel(
    orb, kept, pairs_hbm, density_hbm, raw_hbm, full_ref, pairs, rows, raw, sems
):
    copies = [
        pltpu.make_async_copy(src, dst, sems.at[i])
        for i, (src, dst) in enumerate(((raw_hbm, raw), (density_hbm, rows), (pairs_hbm, pairs)))
    ]
    for copy in copies:
        copy.start()
    for copy in copies[1:]:
        copy.wait()
    tiles = rows.shape[1] // LANES
    size = full_ref.shape[0] - tiles * BS - NOTE
    for t in range(tiles):
        lanes = slice(t * LANES, (t + 1) * LANES)
        full_ref[size + t * BS : size + (t + 1) * BS] = rows[:, lanes]
    shape = (NOTE, LANES)
    lane = lax.broadcasted_iota(jnp.int32, shape, 1)
    note = jnp.zeros(shape, jnp.int32)
    for j in range(pairs.shape[2]):
        note = jnp.where(lane == j, jnp.where(j < kept[0, 0], pairs[0, 0, j], orb), note)
    full_ref[size + tiles * BS :] = note.astype(jnp.float32).astype(jnp.bfloat16)
    copies[0].wait()
    lay_blocks(raw[0, 0], full_ref)


def tail_kernel(size, full_ref, out_ref):
    height = BS // 2
    tiles = (out_ref.shape[0] - NOTE) // height
    for t in range(tiles):
        first = pl.multiple_of(size + t * BS + core_parity() * height, height)
        out_ref[t * height : (t + 1) * height] = full_ref[pl.ds(first, height)]
    out_ref[tiles * height :] = full_ref[full_ref.shape[0] - NOTE :]


def lean_kernel(full_ref, tail_ref, out_ref):
    size = out_ref.shape[0] - NOTE
    out_ref[:size] = full_ref[:size]
    out_ref[size:] = tail_ref[tail_ref.shape[0] - NOTE :]


def relay_kernel(slots, aux_width, raw, full_ref, out_ref, left_ref):
    lay_blocks(raw[0, 0], out_ref)
    size = out_ref.shape[0]
    own = jnp.concatenate([full_ref[at : at + BS] for at in range(0, size, BS)], axis=1)
    for p in range(aux_width):
        cuts = [(j * aux_width + p) * BS for j in range(slots)]
        left_ref[p * BS : (p + 1) * BS] = jnp.concatenate(
            [own[:, cut : cut + BS] for cut in cuts], axis=1
        )


def merge_kernel(size, *refs):
    parts, out_ref = refs[:-1], refs[-1]
    at = 0
    for i, part in enumerate(parts):
        first = size if i < len(parts) - 1 else 0
        count = part.shape[0] - NOTE - first
        out_ref[at : at + count] = part[first : first + count]
        at += count


def exchange_kernel(
    orb, slots, aux_width, meta_ref, density_ref, left_ref, tail, swapped, *refs
):
    packs, (out_ref, rows, half_ref, held) = refs[:orb], refs[orb:]
    fulls = packs[2::2]
    notes = meta_ref[...]
    meta = [notes[i] for i in range(orb * slots)]
    me = lax.axis_index("orb")
    parity = core_parity()
    sign = 1 - 2 * parity
    height = BS // 2
    count = density_ref.shape[1] // LANES
    size = slots * aux_width * BS // LANES * BS
    near = pl.multiple_of(parity * height, height)
    far = pl.multiple_of((1 - parity) * height, height)
    across = opposite(me, orb)
    owners = [me, across]
    rows[me] = density_ref[...]
    for i, full in enumerate(fulls):
        owners += [owner_of(me, i + 1, sign, orb), owner_of(me, i + 1, -sign, orb)]
        for t in range(count):
            lanes = slice(t * LANES, (t + 1) * LANES)
            at = (i * count + t) * BS
            rows[owners[-2], :, lanes] = full[size + t * BS : size + (t + 1) * BS]
            rows[owners[-1], :, lanes] = swapped[at : at + BS]
    for t in range(count):
        lanes = slice(t * LANES, (t + 1) * LANES)
        at = len(fulls) * count * BS + t * height
        rows[across, pl.ds(near, height), lanes] = tail[t * height : (t + 1) * height]
        rows[across, pl.ds(far, height), lanes] = swapped[at : at + height]
    rows[orb] = jnp.zeros_like(rows[orb])
    selected = jnp.concatenate([rows[meta[j]] for j in range(slots)], axis=0)
    half = jnp.dot(left_ref[...], selected, preferred_element_type=jnp.float32)
    half = half.astype(jnp.bfloat16)
    for k in range(orb):
        half_ref[k] = jnp.concatenate(
            [half[p * BS : (p + 1) * BS, k * BS : (k + 1) * BS] for p in range(aux_width)],
            axis=1,
        )
    half_ref[orb] = jnp.zeros_like(half_ref[orb])
    for way in range(orb):
        codes = meta[way * slots : (way + 1) * slots]
        held[owners[way]] = lax.dot_general(
            jnp.concatenate([half_ref[code] for code in codes], axis=1),
            jnp.concatenate([packs[way][at : at + BS] for at in range(0, size, BS)], axis=1),
            (((1,), (1,)), ((), ())),
            preferred_element_type=jnp.float32,
        )
    out_ref[...] = jnp.concatenate([held[n] for n in range(orb)], axis=1)


def shards(density, tensor_blocks, pairs, kept):
    full_width = density.shape[1]
    slots = tensor_blocks.shape[2]
    aux_width = tensor_blocks.shape[3]
    orb = lax.axis_size("orb")
    aux = lax.axis_size("aux")
    rows = full_width // LANES * BS
    size = slots * aux_width * BS // LANES * BS
    vmem = pl.BlockSpec(memory_space=pltpu.VMEM)
    smem = pl.BlockSpec(memory_space=pltpu.SMEM)
    hbm = pl.BlockSpec(memory_space=pltpu.HBM)
    params = pltpu.CompilerParams(vmem_limit_bytes=32 * 1024 * 1024)

    def array(height):
        return jax.ShapeDtypeStruct((height, LANES), jnp.bfloat16)

    def shift(x, step, sign):
        perm = [
            (a * orb + o, a * orb + partner(o, step, sign * (1 - 2 * (a % 2)), orb))
            for a in range(aux)
            for o in range(orb)
        ]
        return lax.ppermute(x, ("aux", "orb"), perm)

    full = pl.pallas_call(
        functools.partial(pack_kernel, orb),
        out_shape=array(size + rows + NOTE),
        in_specs=[smem, hbm, hbm, hbm],
        out_specs=vmem,
        scratch_shapes=[
            pltpu.SMEM(pairs.shape, jnp.int32),
            pltpu.VMEM(density.shape, jnp.bfloat16),
            pltpu.VMEM(tensor_blocks.shape, jnp.bfloat16),
            pltpu.SemaphoreType.DMA((3,)),
        ],
        compiler_params=params,
        name="pack",
    )(
        kept,
        *(pltpu.with_memory_space_constraint(a, pltpu.HBM) for a in (pairs, density, tensor_blocks)),
    )
    tail = pl.pallas_call(
        functools.partial(tail_kernel, size),
        out_shape=array(rows // 2 + NOTE),
        in_specs=[vmem],
        out_specs=vmem,
        compiler_params=params,
        name="tail",
    )(full)
    lean = pl.pallas_call(
        lean_kernel,
        out_shape=array(size + NOTE),
        in_specs=[vmem] * 2,
        out_specs=vmem,
        compiler_params=params,
        name="lean",
    )(full, tail)
    across = [(i, opposite(i, orb)) for i in range(orb)]
    raw = lax.ppermute(tensor_blocks, "orb", across)
    tail_in = lax.ppermute(tail, "orb", across)
    fulls = [shift(full, i, 1) for i in range(1, orb // 2)]
    leans = [shift(lean, i, -1) for i in range(1, orb // 2)]

    tail_in, raw = lax.optimization_barrier((tail_in, raw))
    merged = pl.pallas_call(
        functools.partial(merge_kernel, size),
        out_shape=array(len(fulls) * rows + rows // 2),
        in_specs=[vmem] * (len(fulls) + 1),
        out_specs=vmem,
        compiler_params=params,
        name="merge",
    )(*fulls, tail_in)
    swapped = lax.ppermute(merged, "aux", [(i, i ^ 1) for i in range(aux)])
    across, left = pl.pallas_call(
        functools.partial(relay_kernel, slots, aux_width),
        out_shape=[
            array(size),
            jax.ShapeDtypeStruct((aux_width * BS, slots * BS), jnp.bfloat16),
        ],
        in_specs=[vmem] * 2,
        out_specs=[vmem] * 2,
        compiler_params=params,
        name="relay",
    )(raw, full)
    swapped, leans = lax.optimization_barrier((swapped, leans))
    packs, notes = [full, across], [tail, tail_in]
    for pair in zip(fulls, leans):
        packs += pair
        notes += pair
    codes = jnp.concatenate([n[-NOTE, :slots] for n in notes]).astype(jnp.int32)
    parts = pl.pallas_call(
        functools.partial(exchange_kernel, orb, slots, aux_width),
        out_shape=jax.ShapeDtypeStruct((BS, full_width), jnp.float32),
        in_specs=[vmem] * (orb + 5),
        out_specs=vmem,
        scratch_shapes=[
            pltpu.VMEM((orb + 1, BS, full_width), jnp.bfloat16),
            pltpu.VMEM((orb + 1, BS, aux_width * BS), jnp.bfloat16),
            pltpu.VMEM((orb, BS, BS), jnp.float32),
        ],
        compiler_params=params,
        name="exchange",
    )(codes, density, left, tail_in, swapped, *packs)

    step = 1
    while step < aux:
        ways = 2 if step == 1 or step * 4 > aux else 4
        if step == 2:
            parts = parts.astype(jnp.bfloat16)
        terms = [parts]
        for way in range(1, ways):
            terms.append(lax.ppermute(parts, "aux", [(i, i ^ (way * step)) for i in range(aux)]))
        terms = [term.astype(jnp.float32) for term in terms]
        while len(terms) > 1:
            terms = [terms[i] + terms[i + 1] for i in range(0, len(terms), 2)]
        parts = terms[0]
        step *= ways
    return parts


def solution(mesh):
    return jax.shard_map(
        shards,
        mesh=mesh,
        in_specs=(
            P("orb", None),
            P("orb", "aux", None, None, None),
            P("orb", "aux", None),
            P("orb", "aux"),
        ),
        out_specs=P("orb", None),
        check_vma=False,
    )
```

```python
import functools

import jax
import jax.numpy as jnp
from jax import lax
from jax.experimental import pallas as pl
from jax.experimental.pallas import tpu as pltpu
from jax.sharding import PartitionSpec as P

BS = 64
LANES = 128
NOTE = 8


def lay_blocks(raw, out_ref, first=0):
    slots, aux_width = raw.shape[:2]
    square = raw.reshape(slots * aux_width, BS, BS)
    for tile in range(slots * aux_width // 2):
        both = jnp.concatenate([square[2 * tile], square[2 * tile + 1]], axis=1)
        out_ref[first + tile * BS : first + (tile + 1) * BS] = both
    return slots * aux_width // 2


def partner(i, step, sign, orb):
    if orb == 4:
        return i ^ (2 - sign)
    return (i + sign * step) % orb


def owner_of(me, step, sign, orb):
    if orb == 4:
        return me ^ (2 - sign)
    return lax.rem(me - sign * step + orb, orb)


def core_parity():
    return lax.rem(lax.axis_index("aux"), 2)


def pack_kernel(
    orb, kept, pairs_hbm, density_hbm, raw_hbm, full_ref, pairs, rows, raw, sems
):
    slots = raw.shape[2]
    moves = [(density_hbm, rows), (pairs_hbm, pairs)]
    moves += [(raw_hbm.at[0, 0, j], raw.at[0, 0, j]) for j in range(slots)]
    copies = [
        pltpu.make_async_copy(src, dst, sems.at[i]) for i, (src, dst) in enumerate(moves)
    ]
    for copy in copies:
        copy.start()
    for copy in copies[:2]:
        copy.wait()
    tiles = rows.shape[1] // LANES
    size = full_ref.shape[0] - tiles * BS - NOTE
    for t in range(tiles):
        lanes = slice(t * LANES, (t + 1) * LANES)
        full_ref[size + t * BS : size + (t + 1) * BS] = rows[:, lanes]
    shape = (NOTE, LANES)
    lane = lax.broadcasted_iota(jnp.int32, shape, 1)
    note = jnp.zeros(shape, jnp.int32)
    for j in range(pairs.shape[2]):
        note = jnp.where(lane == j, jnp.where(j < kept[0, 0], pairs[0, 0, j], orb), note)
    full_ref[size + tiles * BS :] = note.astype(jnp.float32).astype(jnp.bfloat16)
    for j in range(slots):
        copies[2 + j].wait()
        lay_blocks(raw[0, 0, j : j + 1], full_ref, j * size // slots)


def tail_kernel(size, full_ref, out_ref):
    height = BS // 2
    tiles = (out_ref.shape[0] - NOTE) // height
    for t in range(tiles):
        first = pl.multiple_of(size + t * BS + core_parity() * height, height)
        out_ref[t * height : (t + 1) * height] = full_ref[pl.ds(first, height)]
    out_ref[tiles * height :] = full_ref[full_ref.shape[0] - NOTE :]


def lean_kernel(full_ref, tail_ref, out_ref):
    size = out_ref.shape[0] - NOTE
    out_ref[:size] = full_ref[:size]
    out_ref[size:] = tail_ref[tail_ref.shape[0] - NOTE :]


def relay_kernel(slots, aux_width, raw, full_ref, out_ref, left_ref):
    lay_blocks(raw[0, 0], out_ref)
    size = out_ref.shape[0]
    own = jnp.concatenate([full_ref[at : at + BS] for at in range(0, size, BS)], axis=1)
    for p in range(aux_width):
        cuts = [(j * aux_width + p) * BS for j in range(slots)]
        left_ref[p * BS : (p + 1) * BS] = jnp.concatenate(
            [own[:, cut : cut + BS] for cut in cuts], axis=1
        )


def merge_kernel(size, *refs):
    parts, out_ref = refs[:-1], refs[-1]
    at = 0
    for i, part in enumerate(parts):
        first = size if i < len(parts) - 1 else 0
        count = part.shape[0] - NOTE - first
        out_ref[at : at + count] = part[first : first + count]
        at += count


def exchange_kernel(
    orb, slots, aux_width, meta_ref, density_ref, left_ref, tail, swapped, *refs
):
    packs, (out_ref, rows, half_ref, held) = refs[:orb], refs[orb:]
    fulls = packs[2::2]
    notes = meta_ref[...]
    meta = [notes[i] for i in range(orb * slots)]
    me = lax.axis_index("orb")
    parity = core_parity()
    sign = 1 - 2 * parity
    height = BS // 2
    count = density_ref.shape[1] // LANES
    size = slots * aux_width * BS // LANES * BS
    near = pl.multiple_of(parity * height, height)
    far = pl.multiple_of((1 - parity) * height, height)
    across = lax.rem(me + orb // 2, orb)
    owners = [me, across]
    rows[me] = density_ref[...]
    for i, full in enumerate(fulls):
        owners += [owner_of(me, i + 1, sign, orb), owner_of(me, i + 1, -sign, orb)]
        for t in range(count):
            lanes = slice(t * LANES, (t + 1) * LANES)
            at = (i * count + t) * BS
            rows[owners[-2], :, lanes] = full[size + t * BS : size + (t + 1) * BS]
            rows[owners[-1], :, lanes] = swapped[at : at + BS]
    for t in range(count):
        lanes = slice(t * LANES, (t + 1) * LANES)
        at = len(fulls) * count * BS + t * height
        rows[across, pl.ds(near, height), lanes] = tail[t * height : (t + 1) * height]
        rows[across, pl.ds(far, height), lanes] = swapped[at : at + height]
    rows[orb] = jnp.zeros_like(rows[orb])
    selected = jnp.concatenate([rows[meta[j]] for j in range(slots)], axis=0)
    half = jnp.dot(left_ref[...], selected, preferred_element_type=jnp.float32)
    half = half.astype(jnp.bfloat16)
    for k in range(orb):
        half_ref[k] = jnp.concatenate(
            [half[p * BS : (p + 1) * BS, k * BS : (k + 1) * BS] for p in range(aux_width)],
            axis=1,
        )
    half_ref[orb] = jnp.zeros_like(half_ref[orb])
    for way in range(orb):
        codes = meta[way * slots : (way + 1) * slots]
        held[owners[way]] = lax.dot_general(
            jnp.concatenate([half_ref[code] for code in codes], axis=1),
            jnp.concatenate([packs[way][at : at + BS] for at in range(0, size, BS)], axis=1),
            (((1,), (1,)), ((), ())),
            preferred_element_type=jnp.float32,
        )
    out_ref[...] = jnp.concatenate([held[n] for n in range(orb)], axis=1)


def shards(density, tensor_blocks, pairs, kept):
    full_width = density.shape[1]
    slots = tensor_blocks.shape[2]
    aux_width = tensor_blocks.shape[3]
    orb = lax.axis_size("orb")
    aux = lax.axis_size("aux")
    rows = full_width // LANES * BS
    size = slots * aux_width * BS // LANES * BS
    vmem = pl.BlockSpec(memory_space=pltpu.VMEM)
    smem = pl.BlockSpec(memory_space=pltpu.SMEM)
    hbm = pl.BlockSpec(memory_space=pltpu.HBM)
    params = pltpu.CompilerParams(vmem_limit_bytes=32 * 1024 * 1024)

    def array(height):
        return jax.ShapeDtypeStruct((height, LANES), jnp.bfloat16)

    def shift(x, step, sign):
        perm = [
            (a * orb + o, a * orb + partner(o, step, sign * (1 - 2 * (a % 2)), orb))
            for a in range(aux)
            for o in range(orb)
        ]
        return lax.ppermute(x, ("aux", "orb"), perm)

    full = pl.pallas_call(
        functools.partial(pack_kernel, orb),
        out_shape=array(size + rows + NOTE),
        in_specs=[smem, hbm, hbm, hbm],
        out_specs=vmem,
        scratch_shapes=[
            pltpu.SMEM(pairs.shape, jnp.int32),
            pltpu.VMEM(density.shape, jnp.bfloat16),
            pltpu.VMEM(tensor_blocks.shape, jnp.bfloat16),
            pltpu.SemaphoreType.DMA((2 + slots,)),
        ],
        compiler_params=params,
        name="pack",
    )(
        kept,
        *(pltpu.with_memory_space_constraint(a, pltpu.HBM) for a in (pairs, density, tensor_blocks)),
    )
    tail = pl.pallas_call(
        functools.partial(tail_kernel, size),
        out_shape=array(rows // 2 + NOTE),
        in_specs=[vmem],
        out_specs=vmem,
        compiler_params=params,
        name="tail",
    )(full)
    lean = pl.pallas_call(
        lean_kernel,
        out_shape=array(size + NOTE),
        in_specs=[vmem] * 2,
        out_specs=vmem,
        compiler_params=params,
        name="lean",
    )(full, tail)
    across = [(i, (i + orb // 2) % orb) for i in range(orb)]
    raw = lax.ppermute(tensor_blocks, "orb", across)
    tail_in = lax.ppermute(tail, "orb", across)
    fulls = [shift(full, i, 1) for i in range(1, orb // 2)]
    leans = [shift(lean, i, -1) for i in range(1, orb // 2)]

    tail_in, raw = lax.optimization_barrier((tail_in, raw))
    merged = pl.pallas_call(
        functools.partial(merge_kernel, size),
        out_shape=array(len(fulls) * rows + rows // 2),
        in_specs=[vmem] * (len(fulls) + 1),
        out_specs=vmem,
        compiler_params=params,
        name="merge",
    )(*fulls, tail_in)
    swapped = lax.ppermute(merged, "aux", [(i, i ^ 1) for i in range(aux)])
    across, left = pl.pallas_call(
        functools.partial(relay_kernel, slots, aux_width),
        out_shape=[
            array(size),
            jax.ShapeDtypeStruct((aux_width * BS, slots * BS), jnp.bfloat16),
        ],
        in_specs=[vmem] * 2,
        out_specs=[vmem] * 2,
        compiler_params=params,
        name="relay",
    )(raw, full)
    swapped, leans = lax.optimization_barrier((swapped, leans))
    packs, notes = [full, across], [tail, tail_in]
    for pair in zip(fulls, leans):
        packs += pair
        notes += pair
    codes = jnp.concatenate([n[-NOTE, :slots] for n in notes]).astype(jnp.int32)
    parts = pl.pallas_call(
        functools.partial(exchange_kernel, orb, slots, aux_width),
        out_shape=jax.ShapeDtypeStruct((BS, full_width), jnp.float32),
        in_specs=[vmem] * (orb + 5),
        out_specs=vmem,
        scratch_shapes=[
            pltpu.VMEM((orb + 1, BS, full_width), jnp.bfloat16),
            pltpu.VMEM((orb + 1, BS, aux_width * BS), jnp.bfloat16),
            pltpu.VMEM((orb, BS, BS), jnp.float32),
        ],
        compiler_params=params,
        name="exchange",
    )(codes, density, left, tail_in, swapped, *packs)

    step = 1
    while step < aux:
        ways = 2 if step == 1 or step * 4 > aux else 4
        if step == 2:
            parts = parts.astype(jnp.bfloat16)
        terms = [parts]
        for way in range(1, ways):
            terms.append(lax.ppermute(parts, "aux", [(i, i ^ (way * step)) for i in range(aux)]))
        terms = [term.astype(jnp.float32) for term in terms]
        while len(terms) > 1:
            terms = [terms[i] + terms[i + 1] for i in range(0, len(terms), 2)]
        parts = terms[0]
        step *= ways
    return parts


def solution(mesh):
    return jax.shard_map(
        shards,
        mesh=mesh,
        in_specs=(
            P("orb", None),
            P("orb", "aux", None, None, None),
            P("orb", "aux", None),
            P("orb", "aux"),
        ),
        out_specs=P("orb", None),
        check_vma=False,
    )
```

```python
import functools

import jax
import jax.numpy as jnp
from jax import lax
from jax.experimental import pallas as pl
from jax.experimental.pallas import tpu as pltpu
from jax.sharding import PartitionSpec as P

BS = 64
LANES = 128
NOTE = 8


def lay_blocks(raw, out_ref):
    slots, aux_width = raw.shape[:2]
    square = raw.reshape(slots * aux_width, BS, BS)
    for tile in range(slots * aux_width // 2):
        both = jnp.concatenate([square[2 * tile], square[2 * tile + 1]], axis=1)
        out_ref[tile * BS : (tile + 1) * BS] = both
    return slots * aux_width // 2


def partner(i, step, sign, orb):
    if orb == 4:
        return i ^ (2 - sign)
    return (i + sign * step) % orb


def owner_of(me, step, sign, orb):
    if orb == 4:
        return me ^ (2 - sign)
    return lax.rem(me - sign * step + orb, orb)


def core_parity():
    return lax.rem(lax.axis_index("aux"), 2)


def pack_kernel(
    orb, kept, pairs_hbm, density_hbm, raw_hbm, full_ref, pairs, rows, raw, sems
):
    copies = [
        pltpu.make_async_copy(src, dst, sems.at[i])
        for i, (src, dst) in enumerate(((raw_hbm, raw), (density_hbm, rows), (pairs_hbm, pairs)))
    ]
    for copy in copies:
        copy.start()
    for copy in copies[1:]:
        copy.wait()
    tiles = rows.shape[1] // LANES
    size = full_ref.shape[0] - tiles * BS - NOTE
    for t in range(tiles):
        lanes = slice(t * LANES, (t + 1) * LANES)
        full_ref[size + t * BS : size + (t + 1) * BS] = rows[:, lanes]
    shape = (NOTE, LANES)
    lane = lax.broadcasted_iota(jnp.int32, shape, 1)
    note = jnp.zeros(shape, jnp.int32)
    for j in range(pairs.shape[2]):
        note = jnp.where(lane == j, jnp.where(j < kept[0, 0], pairs[0, 0, j], orb), note)
    full_ref[size + tiles * BS :] = note.astype(jnp.float32).astype(jnp.bfloat16)
    copies[0].wait()
    lay_blocks(raw[0, 0], full_ref)


def tail_kernel(size, full_ref, out_ref):
    height = BS // 2
    tiles = (out_ref.shape[0] - NOTE) // height
    for t in range(tiles):
        first = pl.multiple_of(size + t * BS + core_parity() * height, height)
        out_ref[t * height : (t + 1) * height] = full_ref[pl.ds(first, height)]
    out_ref[tiles * height :] = full_ref[full_ref.shape[0] - NOTE :]


def lean_kernel(full_ref, tail_ref, out_ref):
    size = out_ref.shape[0] - NOTE
    out_ref[:size] = full_ref[:size]
    out_ref[size:] = tail_ref[tail_ref.shape[0] - NOTE :]


def relay_kernel(slots, aux_width, raw, full_ref, out_ref, left_ref):
    lay_blocks(raw[0, 0], out_ref)
    size = out_ref.shape[0]
    own = jnp.concatenate([full_ref[at : at + BS] for at in range(0, size, BS)], axis=1)
    for p in range(aux_width):
        cuts = [(j * aux_width + p) * BS for j in range(slots)]
        left_ref[p * BS : (p + 1) * BS] = jnp.concatenate(
            [own[:, cut : cut + BS] for cut in cuts], axis=1
        )


def merge_kernel(size, *refs):
    parts, out_ref = refs[:-1], refs[-1]
    at = 0
    for i, part in enumerate(parts):
        first = size if i < len(parts) - 1 else 0
        count = part.shape[0] - NOTE - first
        out_ref[at : at + count] = part[first : first + count]
        at += count


def exchange_kernel(
    orb, slots, aux_width, meta_ref, density_ref, left_ref, tail, swapped, *refs
):
    packs, (out_ref, rows, half_ref, held) = refs[:orb], refs[orb:]
    fulls = packs[2::2]
    notes = meta_ref[...]
    meta = [notes[i] for i in range(orb * slots)]
    me = lax.axis_index("orb")
    parity = core_parity()
    sign = 1 - 2 * parity
    height = BS // 2
    count = density_ref.shape[1] // LANES
    size = slots * aux_width * BS // LANES * BS
    near = pl.multiple_of(parity * height, height)
    far = pl.multiple_of((1 - parity) * height, height)
    across = lax.rem(me + orb // 2, orb)
    owners = [me, across]
    rows[me] = density_ref[...]
    for i, full in enumerate(fulls):
        owners += [owner_of(me, i + 1, sign, orb), owner_of(me, i + 1, -sign, orb)]
        for t in range(count):
            lanes = slice(t * LANES, (t + 1) * LANES)
            at = (i * count + t) * BS
            rows[owners[-2], :, lanes] = full[size + t * BS : size + (t + 1) * BS]
            rows[owners[-1], :, lanes] = swapped[at : at + BS]
    for t in range(count):
        lanes = slice(t * LANES, (t + 1) * LANES)
        at = len(fulls) * count * BS + t * height
        rows[across, pl.ds(near, height), lanes] = tail[t * height : (t + 1) * height]
        rows[across, pl.ds(far, height), lanes] = swapped[at : at + height]
    rows[orb] = jnp.zeros_like(rows[orb])
    selected = jnp.concatenate([rows[meta[j]] for j in range(slots)], axis=0)
    half = jnp.dot(left_ref[...], selected, preferred_element_type=jnp.float32)
    half = half.astype(jnp.bfloat16)
    for k in range(orb):
        half_ref[k] = jnp.concatenate(
            [half[p * BS : (p + 1) * BS, k * BS : (k + 1) * BS] for p in range(aux_width)],
            axis=1,
        )
    half_ref[orb] = jnp.zeros_like(half_ref[orb])
    for way in range(orb):
        codes = meta[way * slots : (way + 1) * slots]
        held[owners[way]] = lax.dot_general(
            jnp.concatenate([half_ref[code] for code in codes], axis=1),
            jnp.concatenate([packs[way][at : at + BS] for at in range(0, size, BS)], axis=1),
            (((1,), (1,)), ((), ())),
            preferred_element_type=jnp.float32,
        )
    out_ref[...] = jnp.concatenate([held[n] for n in range(orb)], axis=1)


def shards(density, tensor_blocks, pairs, kept):
    full_width = density.shape[1]
    slots = tensor_blocks.shape[2]
    aux_width = tensor_blocks.shape[3]
    orb = lax.axis_size("orb")
    aux = lax.axis_size("aux")
    rows = full_width // LANES * BS
    size = slots * aux_width * BS // LANES * BS
    vmem = pl.BlockSpec(memory_space=pltpu.VMEM)
    smem = pl.BlockSpec(memory_space=pltpu.SMEM)
    hbm = pl.BlockSpec(memory_space=pltpu.HBM)
    params = pltpu.CompilerParams(vmem_limit_bytes=32 * 1024 * 1024)

    def array(height):
        return jax.ShapeDtypeStruct((height, LANES), jnp.bfloat16)

    def shift(x, step, sign):
        perm = [
            (a * orb + o, a * orb + partner(o, step, sign * (1 - 2 * (a % 2)), orb))
            for a in range(aux)
            for o in range(orb)
        ]
        return lax.ppermute(x, ("aux", "orb"), perm)

    full = pl.pallas_call(
        functools.partial(pack_kernel, orb),
        out_shape=array(size + rows + NOTE),
        in_specs=[smem, hbm, hbm, hbm],
        out_specs=vmem,
        scratch_shapes=[
            pltpu.SMEM(pairs.shape, jnp.int32),
            pltpu.VMEM(density.shape, jnp.bfloat16),
            pltpu.VMEM(tensor_blocks.shape, jnp.bfloat16),
            pltpu.SemaphoreType.DMA((3,)),
        ],
        compiler_params=params,
        name="pack",
    )(
        kept,
        *(pltpu.with_memory_space_constraint(a, pltpu.HBM) for a in (pairs, density, tensor_blocks)),
    )
    tail = pl.pallas_call(
        functools.partial(tail_kernel, size),
        out_shape=array(rows // 2 + NOTE),
        in_specs=[vmem],
        out_specs=vmem,
        compiler_params=params,
        name="tail",
    )(full)
    lean = pl.pallas_call(
        lean_kernel,
        out_shape=array(size + NOTE),
        in_specs=[vmem] * 2,
        out_specs=vmem,
        compiler_params=params,
        name="lean",
    )(full, tail)
    across = [(i, (i + orb // 2) % orb) for i in range(orb)]
    raw = lax.ppermute(tensor_blocks, "orb", across)
    tail_in = lax.ppermute(tail, "orb", across)
    fulls = [shift(full, i, 1) for i in range(1, orb // 2)]
    leans = [shift(lean, i, -1) for i in range(1, orb // 2)]

    tail_in, raw = lax.optimization_barrier((tail_in, raw))
    merged = pl.pallas_call(
        functools.partial(merge_kernel, size),
        out_shape=array(len(fulls) * rows + rows // 2),
        in_specs=[vmem] * (len(fulls) + 1),
        out_specs=vmem,
        compiler_params=params,
        name="merge",
    )(*fulls, tail_in)
    swapped = lax.ppermute(merged, "aux", [(i, i ^ 1) for i in range(aux)])
    across, left = pl.pallas_call(
        functools.partial(relay_kernel, slots, aux_width),
        out_shape=[
            array(size),
            jax.ShapeDtypeStruct((aux_width * BS, slots * BS), jnp.bfloat16),
        ],
        in_specs=[vmem] * 2,
        out_specs=[vmem] * 2,
        compiler_params=params,
        name="relay",
    )(raw, full)
    swapped, leans = lax.optimization_barrier((swapped, leans))
    packs, notes = [full, across], [tail, tail_in]
    for pair in zip(fulls, leans):
        packs += pair
        notes += pair
    codes = jnp.concatenate([n[-NOTE, :slots] for n in notes]).astype(jnp.int32)
    parts = pl.pallas_call(
        functools.partial(exchange_kernel, orb, slots, aux_width),
        out_shape=jax.ShapeDtypeStruct((BS, full_width), jnp.float32),
        in_specs=[vmem] * (orb + 5),
        out_specs=vmem,
        scratch_shapes=[
            pltpu.VMEM((orb + 1, BS, full_width), jnp.bfloat16),
            pltpu.VMEM((orb + 1, BS, aux_width * BS), jnp.bfloat16),
            pltpu.VMEM((orb, BS, BS), jnp.float32),
        ],
        compiler_params=params,
        name="exchange",
    )(codes, density, left, tail_in, swapped, *packs)

    step = 1
    while step < aux:
        ways = 2 if step == 1 or step * 4 > aux else 4
        if step == 2:
            parts = parts.astype(jnp.bfloat16)
        terms = [parts]
        for way in range(1, ways):
            terms.append(lax.ppermute(parts, "aux", [(i, i ^ (way * step)) for i in range(aux)]))
        terms = [term.astype(jnp.float32) for term in terms[::-1]]
        while len(terms) > 1:
            terms = [terms[i] + terms[i + 1] for i in range(0, len(terms), 2)]
        parts = terms[0]
        step *= ways
    return parts


def solution(mesh):
    return jax.shard_map(
        shards,
        mesh=mesh,
        in_specs=(
            P("orb", None),
            P("orb", "aux", None, None, None),
            P("orb", "aux", None),
            P("orb", "aux"),
        ),
        out_specs=P("orb", None),
        check_vma=False,
    )
```

```python
import functools

import jax
import jax.numpy as jnp
from jax import lax
from jax.experimental import pallas as pl
from jax.experimental.pallas import tpu as pltpu
from jax.sharding import PartitionSpec as P

BS = 64
LANES = 128
NOTE = 16


def lay_blocks(raw, out_ref):
    slots, aux_width = raw.shape[:2]
    square = raw.reshape(slots * aux_width, BS, BS)
    for tile in range(slots * aux_width // 2):
        both = jnp.concatenate([square[2 * tile], square[2 * tile + 1]], axis=1)
        out_ref[tile * BS : (tile + 1) * BS] = both
    return slots * aux_width // 2


def partner(i, step, sign, orb):
    if orb == 4:
        return i ^ (2 - sign)
    return (i + sign * step) % orb


def owner_of(me, step, sign, orb):
    if orb == 4:
        return me ^ (2 - sign)
    return lax.rem(me - sign * step + orb, orb)


def core_parity():
    return lax.rem(lax.axis_index("aux"), 2)


def pack_kernel(
    orb, kept, pairs_hbm, density_hbm, raw_hbm, full_ref, pairs, rows, raw, sems
):
    copies = [
        pltpu.make_async_copy(src, dst, sems.at[i])
        for i, (src, dst) in enumerate(((raw_hbm, raw), (density_hbm, rows), (pairs_hbm, pairs)))
    ]
    for copy in copies:
        copy.start()
    for copy in copies[1:]:
        copy.wait()
    tiles = rows.shape[1] // LANES
    size = full_ref.shape[0] - tiles * BS - NOTE
    for t in range(tiles):
        lanes = slice(t * LANES, (t + 1) * LANES)
        full_ref[size + t * BS : size + (t + 1) * BS] = rows[:, lanes]
    shape = (NOTE, LANES)
    lane = lax.broadcasted_iota(jnp.int32, shape, 1)
    note = jnp.zeros(shape, jnp.int32)
    for j in range(pairs.shape[2]):
        note = jnp.where(lane == j, jnp.where(j < kept[0, 0], pairs[0, 0, j], orb), note)
    full_ref[size + tiles * BS :] = note.astype(jnp.float32).astype(jnp.bfloat16)
    copies[0].wait()
    lay_blocks(raw[0, 0], full_ref)


def tail_kernel(size, full_ref, out_ref):
    height = BS // 2
    tiles = (out_ref.shape[0] - NOTE) // height
    for t in range(tiles):
        first = pl.multiple_of(size + t * BS + core_parity() * height, height)
        out_ref[t * height : (t + 1) * height] = full_ref[pl.ds(first, height)]
    out_ref[tiles * height :] = full_ref[full_ref.shape[0] - NOTE :]


def lean_kernel(full_ref, tail_ref, out_ref):
    size = out_ref.shape[0] - NOTE
    out_ref[:size] = full_ref[:size]
    out_ref[size:] = tail_ref[tail_ref.shape[0] - NOTE :]


def relay_kernel(slots, aux_width, raw, full_ref, out_ref, left_ref):
    lay_blocks(raw[0, 0], out_ref)
    size = out_ref.shape[0]
    own = jnp.concatenate([full_ref[at : at + BS] for at in range(0, size, BS)], axis=1)
    for p in range(aux_width):
        cuts = [(j * aux_width + p) * BS for j in range(slots)]
        left_ref[p * BS : (p + 1) * BS] = jnp.concatenate(
            [own[:, cut : cut + BS] for cut in cuts], axis=1
        )


def merge_kernel(size, *refs):
    parts, out_ref = refs[:-1], refs[-1]
    at = 0
    for i, part in enumerate(parts):
        first = size if i < len(parts) - 1 else 0
        count = part.shape[0] - NOTE - first
        out_ref[at : at + count] = part[first : first + count]
        at += count


def exchange_kernel(
    orb, slots, aux_width, meta_ref, density_ref, left_ref, tail, swapped, *refs
):
    packs, (out_ref, rows, half_ref, held) = refs[:orb], refs[orb:]
    fulls = packs[2::2]
    notes = meta_ref[...]
    meta = [notes[i] for i in range(orb * slots)]
    me = lax.axis_index("orb")
    parity = core_parity()
    sign = 1 - 2 * parity
    height = BS // 2
    count = density_ref.shape[1] // LANES
    size = slots * aux_width * BS // LANES * BS
    near = pl.multiple_of(parity * height, height)
    far = pl.multiple_of((1 - parity) * height, height)
    across = lax.rem(me + orb // 2, orb)
    owners = [me, across]
    rows[me] = density_ref[...]
    for i, full in enumerate(fulls):
        owners += [owner_of(me, i + 1, sign, orb), owner_of(me, i + 1, -sign, orb)]
        for t in range(count):
            lanes = slice(t * LANES, (t + 1) * LANES)
            at = (i * count + t) * BS
            rows[owners[-2], :, lanes] = full[size + t * BS : size + (t + 1) * BS]
            rows[owners[-1], :, lanes] = swapped[at : at + BS]
    for t in range(count):
        lanes = slice(t * LANES, (t + 1) * LANES)
        at = len(fulls) * count * BS + t * height
        rows[across, pl.ds(near, height), lanes] = tail[t * height : (t + 1) * height]
        rows[across, pl.ds(far, height), lanes] = swapped[at : at + height]
    rows[orb] = jnp.zeros_like(rows[orb])
    selected = jnp.concatenate([rows[meta[j]] for j in range(slots)], axis=0)
    half = jnp.dot(left_ref[...], selected, preferred_element_type=jnp.float32)
    half = half.astype(jnp.bfloat16)
    for k in range(orb):
        half_ref[k] = jnp.concatenate(
            [half[p * BS : (p + 1) * BS, k * BS : (k + 1) * BS] for p in range(aux_width)],
            axis=1,
        )
    half_ref[orb] = jnp.zeros_like(half_ref[orb])
    for way in range(orb):
        codes = meta[way * slots : (way + 1) * slots]
        held[owners[way]] = lax.dot_general(
            jnp.concatenate([half_ref[code] for code in codes], axis=1),
            jnp.concatenate([packs[way][at : at + BS] for at in range(0, size, BS)], axis=1),
            (((1,), (1,)), ((), ())),
            preferred_element_type=jnp.float32,
        )
    out_ref[...] = jnp.concatenate([held[n] for n in range(orb)], axis=1)


def shards(density, tensor_blocks, pairs, kept):
    full_width = density.shape[1]
    slots = tensor_blocks.shape[2]
    aux_width = tensor_blocks.shape[3]
    orb = lax.axis_size("orb")
    aux = lax.axis_size("aux")
    rows = full_width // LANES * BS
    size = slots * aux_width * BS // LANES * BS
    vmem = pl.BlockSpec(memory_space=pltpu.VMEM)
    smem = pl.BlockSpec(memory_space=pltpu.SMEM)
    hbm = pl.BlockSpec(memory_space=pltpu.HBM)
    params = pltpu.CompilerParams(vmem_limit_bytes=32 * 1024 * 1024)

    def array(height):
        return jax.ShapeDtypeStruct((height, LANES), jnp.bfloat16)

    def shift(x, step, sign):
        perm = [
            (a * orb + o, a * orb + partner(o, step, sign * (1 - 2 * (a % 2)), orb))
            for a in range(aux)
            for o in range(orb)
        ]
        return lax.ppermute(x, ("aux", "orb"), perm)

    full = pl.pallas_call(
        functools.partial(pack_kernel, orb),
        out_shape=array(size + rows + NOTE),
        in_specs=[smem, hbm, hbm, hbm],
        out_specs=vmem,
        scratch_shapes=[
            pltpu.SMEM(pairs.shape, jnp.int32),
            pltpu.VMEM(density.shape, jnp.bfloat16),
            pltpu.VMEM(tensor_blocks.shape, jnp.bfloat16),
            pltpu.SemaphoreType.DMA((3,)),
        ],
        compiler_params=params,
        name="pack",
    )(
        kept,
        *(pltpu.with_memory_space_constraint(a, pltpu.HBM) for a in (pairs, density, tensor_blocks)),
    )
    tail = pl.pallas_call(
        functools.partial(tail_kernel, size),
        out_shape=array(rows // 2 + NOTE),
        in_specs=[vmem],
        out_specs=vmem,
        compiler_params=params,
        name="tail",
    )(full)
    lean = pl.pallas_call(
        lean_kernel,
        out_shape=array(size + NOTE),
        in_specs=[vmem] * 2,
        out_specs=vmem,
        compiler_params=params,
        name="lean",
    )(full, tail)
    across = [(i, (i + orb // 2) % orb) for i in range(orb)]
    raw = lax.ppermute(tensor_blocks, "orb", across)
    tail_in = lax.ppermute(tail, "orb", across)
    fulls = [shift(full, i, 1) for i in range(1, orb // 2)]
    leans = [shift(lean, i, -1) for i in range(1, orb // 2)]

    tail_in, raw = lax.optimization_barrier((tail_in, raw))
    merged = pl.pallas_call(
        functools.partial(merge_kernel, size),
        out_shape=array(len(fulls) * rows + rows // 2),
        in_specs=[vmem] * (len(fulls) + 1),
        out_specs=vmem,
        compiler_params=params,
        name="merge",
    )(*fulls, tail_in)
    swapped = lax.ppermute(merged, "aux", [(i, i ^ 1) for i in range(aux)])
    across, left = pl.pallas_call(
        functools.partial(relay_kernel, slots, aux_width),
        out_shape=[
            array(size),
            jax.ShapeDtypeStruct((aux_width * BS, slots * BS), jnp.bfloat16),
        ],
        in_specs=[vmem] * 2,
        out_specs=[vmem] * 2,
        compiler_params=params,
        name="relay",
    )(raw, full)
    swapped, leans = lax.optimization_barrier((swapped, leans))
    packs, notes = [full, across], [tail, tail_in]
    for pair in zip(fulls, leans):
        packs += pair
        notes += pair
    codes = jnp.concatenate([n[-NOTE, :slots] for n in notes]).astype(jnp.int32)
    parts = pl.pallas_call(
        functools.partial(exchange_kernel, orb, slots, aux_width),
        out_shape=jax.ShapeDtypeStruct((BS, full_width), jnp.float32),
        in_specs=[vmem] * (orb + 5),
        out_specs=vmem,
        scratch_shapes=[
            pltpu.VMEM((orb + 1, BS, full_width), jnp.bfloat16),
            pltpu.VMEM((orb + 1, BS, aux_width * BS), jnp.bfloat16),
            pltpu.VMEM((orb, BS, BS), jnp.float32),
        ],
        compiler_params=params,
        name="exchange",
    )(codes, density, left, tail_in, swapped, *packs)

    step = 1
    while step < aux:
        ways = 2 if step == 1 or step * 4 > aux else 4
        terms = [parts]
        for way in range(1, ways):
            terms.append(lax.ppermute(parts, "aux", [(i, i ^ (way * step)) for i in range(aux)]))
        while len(terms) > 1:
            terms = [terms[i] + terms[i + 1] for i in range(0, len(terms), 2)]
        parts = terms[0]
        step *= ways
    return parts


def solution(mesh):
    return jax.shard_map(
        shards,
        mesh=mesh,
        in_specs=(
            P("orb", None),
            P("orb", "aux", None, None, None),
            P("orb", "aux", None),
            P("orb", "aux"),
        ),
        out_specs=P("orb", None),
        check_vma=False,
    )
```

```python
import functools

import jax
import jax.numpy as jnp
from jax import lax
from jax.experimental import pallas as pl
from jax.experimental.pallas import tpu as pltpu
from jax.sharding import PartitionSpec as P

BS = 64
LANES = 128
NOTE = 8


def lay_blocks(raw, out_ref):
    slots, aux_width = raw.shape[:2]
    square = raw.reshape(slots * aux_width, BS, BS)
    for tile in range(slots * aux_width // 2):
        both = jnp.concatenate([square[2 * tile], square[2 * tile + 1]], axis=1)
        out_ref[tile * BS : (tile + 1) * BS] = both
    return slots * aux_width // 2


def partner(i, step, sign, orb):
    if orb == 4:
        return i ^ (2 - sign)
    return (i + sign * step) % orb


def owner_of(me, step, sign, orb):
    if orb == 4:
        return me ^ (2 - sign)
    return lax.rem(me - sign * step + orb, orb)


def core_parity():
    return lax.rem(lax.axis_index("aux"), 2)


def pack_kernel(
    orb, kept, pairs_hbm, density_hbm, raw_hbm, full_ref, pairs, rows, raw, sems
):
    copies = [
        pltpu.make_async_copy(src, dst, sems.at[i])
        for i, (src, dst) in enumerate(((raw_hbm, raw), (density_hbm, rows), (pairs_hbm, pairs)))
    ]
    for copy in copies:
        copy.start()
    for copy in copies[1:]:
        copy.wait()
    tiles = rows.shape[1] // LANES
    size = full_ref.shape[0] - tiles * BS - NOTE
    for t in range(tiles):
        lanes = slice(t * LANES, (t + 1) * LANES)
        full_ref[size + t * BS : size + (t + 1) * BS] = rows[:, lanes]
    shape = (NOTE, LANES)
    lane = lax.broadcasted_iota(jnp.int32, shape, 1)
    note = jnp.zeros(shape, jnp.int32)
    for j in range(pairs.shape[2]):
        note = jnp.where(lane == j, jnp.where(j < kept[0, 0], pairs[0, 0, j], orb), note)
    full_ref[size + tiles * BS :] = note.astype(jnp.float32).astype(jnp.bfloat16)
    copies[0].wait()
    lay_blocks(raw[0, 0], full_ref)


def tail_kernel(size, full_ref, out_ref):
    height = BS // 2
    tiles = (out_ref.shape[0] - NOTE) // height
    for t in range(tiles):
        first = pl.multiple_of(size + t * BS + core_parity() * height, height)
        out_ref[t * height : (t + 1) * height] = full_ref[pl.ds(first, height)]
    out_ref[tiles * height :] = full_ref[full_ref.shape[0] - NOTE :]


def lean_kernel(full_ref, tail_ref, out_ref):
    size = out_ref.shape[0] - NOTE
    out_ref[:size] = full_ref[:size]
    out_ref[size:] = tail_ref[tail_ref.shape[0] - NOTE :]


def relay_kernel(slots, aux_width, raw, full_ref, out_ref, left_ref):
    lay_blocks(raw[0, 0], out_ref)
    size = out_ref.shape[0]
    own = jnp.concatenate([full_ref[at : at + BS] for at in range(0, size, BS)], axis=1)
    for p in range(aux_width):
        cuts = [(j * aux_width + p) * BS for j in range(slots)]
        left_ref[p * BS : (p + 1) * BS] = jnp.concatenate(
            [own[:, cut : cut + BS] for cut in cuts], axis=1
        )


def merge_kernel(size, *refs):
    parts, out_ref = refs[:-1], refs[-1]
    at = 0
    for i, part in enumerate(parts):
        first = size if i < len(parts) - 1 else 0
        count = part.shape[0] - NOTE - first
        out_ref[at : at + count] = part[first : first + count]
        at += count


def exchange_kernel(
    orb, slots, aux_width, meta_ref, density_ref, left_ref, tail, swapped, *refs
):
    packs, (out_ref, rows, half_ref, held) = refs[:orb], refs[orb:]
    fulls = packs[2::2]
    notes = meta_ref[...]
    meta = [notes[i] for i in range(orb * slots)]
    me = lax.axis_index("orb")
    parity = core_parity()
    sign = 1 - 2 * parity
    height = BS // 2
    count = density_ref.shape[1] // LANES
    size = slots * aux_width * BS // LANES * BS
    near = pl.multiple_of(parity * height, height)
    far = pl.multiple_of((1 - parity) * height, height)
    across = lax.rem(me + orb // 2, orb)
    owners = [me, across]
    rows[me] = density_ref[...]
    for i, full in enumerate(fulls):
        owners += [owner_of(me, i + 1, sign, orb), owner_of(me, i + 1, -sign, orb)]
        for t in range(count):
            lanes = slice(t * LANES, (t + 1) * LANES)
            at = (i * count + t) * BS
            rows[owners[-2], :, lanes] = full[size + t * BS : size + (t + 1) * BS]
            rows[owners[-1], :, lanes] = swapped[at : at + BS]
    for t in range(count):
        lanes = slice(t * LANES, (t + 1) * LANES)
        at = len(fulls) * count * BS + t * height
        rows[across, pl.ds(near, height), lanes] = tail[t * height : (t + 1) * height]
        rows[across, pl.ds(far, height), lanes] = swapped[at : at + height]
    rows[orb] = jnp.zeros_like(rows[orb])
    selected = jnp.concatenate([rows[meta[j]] for j in range(slots)], axis=0)
    half = jnp.dot(left_ref[...], selected, preferred_element_type=jnp.float32)
    half = half.astype(jnp.bfloat16)
    for k in range(orb):
        half_ref[k] = jnp.concatenate(
            [half[p * BS : (p + 1) * BS, k * BS : (k + 1) * BS] for p in range(aux_width)],
            axis=1,
        )
    half_ref[orb] = jnp.zeros_like(half_ref[orb])
    depth = aux_width * BS // LANES
    for way in range(orb):
        total = None
        for j in range(slots):
            first = j * depth * BS
            tiles = [packs[way][at : at + BS] for at in range(first, first + depth * BS, BS)]
            term = lax.dot_general(
                half_ref[meta[way * slots + j]],
                jnp.concatenate(tiles, axis=1),
                (((1,), (1,)), ((), ())),
                preferred_element_type=jnp.float32,
            )
            total = term if total is None else total + term
        held[owners[way]] = total
    out_ref[...] = jnp.concatenate([held[n] for n in range(orb)], axis=1)


def shards(density, tensor_blocks, pairs, kept):
    full_width = density.shape[1]
    slots = tensor_blocks.shape[2]
    aux_width = tensor_blocks.shape[3]
    orb = lax.axis_size("orb")
    aux = lax.axis_size("aux")
    rows = full_width // LANES * BS
    size = slots * aux_width * BS // LANES * BS
    vmem = pl.BlockSpec(memory_space=pltpu.VMEM)
    smem = pl.BlockSpec(memory_space=pltpu.SMEM)
    hbm = pl.BlockSpec(memory_space=pltpu.HBM)
    params = pltpu.CompilerParams(vmem_limit_bytes=32 * 1024 * 1024)

    def array(height):
        return jax.ShapeDtypeStruct((height, LANES), jnp.bfloat16)

    def shift(x, step, sign):
        perm = [
            (a * orb + o, a * orb + partner(o, step, sign * (1 - 2 * (a % 2)), orb))
            for a in range(aux)
            for o in range(orb)
        ]
        return lax.ppermute(x, ("aux", "orb"), perm)

    full = pl.pallas_call(
        functools.partial(pack_kernel, orb),
        out_shape=array(size + rows + NOTE),
        in_specs=[smem, hbm, hbm, hbm],
        out_specs=vmem,
        scratch_shapes=[
            pltpu.SMEM(pairs.shape, jnp.int32),
            pltpu.VMEM(density.shape, jnp.bfloat16),
            pltpu.VMEM(tensor_blocks.shape, jnp.bfloat16),
            pltpu.SemaphoreType.DMA((3,)),
        ],
        compiler_params=params,
        name="pack",
    )(
        kept,
        *(pltpu.with_memory_space_constraint(a, pltpu.HBM) for a in (pairs, density, tensor_blocks)),
    )
    tail = pl.pallas_call(
        functools.partial(tail_kernel, size),
        out_shape=array(rows // 2 + NOTE),
        in_specs=[vmem],
        out_specs=vmem,
        compiler_params=params,
        name="tail",
    )(full)
    lean = pl.pallas_call(
        lean_kernel,
        out_shape=array(size + NOTE),
        in_specs=[vmem] * 2,
        out_specs=vmem,
        compiler_params=params,
        name="lean",
    )(full, tail)
    across = [(i, (i + orb // 2) % orb) for i in range(orb)]
    raw = lax.ppermute(tensor_blocks, "orb", across)
    tail_in = lax.ppermute(tail, "orb", across)
    fulls = [shift(full, i, 1) for i in range(1, orb // 2)]
    leans = [shift(lean, i, -1) for i in range(1, orb // 2)]

    tail_in, raw = lax.optimization_barrier((tail_in, raw))
    merged = pl.pallas_call(
        functools.partial(merge_kernel, size),
        out_shape=array(len(fulls) * rows + rows // 2),
        in_specs=[vmem] * (len(fulls) + 1),
        out_specs=vmem,
        compiler_params=params,
        name="merge",
    )(*fulls, tail_in)
    swapped = lax.ppermute(merged, "aux", [(i, i ^ 1) for i in range(aux)])
    across, left = pl.pallas_call(
        functools.partial(relay_kernel, slots, aux_width),
        out_shape=[
            array(size),
            jax.ShapeDtypeStruct((aux_width * BS, slots * BS), jnp.bfloat16),
        ],
        in_specs=[vmem] * 2,
        out_specs=[vmem] * 2,
        compiler_params=params,
        name="relay",
    )(raw, full)
    swapped, leans = lax.optimization_barrier((swapped, leans))
    packs, notes = [full, across], [tail, tail_in]
    for pair in zip(fulls, leans):
        packs += pair
        notes += pair
    codes = jnp.concatenate([n[-NOTE, :slots] for n in notes]).astype(jnp.int32)
    parts = pl.pallas_call(
        functools.partial(exchange_kernel, orb, slots, aux_width),
        out_shape=jax.ShapeDtypeStruct((BS, full_width), jnp.float32),
        in_specs=[vmem] * (orb + 5),
        out_specs=vmem,
        scratch_shapes=[
            pltpu.VMEM((orb + 1, BS, full_width), jnp.bfloat16),
            pltpu.VMEM((orb + 1, BS, aux_width * BS), jnp.bfloat16),
            pltpu.VMEM((orb, BS, BS), jnp.float32),
        ],
        compiler_params=params,
        name="exchange",
    )(codes, density, left, tail_in, swapped, *packs)

    step = 1
    while step < aux:
        ways = 2 if step == 1 or step * 4 > aux else 4
        if step == 2:
            parts = parts.astype(jnp.bfloat16)
        terms = [parts]
        for way in range(1, ways):
            terms.append(lax.ppermute(parts, "aux", [(i, i ^ (way * step)) for i in range(aux)]))
        terms = [term.astype(jnp.float32) for term in terms]
        while len(terms) > 1:
            terms = [terms[i] + terms[i + 1] for i in range(0, len(terms), 2)]
        parts = terms[0]
        step *= ways
    return parts


def solution(mesh):
    return jax.shard_map(
        shards,
        mesh=mesh,
        in_specs=(
            P("orb", None),
            P("orb", "aux", None, None, None),
            P("orb", "aux", None),
            P("orb", "aux"),
        ),
        out_specs=P("orb", None),
        check_vma=False,
    )
```

```python
import functools

import jax
import jax.numpy as jnp
from jax import lax
from jax.experimental import pallas as pl
from jax.experimental.pallas import tpu as pltpu
from jax.sharding import PartitionSpec as P

BS = 64
LANES = 128
NOTE = 8


def lay_blocks(raw, out_ref):
    slots, aux_width = raw.shape[:2]
    square = raw.reshape(slots * aux_width, BS, BS)
    for tile in range(slots * aux_width // 2):
        both = jnp.concatenate([square[2 * tile], square[2 * tile + 1]], axis=1)
        out_ref[tile * BS : (tile + 1) * BS] = both
    return slots * aux_width // 2


def partner(i, step, sign, orb):
    if orb == 4:
        return i ^ (2 - sign)
    return (i + sign * step) % orb


def owner_of(me, step, sign, orb):
    if orb == 4:
        return me ^ (2 - sign)
    return lax.rem(me - sign * step + orb, orb)


def core_parity():
    return lax.rem(lax.axis_index("aux"), 2)


def pack_kernel(
    orb, kept, pairs_hbm, density_hbm, raw_hbm, full_ref, pairs, rows, raw, sems
):
    copies = [
        pltpu.make_async_copy(src, dst, sems.at[i])
        for i, (src, dst) in enumerate(((raw_hbm, raw), (density_hbm, rows), (pairs_hbm, pairs)))
    ]
    for copy in copies:
        copy.start()
    for copy in copies[1:]:
        copy.wait()
    tiles = rows.shape[1] // LANES
    size = full_ref.shape[0] - tiles * BS - NOTE
    for t in range(tiles):
        lanes = slice(t * LANES, (t + 1) * LANES)
        full_ref[size + t * BS : size + (t + 1) * BS] = rows[:, lanes]
    shape = (NOTE, LANES)
    lane = lax.broadcasted_iota(jnp.int32, shape, 1)
    note = jnp.zeros(shape, jnp.int32)
    for j in range(pairs.shape[2]):
        note = jnp.where(lane == j, jnp.where(j < kept[0, 0], pairs[0, 0, j], orb), note)
    full_ref[size + tiles * BS :] = note.astype(jnp.float32).astype(jnp.bfloat16)
    copies[0].wait()
    lay_blocks(raw[0, 0], full_ref)


def tail_kernel(size, full_ref, out_ref):
    height = BS // 2
    tiles = (out_ref.shape[0] - NOTE) // height
    for t in range(tiles):
        first = pl.multiple_of(size + t * BS + core_parity() * height, height)
        out_ref[t * height : (t + 1) * height] = full_ref[pl.ds(first, height)]
    out_ref[tiles * height :] = full_ref[full_ref.shape[0] - NOTE :]


def lean_kernel(full_ref, tail_ref, out_ref):
    size = out_ref.shape[0] - NOTE
    out_ref[:size] = full_ref[:size]
    out_ref[size:] = tail_ref[tail_ref.shape[0] - NOTE :]


def turn(ref, size):
    joined = jnp.concatenate([ref[at : at + BS] for at in range(0, size, BS)], axis=1)
    return joined.astype(jnp.float32).T.astype(jnp.bfloat16)


def relay_kernel(slots, aux_width, raw, full_ref, out_ref, left_ref, own_ref, laid):
    lay_blocks(raw[0, 0], laid)
    size = laid.shape[0]
    out_ref[...] = turn(laid, size)
    own_ref[...] = turn(full_ref, size)
    own = jnp.concatenate([full_ref[at : at + BS] for at in range(0, size, BS)], axis=1)
    for p in range(aux_width):
        cuts = [(j * aux_width + p) * BS for j in range(slots)]
        left_ref[p * BS : (p + 1) * BS] = jnp.concatenate(
            [own[:, cut : cut + BS] for cut in cuts], axis=1
        )


def merge_kernel(size, *refs):
    parts, out_ref = refs[:-1], refs[-1]
    at = 0
    for i, part in enumerate(parts):
        first = size if i < len(parts) - 1 else 0
        count = part.shape[0] - NOTE - first
        out_ref[at : at + count] = part[first : first + count]
        at += count


def exchange_kernel(
    orb, slots, aux_width, meta_ref, density_ref, left_ref, tail, swapped, *refs
):
    turned, packs = refs[:2], (None, None, *refs[2:orb])
    out_ref, rows, half_ref, held = refs[orb:]
    fulls = packs[2::2]
    notes = meta_ref[...]
    meta = [notes[i] for i in range(orb * slots)]
    me = lax.axis_index("orb")
    parity = core_parity()
    sign = 1 - 2 * parity
    height = BS // 2
    count = density_ref.shape[1] // LANES
    size = slots * aux_width * BS // LANES * BS
    near = pl.multiple_of(parity * height, height)
    far = pl.multiple_of((1 - parity) * height, height)
    across = lax.rem(me + orb // 2, orb)
    owners = [me, across]
    rows[me] = density_ref[...]
    for i, full in enumerate(fulls):
        owners += [owner_of(me, i + 1, sign, orb), owner_of(me, i + 1, -sign, orb)]
        for t in range(count):
            lanes = slice(t * LANES, (t + 1) * LANES)
            at = (i * count + t) * BS
            rows[owners[-2], :, lanes] = full[size + t * BS : size + (t + 1) * BS]
            rows[owners[-1], :, lanes] = swapped[at : at + BS]
    for t in range(count):
        lanes = slice(t * LANES, (t + 1) * LANES)
        at = len(fulls) * count * BS + t * height
        rows[across, pl.ds(near, height), lanes] = tail[t * height : (t + 1) * height]
        rows[across, pl.ds(far, height), lanes] = swapped[at : at + height]
    rows[orb] = jnp.zeros_like(rows[orb])
    selected = jnp.concatenate([rows[meta[j]] for j in range(slots)], axis=0)
    half = jnp.dot(left_ref[...], selected, preferred_element_type=jnp.float32)
    half = half.astype(jnp.bfloat16)
    for k in range(orb):
        half_ref[k] = jnp.concatenate(
            [half[p * BS : (p + 1) * BS, k * BS : (k + 1) * BS] for p in range(aux_width)],
            axis=1,
        )
    half_ref[orb] = jnp.zeros_like(half_ref[orb])
    for way in range(orb):
        codes = meta[way * slots : (way + 1) * slots]
        joined = jnp.concatenate([half_ref[code] for code in codes], axis=1)
        if way < 2:
            held[owners[way]] = jnp.dot(
                joined, turned[way][...], preferred_element_type=jnp.float32
            )
            continue
        held[owners[way]] = lax.dot_general(
            joined,
            jnp.concatenate([packs[way][at : at + BS] for at in range(0, size, BS)], axis=1),
            (((1,), (1,)), ((), ())),
            preferred_element_type=jnp.float32,
        )
    out_ref[...] = jnp.concatenate([held[n] for n in range(orb)], axis=1)


def shards(density, tensor_blocks, pairs, kept):
    full_width = density.shape[1]
    slots = tensor_blocks.shape[2]
    aux_width = tensor_blocks.shape[3]
    orb = lax.axis_size("orb")
    aux = lax.axis_size("aux")
    rows = full_width // LANES * BS
    size = slots * aux_width * BS // LANES * BS
    vmem = pl.BlockSpec(memory_space=pltpu.VMEM)
    smem = pl.BlockSpec(memory_space=pltpu.SMEM)
    hbm = pl.BlockSpec(memory_space=pltpu.HBM)
    params = pltpu.CompilerParams(vmem_limit_bytes=32 * 1024 * 1024)

    def array(height):
        return jax.ShapeDtypeStruct((height, LANES), jnp.bfloat16)

    def shift(x, step, sign):
        perm = [
            (a * orb + o, a * orb + partner(o, step, sign * (1 - 2 * (a % 2)), orb))
            for a in range(aux)
            for o in range(orb)
        ]
        return lax.ppermute(x, ("aux", "orb"), perm)

    full = pl.pallas_call(
        functools.partial(pack_kernel, orb),
        out_shape=array(size + rows + NOTE),
        in_specs=[smem, hbm, hbm, hbm],
        out_specs=vmem,
        scratch_shapes=[
            pltpu.SMEM(pairs.shape, jnp.int32),
            pltpu.VMEM(density.shape, jnp.bfloat16),
            pltpu.VMEM(tensor_blocks.shape, jnp.bfloat16),
            pltpu.SemaphoreType.DMA((3,)),
        ],
        compiler_params=params,
        name="pack",
    )(
        kept,
        *(pltpu.with_memory_space_constraint(a, pltpu.HBM) for a in (pairs, density, tensor_blocks)),
    )
    tail = pl.pallas_call(
        functools.partial(tail_kernel, size),
        out_shape=array(rows // 2 + NOTE),
        in_specs=[vmem],
        out_specs=vmem,
        compiler_params=params,
        name="tail",
    )(full)
    lean = pl.pallas_call(
        lean_kernel,
        out_shape=array(size + NOTE),
        in_specs=[vmem] * 2,
        out_specs=vmem,
        compiler_params=params,
        name="lean",
    )(full, tail)
    across = [(i, (i + orb // 2) % orb) for i in range(orb)]
    raw = lax.ppermute(tensor_blocks, "orb", across)
    tail_in = lax.ppermute(tail, "orb", across)
    fulls = [shift(full, i, 1) for i in range(1, orb // 2)]
    leans = [shift(lean, i, -1) for i in range(1, orb // 2)]

    tail_in, raw = lax.optimization_barrier((tail_in, raw))
    merged = pl.pallas_call(
        functools.partial(merge_kernel, size),
        out_shape=array(len(fulls) * rows + rows // 2),
        in_specs=[vmem] * (len(fulls) + 1),
        out_specs=vmem,
        compiler_params=params,
        name="merge",
    )(*fulls, tail_in)
    swapped = lax.ppermute(merged, "aux", [(i, i ^ 1) for i in range(aux)])
    across, left, own = pl.pallas_call(
        functools.partial(relay_kernel, slots, aux_width),
        out_shape=[
            jax.ShapeDtypeStruct((slots * aux_width * BS, BS), jnp.bfloat16),
            jax.ShapeDtypeStruct((aux_width * BS, slots * BS), jnp.bfloat16),
            jax.ShapeDtypeStruct((slots * aux_width * BS, BS), jnp.bfloat16),
        ],
        in_specs=[vmem] * 2,
        out_specs=[vmem] * 3,
        scratch_shapes=[pltpu.VMEM((size, LANES), jnp.bfloat16)],
        compiler_params=params,
        name="relay",
    )(raw, full)
    swapped, leans = lax.optimization_barrier((swapped, leans))
    packs, notes = [own, across], [tail, tail_in]
    for pair in zip(fulls, leans):
        packs += pair
        notes += pair
    codes = jnp.concatenate([n[-NOTE, :slots] for n in notes]).astype(jnp.int32)
    parts = pl.pallas_call(
        functools.partial(exchange_kernel, orb, slots, aux_width),
        out_shape=jax.ShapeDtypeStruct((BS, full_width), jnp.float32),
        in_specs=[vmem] * (orb + 5),
        out_specs=vmem,
        scratch_shapes=[
            pltpu.VMEM((orb + 1, BS, full_width), jnp.bfloat16),
            pltpu.VMEM((orb + 1, BS, aux_width * BS), jnp.bfloat16),
            pltpu.VMEM((orb, BS, BS), jnp.float32),
        ],
        compiler_params=params,
        name="exchange",
    )(codes, density, left, tail_in, swapped, *packs)

    step = 1
    while step < aux:
        ways = 2 if step == 1 or step * 4 > aux else 4
        if step == 2:
            parts = parts.astype(jnp.bfloat16)
        terms = [parts]
        for way in range(1, ways):
            terms.append(lax.ppermute(parts, "aux", [(i, i ^ (way * step)) for i in range(aux)]))
        terms = [term.astype(jnp.float32) for term in terms]
        while len(terms) > 1:
            terms = [terms[i] + terms[i + 1] for i in range(0, len(terms), 2)]
        parts = terms[0]
        step *= ways
    return parts


def solution(mesh):
    return jax.shard_map(
        shards,
        mesh=mesh,
        in_specs=(
            P("orb", None),
            P("orb", "aux", None, None, None),
            P("orb", "aux", None),
            P("orb", "aux"),
        ),
        out_specs=P("orb", None),
        check_vma=False,
    )
```

```python
import functools

import jax
import jax.numpy as jnp
from jax import lax
from jax.experimental import pallas as pl
from jax.experimental.pallas import tpu as pltpu
from jax.sharding import PartitionSpec as P

BS = 64
LANES = 128
NOTE = 8


def lay_blocks(raw, out_ref):
    slots, aux_width = raw.shape[:2]
    square = raw.reshape(slots * aux_width, BS, BS)
    for tile in range(slots * aux_width // 2):
        both = jnp.concatenate([square[2 * tile], square[2 * tile + 1]], axis=1)
        out_ref[tile * BS : (tile + 1) * BS] = both
    return slots * aux_width // 2


def partner(i, step, sign, orb):
    if orb == 4:
        return i ^ (2 - sign)
    return (i + sign * step) % orb


def owner_of(me, step, sign, orb):
    if orb == 4:
        return me ^ (2 - sign)
    return lax.rem(me - sign * step + orb, orb)


def core_parity():
    return lax.rem(lax.axis_index("aux"), 2)


def pack_kernel(
    orb, kept, pairs_hbm, density_hbm, raw_hbm, full_ref, pairs, rows, raw, sems
):
    copies = [
        pltpu.make_async_copy(src, dst, sems.at[i])
        for i, (src, dst) in enumerate(((raw_hbm, raw), (density_hbm, rows), (pairs_hbm, pairs)))
    ]
    for copy in copies:
        copy.start()
    for copy in copies[1:]:
        copy.wait()
    tiles = rows.shape[1] // LANES
    size = full_ref.shape[0] - tiles * BS - NOTE
    for t in range(tiles):
        lanes = slice(t * LANES, (t + 1) * LANES)
        full_ref[size + t * BS : size + (t + 1) * BS] = rows[:, lanes]
    shape = (NOTE, LANES)
    lane = lax.broadcasted_iota(jnp.int32, shape, 1)
    note = jnp.zeros(shape, jnp.int32)
    for j in range(pairs.shape[2]):
        note = jnp.where(lane == j, jnp.where(j < kept[0, 0], pairs[0, 0, j], orb), note)
    full_ref[size + tiles * BS :] = note.astype(jnp.float32).astype(jnp.bfloat16)
    copies[0].wait()
    lay_blocks(raw[0, 0], full_ref)


def tail_kernel(size, full_ref, out_ref):
    height = BS // 2
    tiles = (out_ref.shape[0] - NOTE) // height
    for t in range(tiles):
        first = pl.multiple_of(size + t * BS + core_parity() * height, height)
        out_ref[t * height : (t + 1) * height] = full_ref[pl.ds(first, height)]
    out_ref[tiles * height :] = full_ref[full_ref.shape[0] - NOTE :]


def lean_kernel(full_ref, tail_ref, out_ref):
    size = out_ref.shape[0] - NOTE
    out_ref[:size] = full_ref[:size]
    out_ref[size:] = tail_ref[tail_ref.shape[0] - NOTE :]


def relay_kernel(slots, aux_width, raw, full_ref, out_ref, left_ref):
    lay_blocks(raw[0, 0], out_ref)
    size = out_ref.shape[0]
    own = jnp.concatenate([full_ref[at : at + BS] for at in range(0, size, BS)], axis=1)
    for p in range(aux_width):
        cuts = [(j * aux_width + p) * BS for j in range(slots)]
        left_ref[p * BS : (p + 1) * BS] = jnp.concatenate(
            [own[:, cut : cut + BS] for cut in cuts], axis=1
        )


def merge_kernel(size, *refs):
    parts, out_ref = refs[:-1], refs[-1]
    at = 0
    for i, part in enumerate(parts):
        first = size if i < len(parts) - 1 else 0
        count = part.shape[0] - NOTE - first
        out_ref[at : at + count] = part[first : first + count]
        at += count


def exchange_kernel(
    orb, slots, aux_width, meta_ref, density_ref, left_ref, tail, swapped, *refs
):
    packs, (out_ref, rows, half_ref, held) = refs[:orb], refs[orb:]
    fulls = packs[2::2]
    notes = meta_ref[...]
    meta = [notes[i] for i in range(orb * slots)]
    me = lax.axis_index("orb")
    parity = core_parity()
    sign = 1 - 2 * parity
    height = BS // 2
    count = density_ref.shape[1] // LANES
    size = slots * aux_width * BS // LANES * BS
    near = pl.multiple_of(parity * height, height)
    far = pl.multiple_of((1 - parity) * height, height)
    across = lax.rem(me + orb // 2, orb)
    owners = [me, across]
    rows[me] = density_ref[...]
    for i, full in enumerate(fulls):
        owners += [owner_of(me, i + 1, sign, orb), owner_of(me, i + 1, -sign, orb)]
        for t in range(count):
            lanes = slice(t * LANES, (t + 1) * LANES)
            at = (i * count + t) * BS
            rows[owners[-2], :, lanes] = full[size + t * BS : size + (t + 1) * BS]
            rows[owners[-1], :, lanes] = swapped[at : at + BS]
    for t in range(count):
        lanes = slice(t * LANES, (t + 1) * LANES)
        at = len(fulls) * count * BS + t * height
        rows[across, pl.ds(near, height), lanes] = tail[t * height : (t + 1) * height]
        rows[across, pl.ds(far, height), lanes] = swapped[at : at + height]
    rows[orb] = jnp.zeros_like(rows[orb])
    selected = jnp.concatenate([rows[meta[j]] for j in range(slots)], axis=0)
    half = jnp.dot(left_ref[...], selected, preferred_element_type=jnp.float32)
    half = half.astype(jnp.bfloat16)
    for k in range(orb):
        half_ref[k] = jnp.concatenate(
            [half[p * BS : (p + 1) * BS, k * BS : (k + 1) * BS] for p in range(aux_width)],
            axis=1,
        )
    half_ref[orb] = jnp.zeros_like(half_ref[orb])
    for way in range(orb):
        codes = meta[way * slots : (way + 1) * slots]
        held[owners[way]] = lax.dot_general(
            jnp.concatenate([half_ref[code] for code in codes], axis=1),
            jnp.concatenate([packs[way][at : at + BS] for at in range(0, size, BS)], axis=1),
            (((1,), (1,)), ((), ())),
            preferred_element_type=jnp.float32,
        )
    out_ref[...] = jnp.concatenate([held[n] for n in range(orb)], axis=1)


def shards(density, tensor_blocks, pairs, kept):
    full_width = density.shape[1]
    slots = tensor_blocks.shape[2]
    aux_width = tensor_blocks.shape[3]
    orb = lax.axis_size("orb")
    aux = lax.axis_size("aux")
    rows = full_width // LANES * BS
    size = slots * aux_width * BS // LANES * BS
    vmem = pl.BlockSpec(memory_space=pltpu.VMEM)
    smem = pl.BlockSpec(memory_space=pltpu.SMEM)
    hbm = pl.BlockSpec(memory_space=pltpu.HBM)
    params = pltpu.CompilerParams(vmem_limit_bytes=32 * 1024 * 1024)

    def array(height):
        return jax.ShapeDtypeStruct((height, LANES), jnp.bfloat16)

    def shift(x, step, sign):
        perm = [
            (a * orb + o, a * orb + partner(o, step, sign * (1 - 2 * (a % 2)), orb))
            for a in range(aux)
            for o in range(orb)
        ]
        return lax.ppermute(x, ("aux", "orb"), perm)

    full = pl.pallas_call(
        functools.partial(pack_kernel, orb),
        out_shape=array(size + rows + NOTE),
        in_specs=[smem, hbm, hbm, hbm],
        out_specs=vmem,
        scratch_shapes=[
            pltpu.SMEM(pairs.shape, jnp.int32),
            pltpu.VMEM(density.shape, jnp.bfloat16),
            pltpu.VMEM(tensor_blocks.shape, jnp.bfloat16),
            pltpu.SemaphoreType.DMA((3,)),
        ],
        compiler_params=params,
        name="pack",
    )(
        kept,
        *(pltpu.with_memory_space_constraint(a, pltpu.HBM) for a in (pairs, density, tensor_blocks)),
    )
    tail = pl.pallas_call(
        functools.partial(tail_kernel, size),
        out_shape=array(rows // 2 + NOTE),
        in_specs=[vmem],
        out_specs=vmem,
        compiler_params=params,
        name="tail",
    )(full)
    lean = pl.pallas_call(
        lean_kernel,
        out_shape=array(size + NOTE),
        in_specs=[vmem] * 2,
        out_specs=vmem,
        compiler_params=params,
        name="lean",
    )(full, tail)
    across = [(i, (i + orb // 2) % orb) for i in range(orb)]
    raw = lax.ppermute(tensor_blocks, "orb", across)
    tail_in = lax.ppermute(tail, "orb", across)
    fulls = [shift(full, i, 1) for i in range(1, orb // 2)]
    leans = [shift(lean, i, -1) for i in range(1, orb // 2)]

    tail_in, raw = lax.optimization_barrier((tail_in, raw))
    merged = pl.pallas_call(
        functools.partial(merge_kernel, size),
        out_shape=array(len(fulls) * rows + rows // 2),
        in_specs=[vmem] * (len(fulls) + 1),
        out_specs=vmem,
        compiler_params=params,
        name="merge",
    )(*fulls, tail_in)
    swapped = lax.ppermute(merged, "aux", [(i, i ^ 1) for i in range(aux)])
    across, left = pl.pallas_call(
        functools.partial(relay_kernel, slots, aux_width),
        out_shape=[
            array(size),
            jax.ShapeDtypeStruct((aux_width * BS, slots * BS), jnp.bfloat16),
        ],
        in_specs=[vmem] * 2,
        out_specs=[vmem] * 2,
        compiler_params=params,
        name="relay",
    )(raw, full)
    swapped, leans = lax.optimization_barrier((swapped, leans))
    packs, notes = [full, across], [tail, tail_in]
    for pair in zip(fulls, leans):
        packs += pair
        notes += pair
    codes = jnp.concatenate([n[-NOTE, :slots] for n in notes]).astype(jnp.int32)
    parts = pl.pallas_call(
        functools.partial(exchange_kernel, orb, slots, aux_width),
        out_shape=jax.ShapeDtypeStruct((BS, full_width), jnp.float32),
        in_specs=[vmem] * (orb + 5),
        out_specs=vmem,
        scratch_shapes=[
            pltpu.VMEM((orb + 1, BS, full_width), jnp.bfloat16),
            pltpu.VMEM((orb + 1, BS, aux_width * BS), jnp.bfloat16),
            pltpu.VMEM((orb, BS, BS), jnp.float32),
        ],
        compiler_params=params,
        name="exchange",
    )(codes, density, left, tail_in, swapped, *packs)

    step = 1
    while step < aux:
        ways = 2 if step == 1 or step * 4 > aux else 4
        if step == 2:
            parts = parts.astype(jnp.bfloat16)
        terms = [parts]
        for way in (2, 1, 3) if ways == 4 else (1,):
            terms.append(lax.ppermute(parts, "aux", [(i, i ^ (way * step)) for i in range(aux)]))
        terms = [term.astype(jnp.float32) for term in terms]
        while len(terms) > 1:
            terms = [terms[i] + terms[i + 1] for i in range(0, len(terms), 2)]
        parts = terms[0]
        step *= ways
    return parts


def solution(mesh):
    return jax.shard_map(
        shards,
        mesh=mesh,
        in_specs=(
            P("orb", None),
            P("orb", "aux", None, None, None),
            P("orb", "aux", None),
            P("orb", "aux"),
        ),
        out_specs=P("orb", None),
        check_vma=False,
    )
```

```python
import functools

import jax
import jax.numpy as jnp
from jax import lax
from jax.experimental import pallas as pl
from jax.experimental.pallas import tpu as pltpu
from jax.sharding import PartitionSpec as P

BS = 64
LANES = 128
NOTE = 8


def lay_blocks(raw, out_ref):
    slots, aux_width = raw.shape[:2]
    square = raw.reshape(slots * aux_width, BS, BS)
    for tile in range(slots * aux_width // 2):
        both = jnp.concatenate([square[2 * tile], square[2 * tile + 1]], axis=1)
        out_ref[tile * BS : (tile + 1) * BS] = both
    return slots * aux_width // 2


def partner(i, step, sign, orb):
    if orb == 4:
        return i ^ (2 - sign)
    return (i + sign * step) % orb


def owner_of(me, step, sign, orb):
    if orb == 4:
        return me ^ (2 - sign)
    return lax.rem(me - sign * step + orb, orb)


def core_parity():
    return lax.rem(lax.axis_index("aux"), 2)


def pack_kernel(
    orb, kept, pairs_hbm, density_hbm, raw_hbm, full_ref, pairs, rows, raw, sems
):
    copies = [
        pltpu.make_async_copy(src, dst, sems.at[i])
        for i, (src, dst) in enumerate(((raw_hbm, raw), (density_hbm, rows), (pairs_hbm, pairs)))
    ]
    for copy in copies:
        copy.start()
    for copy in copies[1:]:
        copy.wait()
    tiles = rows.shape[1] // LANES
    size = full_ref.shape[0] - tiles * BS - NOTE
    for t in range(tiles):
        lanes = slice(t * LANES, (t + 1) * LANES)
        full_ref[size + t * BS : size + (t + 1) * BS] = rows[:, lanes]
    shape = (NOTE, LANES)
    lane = lax.broadcasted_iota(jnp.int32, shape, 1)
    note = jnp.zeros(shape, jnp.int32)
    for j in range(pairs.shape[2]):
        note = jnp.where(lane == j, jnp.where(j < kept[0, 0], pairs[0, 0, j], orb), note)
    full_ref[size + tiles * BS :] = note.astype(jnp.float32).astype(jnp.bfloat16)
    copies[0].wait()
    lay_blocks(raw[0, 0], full_ref)


def tail_kernel(size, full_ref, out_ref):
    height = BS // 2
    tiles = (out_ref.shape[0] - NOTE) // height
    for t in range(tiles):
        first = pl.multiple_of(size + t * BS + core_parity() * height, height)
        out_ref[t * height : (t + 1) * height] = full_ref[pl.ds(first, height)]
    out_ref[tiles * height :] = full_ref[full_ref.shape[0] - NOTE :]


def lean_kernel(full_ref, tail_ref, out_ref):
    size = out_ref.shape[0] - NOTE
    out_ref[:size] = full_ref[:size]
    out_ref[size:] = tail_ref[tail_ref.shape[0] - NOTE :]


def relay_kernel(slots, aux_width, raw, full_ref, out_ref, left_ref):
    lay_blocks(raw[0, 0], out_ref)
    size = out_ref.shape[0]
    own = jnp.concatenate([full_ref[at : at + BS] for at in range(0, size, BS)], axis=1)
    for p in range(aux_width):
        cuts = [(j * aux_width + p) * BS for j in range(slots)]
        left_ref[p * BS : (p + 1) * BS] = jnp.concatenate(
            [own[:, cut : cut + BS] for cut in cuts], axis=1
        )


def merge_kernel(size, *refs):
    parts, out_ref = refs[:-1], refs[-1]
    at = 0
    for i, part in enumerate(parts):
        first = size if i < len(parts) - 1 else 0
        count = part.shape[0] - NOTE - first
        out_ref[at : at + count] = part[first : first + count]
        at += count


def exchange_kernel(
    orb, slots, aux_width, meta_ref, density_ref, left_ref, tail, swapped, *refs
):
    packs, (out_ref, rows, half_ref, held) = refs[:orb], refs[orb:]
    fulls = packs[2::2]
    notes = meta_ref[...]
    bits = orb.bit_length()
    meta = []
    for way in range(orb):
        word = notes[way]
        meta += [(word >> (bits * j)) & ((1 << bits) - 1) for j in range(slots)]
    me = lax.axis_index("orb")
    parity = core_parity()
    sign = 1 - 2 * parity
    height = BS // 2
    count = density_ref.shape[1] // LANES
    size = slots * aux_width * BS // LANES * BS
    near = pl.multiple_of(parity * height, height)
    far = pl.multiple_of((1 - parity) * height, height)
    across = lax.rem(me + orb // 2, orb)
    owners = [me, across]
    rows[me] = density_ref[...]
    for i, full in enumerate(fulls):
        owners += [owner_of(me, i + 1, sign, orb), owner_of(me, i + 1, -sign, orb)]
        for t in range(count):
            lanes = slice(t * LANES, (t + 1) * LANES)
            at = (i * count + t) * BS
            rows[owners[-2], :, lanes] = full[size + t * BS : size + (t + 1) * BS]
            rows[owners[-1], :, lanes] = swapped[at : at + BS]
    for t in range(count):
        lanes = slice(t * LANES, (t + 1) * LANES)
        at = len(fulls) * count * BS + t * height
        rows[across, pl.ds(near, height), lanes] = tail[t * height : (t + 1) * height]
        rows[across, pl.ds(far, height), lanes] = swapped[at : at + height]
    rows[orb] = jnp.zeros_like(rows[orb])
    selected = jnp.concatenate([rows[meta[j]] for j in range(slots)], axis=0)
    half = jnp.dot(left_ref[...], selected, preferred_element_type=jnp.float32)
    half = half.astype(jnp.bfloat16)
    for k in range(orb):
        half_ref[k] = jnp.concatenate(
            [half[p * BS : (p + 1) * BS, k * BS : (k + 1) * BS] for p in range(aux_width)],
            axis=1,
        )
    half_ref[orb] = jnp.zeros_like(half_ref[orb])
    for way in range(orb):
        codes = meta[way * slots : (way + 1) * slots]
        held[owners[way]] = lax.dot_general(
            jnp.concatenate([half_ref[code] for code in codes], axis=1),
            jnp.concatenate([packs[way][at : at + BS] for at in range(0, size, BS)], axis=1),
            (((1,), (1,)), ((), ())),
            preferred_element_type=jnp.float32,
        )
    out_ref[...] = jnp.concatenate([held[n] for n in range(orb)], axis=1)


def shards(density, tensor_blocks, pairs, kept):
    full_width = density.shape[1]
    slots = tensor_blocks.shape[2]
    aux_width = tensor_blocks.shape[3]
    orb = lax.axis_size("orb")
    aux = lax.axis_size("aux")
    rows = full_width // LANES * BS
    size = slots * aux_width * BS // LANES * BS
    vmem = pl.BlockSpec(memory_space=pltpu.VMEM)
    smem = pl.BlockSpec(memory_space=pltpu.SMEM)
    hbm = pl.BlockSpec(memory_space=pltpu.HBM)
    params = pltpu.CompilerParams(vmem_limit_bytes=32 * 1024 * 1024)

    def array(height):
        return jax.ShapeDtypeStruct((height, LANES), jnp.bfloat16)

    def shift(x, step, sign):
        perm = [
            (a * orb + o, a * orb + partner(o, step, sign * (1 - 2 * (a % 2)), orb))
            for a in range(aux)
            for o in range(orb)
        ]
        return lax.ppermute(x, ("aux", "orb"), perm)

    full = pl.pallas_call(
        functools.partial(pack_kernel, orb),
        out_shape=array(size + rows + NOTE),
        in_specs=[smem, hbm, hbm, hbm],
        out_specs=vmem,
        scratch_shapes=[
            pltpu.SMEM(pairs.shape, jnp.int32),
            pltpu.VMEM(density.shape, jnp.bfloat16),
            pltpu.VMEM(tensor_blocks.shape, jnp.bfloat16),
            pltpu.SemaphoreType.DMA((3,)),
        ],
        compiler_params=params,
        name="pack",
    )(
        kept,
        *(pltpu.with_memory_space_constraint(a, pltpu.HBM) for a in (pairs, density, tensor_blocks)),
    )
    tail = pl.pallas_call(
        functools.partial(tail_kernel, size),
        out_shape=array(rows // 2 + NOTE),
        in_specs=[vmem],
        out_specs=vmem,
        compiler_params=params,
        name="tail",
    )(full)
    lean = pl.pallas_call(
        lean_kernel,
        out_shape=array(size + NOTE),
        in_specs=[vmem] * 2,
        out_specs=vmem,
        compiler_params=params,
        name="lean",
    )(full, tail)
    across = [(i, (i + orb // 2) % orb) for i in range(orb)]
    raw = lax.ppermute(tensor_blocks, "orb", across)
    tail_in = lax.ppermute(tail, "orb", across)
    fulls = [shift(full, i, 1) for i in range(1, orb // 2)]
    leans = [shift(lean, i, -1) for i in range(1, orb // 2)]

    tail_in, raw = lax.optimization_barrier((tail_in, raw))
    merged = pl.pallas_call(
        functools.partial(merge_kernel, size),
        out_shape=array(len(fulls) * rows + rows // 2),
        in_specs=[vmem] * (len(fulls) + 1),
        out_specs=vmem,
        compiler_params=params,
        name="merge",
    )(*fulls, tail_in)
    swapped = lax.ppermute(merged, "aux", [(i, i ^ 1) for i in range(aux)])
    across, left = pl.pallas_call(
        functools.partial(relay_kernel, slots, aux_width),
        out_shape=[
            array(size),
            jax.ShapeDtypeStruct((aux_width * BS, slots * BS), jnp.bfloat16),
        ],
        in_specs=[vmem] * 2,
        out_specs=[vmem] * 2,
        compiler_params=params,
        name="relay",
    )(raw, full)
    swapped, leans = lax.optimization_barrier((swapped, leans))
    packs, notes = [full, across], [tail, tail_in]
    for pair in zip(fulls, leans):
        packs += pair
        notes += pair
    codes = jnp.concatenate([n[-NOTE, :slots] for n in notes]).astype(jnp.int32)
    places = 1 << (orb.bit_length() * jnp.arange(slots, dtype=jnp.int32))
    codes = jnp.sum(codes.reshape(orb, slots) * places, axis=1, dtype=jnp.int32)
    parts = pl.pallas_call(
        functools.partial(exchange_kernel, orb, slots, aux_width),
        out_shape=jax.ShapeDtypeStruct((BS, full_width), jnp.float32),
        in_specs=[vmem] * (orb + 5),
        out_specs=vmem,
        scratch_shapes=[
            pltpu.VMEM((orb + 1, BS, full_width), jnp.bfloat16),
            pltpu.VMEM((orb + 1, BS, aux_width * BS), jnp.bfloat16),
            pltpu.VMEM((orb, BS, BS), jnp.float32),
        ],
        compiler_params=params,
        name="exchange",
    )(codes, density, left, tail_in, swapped, *packs)

    step = 1
    while step < aux:
        ways = 2 if step == 1 or step * 4 > aux else 4
        if step == 2:
            parts = parts.astype(jnp.bfloat16)
        terms = [parts]
        for way in (2, 1, 3) if ways == 4 else (1,):
            terms.append(lax.ppermute(parts, "aux", [(i, i ^ (way * step)) for i in range(aux)]))
        terms = [term.astype(jnp.float32) for term in terms]
        while len(terms) > 1:
            terms = [terms[i] + terms[i + 1] for i in range(0, len(terms), 2)]
        parts = terms[0]
        step *= ways
    return parts


def solution(mesh):
    return jax.shard_map(
        shards,
        mesh=mesh,
        in_specs=(
            P("orb", None),
            P("orb", "aux", None, None, None),
            P("orb", "aux", None),
            P("orb", "aux"),
        ),
        out_specs=P("orb", None),
        check_vma=False,
    )
```
